32 devices in a mesh: nodes: 8 (over z, y), heads: 4 (over x, core).
Axes of the slice: x: 2, y: 2, z: 4, core: 2. Of those that a mesh axis runs over, the one named last changes fastest.
Arguments:
- node_state: bfloat16 [2, 4096, 512], P(None, 'nodes', 'heads'), may hold values from -6 to 6
- noise_embed: float32 [2, 256], replicated, may hold values from -5 to 5
- out_grad: bfloat16 [2, 4096, 512], P(None, 'nodes', 'heads'), may hold values from -6 to 6
- neighbours: int32 [2, 4096, 16], P(None, 'nodes'), may hold values from 0 to 4095, as said below
- patch_sizes: int32 [2, 8], P(None, 'nodes'), may hold values from 256 to 512, as said below
- w_project: float32 [512, 1536], P('nodes', 'heads'), may hold values from -0.25 to 0.25
- w_output: float32 [512, 512], P('heads', 'nodes'), may hold values from -0.75 to 0.75
- w_expand: float32 [512, 2048], P('nodes', 'heads'), may hold values from -0.25 to 0.25
- w_contract: float32 [2048, 512], P('heads', 'nodes'), may hold values from -0.125 to 0.125
- momentum_project: float32 [512, 1536], P('nodes', 'heads'), may hold values from -96 to 96
- momentum_output: float32 [512, 512], P('heads', 'nodes'), may hold values from -160 to 160
- momentum_expand: float32 [512, 2048], P('nodes', 'heads'), may hold values from -160 to 160
- momentum_contract: float32 [2048, 512], P('heads', 'nodes'), may hold values from -256 to 256
- w_modulate: float32 [4, 256, 512], P(None, None, 'heads'), may hold values from -0.1875 to 0.1875
- b_modulate: float32 [4, 512], P(None, 'heads'), may hold values from -0.6 to 0.6
- first_modulate: float32 [4, 256, 512], P(None, None, 'heads'), may hold values from -28 to 28
- second_modulate: float32 [4, 256, 512], P(None, None, 'heads'), may hold values from 1.536 to 6.144
- first_bias: float32 [4, 512], P(None, 'heads'), may hold values from -28 to 28
- second_bias: float32 [4, 512], P(None, 'heads'), may hold values from 1.536 to 6.144
Outputs:
- layer_output: bfloat16 [2, 4096, 512], P(None, 'nodes', 'heads')
- input_grad: float32 [2, 4096, 512], P(None, 'nodes', 'heads')
- new_momentum_project: float32 [512, 1536], P('nodes', 'heads')
- new_momentum_output: float32 [512, 512], P('heads', 'nodes')
- new_momentum_expand: float32 [512, 2048], P('nodes', 'heads')
- new_momentum_contract: float32 [2048, 512], P('heads', 'nodes')
- new_project: float32 [512, 1536], P('nodes', 'heads')
- new_output: float32 [512, 512], P('heads', 'nodes')
- new_expand: float32 [512, 2048], P('nodes', 'heads')
- new_contract: float32 [2048, 512], P('heads', 'nodes')
- new_first_modulate: float32 [4, 256, 512], P(None, None, 'heads')
- new_second_modulate: float32 [4, 256, 512], P(None, None, 'heads')
- new_modulate: float32 [4, 256, 512], P(None, None, 'heads')
- new_first_bias: float32 [4, 512], P(None, 'heads')
- new_second_bias: float32 [4, 512], P(None, 'heads')
- new_bias: float32 [4, 512], P(None, 'heads')
The draws below stay inside these ranges and needn't reach their ends.
Inputs may be any that keep to these rules, and one draw needn't show every extreme that they name: `neighbours`: each entry is patch times 512 plus slot of a live node in the same patch or in one of the two patches beside it, patches taken cyclically. `patch_sizes`: in each micro-batch the last patch holds exactly 512 live nodes and another exactly half of 512; live nodes fill the lowest slots of a patch.
All inputs are finite; a program needn't handle non-finite values.
Results may differ from the reference program's by a relative error of at most 0.007.
The reference program's roundings to bfloat16 on the way count: a program that leaves them out, or rounds other values in their place, can miss the bound.
Values may be sent and summed in bfloat16 or wider, within the bound.
A program may use at most 128 MiB of HBM per device.

```python
import math
import jax
import jax.numpy as jnp
from jax import lax

D = 512
HEADS = 4
FF = 2048
HD = 128
CD = 256
K = 16
CAP = 512
MB = 2
NS_STEPS = 5
STEP = 10
NODES = 4096
N_NODES = 8


def patch_table(key):
    base = jax.random.fold_in(key, 11)
    key_sizes, key_full, key_half = jax.random.split(base, 3)
    counts = jax.random.randint(key_sizes, (MB, N_NODES), CAP // 2, CAP + 1)
    half_spot = jax.random.randint(key_half, (MB, 1), 0, N_NODES - 1)
    full_spot = jax.random.randint(key_full, (MB, 1), 0, N_NODES)
    full_spot = jnp.where(full_spot == half_spot, N_NODES - 1, full_spot)
    columns = jnp.arange(N_NODES, dtype=jnp.int32)[None, :]
    counts = jnp.where(columns == full_spot, CAP, counts)
    counts = jnp.where(columns == N_NODES - 1, CAP, counts)
    counts = jnp.where(columns == half_spot, CAP // 2, counts)
    return counts.astype(jnp.int32)


def draw_patch_sizes(key, part):
    return patch_table(key)


def draw_neighbours(key, part):
    counts = patch_table(key)
    key = jax.random.fold_in(key, 23)
    key_side, key_slot = jax.random.split(key)
    side = jax.random.randint(key_side, (MB, NODES, K), 0, 8)
    step_over = jnp.where(side == 0, -1, jnp.where(side == 1, 1, 0)).astype(jnp.int32)
    home = (jnp.arange(NODES, dtype=jnp.int32) // CAP)[None, :, None]
    target = jnp.mod(home + step_over, N_NODES)
    batch_ids = jnp.arange(MB, dtype=jnp.int32)[:, None, None]
    live_count = counts[batch_ids, target]
    slot = jnp.mod(jax.random.randint(key_slot, (MB, NODES, K), 0, 1048576), live_count)
    entries = (target * CAP + slot).astype(jnp.int32)
    entries = entries.at[:, 0, 0].set(0)
    entries = entries.at[:, NODES - 1, 0].set(NODES - 1)
    return entries.astype(jnp.int32)


def block_levels(own_key, dims, cuts, low, high):
    def one(position, shards_of):
        draws = jax.random.uniform(jax.random.fold_in(jax.random.fold_in(own_key, 6), position), (shards_of,), jnp.float32, low / len(cuts), high / len(cuts))
        return jnp.repeat(jnp.exp(draws), dims[position] // shards_of).reshape((-1,) + (1,) * (len(dims) - position - 1))

    factor_of = one(*cuts[0])
    for cut in cuts[1:]:
        factor_of = factor_of * one(*cut)
    return factor_of


def noise(rng, extent, scale, most, cuts=(), kind=jnp.bfloat16):
    drawn = jax.random.normal(rng, extent, jnp.float32) * scale
    if len(cuts) > 0:
        drawn = block_levels(rng, extent, cuts, -0.22, 0.18) * drawn
    return jnp.clip(drawn, min=-most, max=most).astype(kind)


def setup_inputs(seed: int = 0) -> dict:
    key_list = jax.random.split(jax.random.key(seed), 20)
    return {
        "node_state": noise(key_list[0], (MB, NODES, D), 1.0, 6.0, ((1, 8), (2, 4))),
        "noise_embed": noise(key_list[1], (MB, CD), 1.0, 5.0, (), jnp.float32),
        "out_grad": noise(key_list[2], (MB, NODES, D), 1.0, 6.0, ((1, 8), (2, 4))),
        "neighbours": draw_neighbours(jax.random.fold_in(key_list[19], 71), 0),
        "patch_sizes": draw_patch_sizes(jax.random.fold_in(key_list[19], 71), 0),
        "w_project": noise(key_list[5], (D, 3 * D), D ** -0.5, 0.25, ((0, 8), (1, 4)), jnp.float32),
        "w_output": noise(key_list[6], (D, D), (D // 8) ** -0.5, 0.75, ((0, 4), (1, 8)), jnp.float32),
        "w_expand": noise(key_list[7], (D, FF), D ** -0.5, 0.25, ((0, 8), (1, 4)), jnp.float32),
        "w_contract": noise(key_list[8], (FF, D), FF ** -0.5, 0.125, ((0, 4), (1, 8)), jnp.float32),
        "momentum_project": noise(key_list[9], (D, 3 * D), (0.2 * (0.75 * MB * NODES) ** 0.5), 96.0, ((0, 8), (1, 4)), jnp.float32),
        "momentum_output": noise(key_list[10], (D, D), (0.35 * (0.75 * MB * NODES) ** 0.5), 160.0, ((0, 4), (1, 8)), jnp.float32),
        "momentum_expand": noise(key_list[11], (D, FF), (0.35 * (0.75 * MB * NODES) ** 0.5), 160.0, ((0, 8), (1, 4)), jnp.float32),
        "momentum_contract": noise(key_list[12], (FF, D), (0.6 * (0.75 * MB * NODES) ** 0.5), 256.0, ((0, 4), (1, 8)), jnp.float32),
        "w_modulate": noise(key_list[13], (4, CD, D), (4 * CD) ** -0.5, 0.1875, ((2, 4),), jnp.float32),
        "b_modulate": noise(key_list[14], (4, D), 0.1, 0.6, ((1, 4),), jnp.float32),
        "first_modulate": noise(key_list[15], (4, CD, D), (0.055 * (0.75 * MB * NODES) ** 0.5), 28.0, ((2, 4),), jnp.float32),
        "second_modulate": jnp.clip(jnp.exp(math.log(6.144) - 1.3862944 * jax.random.uniform(key_list[16], (4, CD, D), jnp.float32) ** block_levels(key_list[16], (4, CD, D), ((2, 4),), -0.2, 0.2)), 1.536, 6.144),
        "first_bias": noise(key_list[17], (4, D), (0.055 * (0.75 * MB * NODES) ** 0.5), 28.0, ((1, 4),), jnp.float32),
        "second_bias": jnp.clip(jnp.exp(math.log(6.144) - 1.3862944 * jax.random.uniform(key_list[18], (4, D), jnp.float32) ** block_levels(key_list[18], (4, D), ((1, 4),), -0.2, 0.2)), 1.536, 6.144),
    }


EPS_NORM = 1e-06
NEWTON_A = 3.4445
NEWTON_B = -4.775
NEWTON_C = 2.0315
MOMENTUM_DECAY = 0.5
LR_MUON = 1.0
LR_ADAM = 0.04
DECAY_WEIGHT = 0.01
BETA_FIRST = 0.9
BETA_SECOND = 0.999
EPS_ADAM = 1e-08
HIGH = lax.Precision.HIGHEST

@jax.custom_vjp
def low(v):
    return lax.optimization_barrier(v.astype(jnp.bfloat16)).astype(jnp.float32)

@jax.custom_vjp
def low_back(v):
    return v

def low_keep(v):
    return (low(v), None)

def low_pass(kept, grad):
    return (grad,)

def back_keep(v):
    return (v, None)

def back_low(kept, grad):
    return (low(grad),)
low.defvjp(low_keep, low_pass)
low_back.defvjp(back_keep, back_low)

def norm_rows(values):
    row_mean = lax.optimization_barrier(jnp.mean(values, axis=-1, keepdims=True))
    spread = lax.optimization_barrier(jnp.mean(values * values, axis=-1, keepdims=True)) - row_mean * row_mean
    return (values - row_mean) * lax.rsqrt(spread + EPS_NORM)

def attend_block(queries, key_all, value_all, local_ids):
    key_rows = key_all[local_ids]
    value_rows = value_all[local_ids]
    scores = jnp.einsum('bhd,bkhd->bhk', queries, key_rows, precision=HIGH) * HD ** (-0.5)
    row_max = lax.optimization_barrier(jnp.max(scores, axis=-1, keepdims=True))
    exp_terms = jnp.exp(scores - row_max)
    prob = exp_terms / lax.optimization_barrier(jnp.sum(exp_terms, axis=-1, keepdims=True))
    mixed = jnp.einsum('bhk,bkhd->bhd', low(prob), value_rows, precision=HIGH)
    return low(mixed)

def forward(state_rows, noise_row, w_project, w_output, w_expand, w_contract, w_modulate, b_modulate, neighbour_ids):
    row_count = state_rows.shape[0]
    low_project = low(w_project)
    low_output = low(w_output)
    low_expand = low(w_expand)
    low_contract = low(w_contract)
    modulation = jnp.einsum('c,jcd->jd', noise_row, w_modulate, precision=HIGH) + b_modulate
    a_one = low(norm_rows(state_rows) * (1.0 + modulation[1]) + modulation[0])
    projected = low(low_back(jnp.dot(a_one, low_project, precision=HIGH)))
    projected = projected.reshape(row_count, HEADS, 3, HD)
    queries = projected[:, :, 0]
    key_all = projected[:, :, 1]
    value_all = projected[:, :, 2]
    block_count = row_count // CAP

    def one_block(pair):
        return attend_block(pair[0], key_all, value_all, pair[1])
    mixed = lax.map(jax.checkpoint(one_block), (queries.reshape(block_count, CAP, HEADS, HD), neighbour_ids.reshape(block_count, CAP, K)))
    mixed = mixed.reshape(row_count, D)
    hidden_one = state_rows + low_back(jnp.dot(mixed, low_output, precision=HIGH))
    a_two = low(norm_rows(hidden_one) * (1.0 + modulation[3]) + modulation[2])
    up_rows = low_back(jnp.dot(a_two, low_expand, precision=HIGH))
    act = low(up_rows * jax.nn.sigmoid(up_rows))
    return hidden_one + low_back(jnp.dot(act, low_contract, precision=HIGH))

def orthogonal(matrix):
    is_tall = matrix.shape[0] > matrix.shape[1]
    iterate = matrix.T if is_tall else matrix
    iterate = iterate / (jnp.sqrt(jnp.sum(iterate * iterate)) + 1e-07)
    for repeat in range(NS_STEPS):
        square = jnp.dot(iterate, iterate.T, precision=HIGH)
        polynomial = NEWTON_B * square + NEWTON_C * jnp.dot(square, square, precision=HIGH)
        iterate = NEWTON_A * iterate + jnp.dot(polynomial, iterate, precision=HIGH)
    return iterate.T if is_tall else iterate

def muon_step(weight, momentum, gradient):
    moment_new = MOMENTUM_DECAY * momentum + gradient
    factor = max(1.0, weight.shape[0] / weight.shape[1]) ** 0.5
    updated = weight * (1.0 - LR_MUON * DECAY_WEIGHT) - LR_MUON * factor * orthogonal(moment_new)
    return (moment_new, updated)

def adam_step(weight, first_old, second_old, gradient):
    first_new = BETA_FIRST * first_old + (1.0 - BETA_FIRST) * gradient
    second_new = BETA_SECOND * second_old + (1.0 - BETA_SECOND) * gradient * gradient
    first_hat = first_new / (1.0 - BETA_FIRST ** STEP)
    second_hat = second_new / (1.0 - BETA_SECOND ** STEP)
    updated = weight * (1.0 - LR_ADAM * DECAY_WEIGHT) - LR_ADAM * first_hat / (jnp.sqrt(second_hat) + EPS_ADAM)
    return (first_new, second_new, updated)

def reference(node_state, noise_embed, out_grad, neighbours, patch_sizes, w_project, w_output, w_expand, w_contract, momentum_project, momentum_output, momentum_expand, momentum_contract, w_modulate, b_modulate, first_modulate, second_modulate, first_bias, second_bias):
    params = (w_project, w_output, w_expand, w_contract, w_modulate, b_modulate)
    grads = tuple((jnp.zeros_like(weight) for weight in params))
    outputs = []
    input_grads = []
    slots = jnp.arange(CAP, dtype=jnp.int32)
    for batch in range(MB):
        live_rows = (slots[None, :] < patch_sizes[batch][:, None]).reshape(NODES, 1).astype(jnp.float32)
        state_rows = node_state[batch].astype(jnp.float32)
        noise_row = noise_embed[batch]
        neighbour_ids = neighbours[batch]

        def run(state_in, *weights):
            return forward(state_in, noise_row, *weights, neighbour_ids)
        result, pull = jax.vjp(run, state_rows, *params)
        pulled = pull(out_grad[batch].astype(jnp.float32) * live_rows)
        outputs.append((result * live_rows).astype(jnp.bfloat16))
        input_grads.append(pulled[0])
        grads = tuple((total + piece for total, piece in zip(grads, pulled[1:])))
    mom_project, new_project = muon_step(w_project, momentum_project, grads[0])
    mom_output, new_output = muon_step(w_output, momentum_output, grads[1])
    mom_expand, new_expand = muon_step(w_expand, momentum_expand, grads[2])
    mom_contract, new_contract = muon_step(w_contract, momentum_contract, grads[3])
    first_mod, second_mod, new_mod = adam_step(w_modulate, first_modulate, second_modulate, grads[4])
    first_b, second_b, new_b = adam_step(b_modulate, first_bias, second_bias, grads[5])
    return (jnp.stack(outputs), jnp.stack(input_grads), mom_project, mom_output, mom_expand, mom_contract, new_project, new_output, new_expand, new_contract, first_mod, second_mod, new_mod, first_b, second_b, new_b)
```

```python
import functools

import jax
import jax.numpy as jnp
from jax import lax
from jax.experimental import pallas as pl
from jax.experimental.pallas import tpu as pltpu
from jax.sharding import PartitionSpec as P

NS_STEPS = 5
STEP = 10


EPS_NORM = 1e-06
NEWTON_A = 3.4445
NEWTON_B = -4.775
NEWTON_C = 2.0315
MOMENTUM_DECAY = 0.5
LR_MUON = 1.0
LR_ADAM = 0.04
DECAY_WEIGHT = 0.01
BETA_FIRST = 0.9
BETA_SECOND = 0.999
EPS_ADAM = 1e-08
HIGH = lax.Precision.HIGHEST
MESH = pl.DeviceIdType.MESH
F32 = jnp.float32
BF16 = jnp.bfloat16
NN = (((1,), (0,)), ((), ()))
NT = (((1,), (1,)), ((), ()))
TN = (((0,), (0,)), ((), ()))


def mul(left, right, dims=NN):
    return lax.dot_general(left, right, dims, preferred_element_type=F32)


class Links:
    def __init__(self, send_sems, recv_sems):
        self.send_sems, self.recv_sems = send_sems, recv_sems
        self.copies = []

    def send(self, source, target, device):
        slot = len(self.copies)
        copy = pltpu.make_async_remote_copy(
            src_ref=source,
            dst_ref=target,
            send_sem=self.send_sems.at[slot],
            recv_sem=self.recv_sems.at[slot],
            device_id=device,
            device_id_type=MESH,
        )
        copy.start()
        self.copies.append(copy)
        return copy

    def close(self):
        for copy in self.copies:
            copy.wait_send()


def meet(devices):
    barrier = pltpu.get_barrier_semaphore()
    for device in devices:
        pl.semaphore_signal(barrier, inc=1, device_id=device, device_id_type=MESH)
    pl.semaphore_wait(barrier, len(devices))


def norm_rows(values):
    width = values.shape[-1]
    row_mean = jnp.sum(values, axis=-1, keepdims=True) / width
    square_mean = jnp.sum(values * values, axis=-1, keepdims=True) / width
    inv_root = lax.rsqrt(square_mean - row_mean * row_mean + EPS_NORM)
    return ((values - row_mean) * inv_root, inv_root)


def wide(ref, *index):
    return jnp.concatenate([ref[(head, *index)] for head in range(ref.shape[0])], axis=-1)


def mod_row(mod_ref, batch, number):
    return wide(mod_ref, slice(batch * 4 + number, batch * 4 + number + 1), slice(None))


def attend_kernel(
    patch_count,
    own_gather,
    state_ref,
    cot_ref,
    index_ref,
    mod_ref,
    weight_ref,
    state_all,
    cot_all,
    mod_all,
    a_one,
    queries,
    key_value,
    prob_low,
    mixed_all,
    weight_all,
    output_all,
    halo,
    count,
    send_sems,
    recv_sems,
):
    node, head = lax.axis_index("nodes"), lax.axis_index("heads")
    after, before = lax.rem(node + 1, patch_count), lax.rem(node + patch_count - 1, patch_count)
    across, sibling = lax.rem(head + 2, 4), head + 1 - 2 * lax.rem(head, 2)
    to_across, to_sibling, to_diagonal = (node, across), (node, sibling), (node, 3 - head)
    to_after, to_before = (after, head), (before, head)
    partner = node + 1 - 2 * lax.rem(node, 2)
    peers = [(lax.rem(node + 2 * k, patch_count), head) for k in range(1, patch_count // 2)]
    met = [to_across, to_sibling, to_diagonal, to_after, to_before]
    meet(met + peers if own_gather else met)
    micro_count, capacity, share = state_ref.shape
    head_dim = queries.shape[-1]
    total = 3 * capacity
    links = Links(send_sems, recv_sems)

    state_across = links.send(state_ref, state_all.at[head], to_across)
    state_after = links.send(state_ref, halo.at[0, head], to_after)
    state_before = links.send(state_ref, halo.at[1, head], to_before)
    state_sibling = links.send(state_ref, state_all.at[head], to_sibling)
    mod_copies = [
        links.send(mod_ref, mod_all.at[head], to)
        for to in (to_across, to_sibling, to_diagonal)
    ]
    first_columns, other_columns = pl.ds(0, 3 * head_dim), pl.ds(3 * head_dim, weight_ref.shape[-1] - 3 * head_dim)

    def spread(columns):
        part = weight_ref.at[:, columns]
        into = weight_all.at[node, :, columns]
        return [links.send(part, into, to) for to in peers], [
            links.send(part, into, (partner, head))
        ]

    def pass_on(arriving, columns):
        passed = []
        for k, copy in enumerate(arriving):
            copy.wait_recv()
            owner = lax.rem(node + patch_count - 2 * (k + 1), patch_count)
            passed.append(
                links.send(
                    weight_all.at[owner, :, columns],
                    weight_all.at[owner, :, columns],
                    (partner, head),
                )
            )
        return passed

    if own_gather:
        first_peers, first_partner = spread(first_columns)
        weight_all[node] = weight_ref[...]
    state_all[head] = state_ref[...]
    cot_all[head] = cot_ref[...]
    mod_all[head] = mod_ref[...]

    group = index_ref.shape[-1] // 16
    blocks = total // share

    def count_group(batch, place):
        ids = index_ref[batch, pl.ds(place, 1), :]
        lanes = lax.broadcasted_iota(jnp.int32, ids.shape, 1)
        code = (ids >> 7) + 16 * (lanes >> 4)
        rows = lax.broadcasted_iota(jnp.int32, (blocks * group, ids.shape[1]), 0)
        pick = jnp.where(code == (rows // group) + 16 * (rows % group), 1.0, 0.0).astype(BF16)
        slots = lax.broadcasted_iota(jnp.int32, (share, ids.shape[1]), 0)
        spot = jnp.where((ids & 127) == slots, 1.0, 0.0).astype(BF16)
        found = mul(pick, spot, NT).astype(BF16)
        for block in range(blocks):
            count[batch, pl.ds(pl.multiple_of(place * group, group), group), block * share : (block + 1) * share] = found[
                block * group : (block + 1) * group
            ]

    for batch in range(micro_count):

        @pl.loop(0, capacity // group)
        def _(place):
            count_group(batch, place)

    state_across.wait_recv()
    pass_state = links.send(state_all.at[across], state_all.at[across], to_sibling)
    halo_across, halo_sibling = [], []
    for side, copy in ((0, state_after), (1, state_before)):
        copy.wait_recv()
        halo_across.append(links.send(halo.at[side, head], halo.at[side, head], to_across))
        halo_sibling.append(links.send(halo.at[side, head], halo.at[side, head], to_sibling))
    if own_gather:
        first_passed = pass_on(first_peers, first_columns)
        other_peers, other_partner = spread(other_columns)
    state_sibling.wait_recv()
    pass_state.wait_recv()
    for copy in mod_copies:
        copy.wait_recv()
    if own_gather:
        for copy in first_partner + first_passed:
            copy.wait_recv()
    inv_head = head_dim ** (-0.5)
    tile = capacity // 2

    def project(source, patch):
        for batch in range(micro_count):
            shift, scale = mod_row(mod_all, batch, 0), 1.0 + mod_row(mod_all, batch, 1)

            @pl.loop(0, capacity // tile)
            def _(step):
                rows = pl.ds(pl.multiple_of(step * tile, tile), tile)
                normed, _ = norm_rows(wide(source, batch, rows, slice(None)).astype(F32))
                a_rows = (normed * scale + shift).astype(BF16)
                a_one[patch, batch, rows, :] = a_rows
                first = 0 if patch == 1 else head_dim
                weight = weight_all[:, :, first : 3 * head_dim].reshape(4 * share, 3 * head_dim - first)
                out = mul(a_rows, weight).astype(BF16)
                if patch == 1:
                    queries[batch, rows, :] = out[:, :head_dim]
                key_value[batch, patch, rows, :] = out[:, out.shape[1] - 2 * head_dim :]

    project(state_all, 1)
    for side in range(2):
        halo_across[side].wait_recv()
        halo_sibling.append(links.send(halo.at[side, across], halo.at[side, across], to_sibling))
    cot_across = links.send(cot_ref, cot_all.at[head], to_across)
    cot_sibling = links.send(cot_ref, cot_all.at[head], to_sibling)
    for copy in halo_sibling:
        copy.wait_recv()
    project(halo.at[0], 0)
    project(halo.at[1], 2)
    if own_gather:
        other_passed = pass_on(other_peers, other_columns)

    attend_rows = 128
    mixed_copies = []
    for batch in range(micro_count):

        @pl.loop(0, capacity // attend_rows)
        def _(step):
            rows = pl.ds(pl.multiple_of(step * attend_rows, attend_rows), attend_rows)
            keys = key_value[batch, :, :, :head_dim].reshape(total, head_dim)
            values = key_value[batch, :, :, head_dim:].reshape(total, head_dim)
            scores = mul(queries[batch, rows, :], keys, NT) * inv_head
            times = count[batch, rows, :].astype(F32)
            scores = jnp.where(times > 0.0, scores, -1e30)
            exps = jnp.exp(scores - jnp.max(scores, axis=-1, keepdims=True)) * times
            prob = (exps * (1.0 / jnp.sum(exps, axis=-1, keepdims=True))).astype(BF16)
            prob_low[batch, rows, :] = prob
            mixed_all[head, batch, rows, :] = mul(prob, values).astype(BF16)

        part = mixed_all.at[head, batch]
        mixed_copies.append(
            (batch, links.send(part, part, to_across), links.send(part, part, to_sibling))
        )

    cot_across.wait_recv()
    last = [cot_sibling, links.send(cot_all.at[across], cot_all.at[across], to_sibling)]
    if own_gather:
        for copy in other_partner + other_passed:
            copy.wait_recv()
        output_columns = pl.ds(3 * head_dim, head_dim)
        output_all[head] = weight_all[:, :, 3 * head_dim : 4 * head_dim]
        output_part = weight_all.at[:, :, output_columns]
        output_across = links.send(output_part, output_all.at[head], to_across)
        last.append(links.send(output_part, output_all.at[head], to_sibling))
        output_across.wait_recv()
        last.append(links.send(output_all.at[across], output_all.at[across], to_sibling))
    for batch, copy, other in mixed_copies:
        copy.wait_recv()
        part = mixed_all.at[across, batch]
        last += [other, links.send(part, part, to_sibling)]
    for copy in last:
        copy.wait_recv()
    links.close()


def adam_step(weight, first_old, second_old, gradient):
    first_new = BETA_FIRST * first_old + (1.0 - BETA_FIRST) * gradient
    second_new = BETA_SECOND * second_old + (1.0 - BETA_SECOND) * gradient * gradient
    first_hat = first_new / (1.0 - BETA_FIRST**STEP)
    second_hat = second_new / (1.0 - BETA_SECOND**STEP)
    updated = weight * (1.0 - LR_ADAM * DECAY_WEIGHT) - LR_ADAM * first_hat / (
        jnp.sqrt(second_hat) + EPS_ADAM
    )
    return (first_new, second_new, updated)


def orthogonal(matrix):
    scale = 1.0 / (jnp.sqrt(jnp.sum(matrix * matrix)) + 1e-07)
    gram = jnp.dot(matrix, matrix.T, precision=HIGH) * (scale * scale)
    eye = jnp.eye(gram.shape[0], dtype=F32)
    chain = None
    for repeat in range(NS_STEPS):
        factor = NEWTON_A * eye + NEWTON_B * gram + NEWTON_C * jnp.dot(gram, gram, precision=HIGH)
        chain = factor if chain is None else jnp.dot(factor, chain, precision=HIGH)
        if repeat < NS_STEPS - 1:
            gram = jnp.dot(factor, jnp.dot(factor, gram, precision=HIGH), precision=HIGH)
    return jnp.dot(chain, matrix, precision=HIGH) * scale


def per_device(
    node_state,
    noise_embed,
    out_grad,
    neighbours,
    patch_sizes,
    w_project,
    w_output,
    w_expand,
    w_contract,
    momentum_project,
    momentum_output,
    momentum_expand,
    momentum_contract,
    w_modulate,
    b_modulate,
    first_modulate,
    second_modulate,
    first_bias,
    second_bias,
):
    micro_count, capacity, share = node_state.shape
    head_count = lax.axis_size("heads")
    patch_count = lax.axis_size("nodes")
    full_width = share * head_count
    head_dim = w_output.shape[0]
    total_rows = capacity * patch_count
    patch_index = lax.axis_index("nodes")
    head_index = lax.axis_index("heads")
    inv_head = head_dim ** (-0.5)
    hidden = w_expand.shape[1]
    shard_rows = w_project.shape[0]
    own_gather = patch_count == 8

    modulation = (
        jnp.einsum("bc,jcd->bjd", noise_embed, w_modulate, precision=HIGH) + b_modulate
    ).reshape(micro_count * 4, share)
    local_index = jnp.mod(neighbours - (patch_index - 1) * capacity, total_rows)
    index_rows = local_index.reshape(micro_count, capacity // 16, 256)
    weight_cat = jnp.concatenate([w_project, w_output.T, w_expand, w_contract.T], axis=1)
    low_cat = weight_cat.astype(BF16)
    weight_width = low_cat.shape[1]
    if not own_gather:
        low_cat = lax.all_gather(low_cat, "nodes", axis=0, tiled=True).reshape(8, full_width // 8, weight_width)
    vmem = pl.BlockSpec(memory_space=pltpu.VMEM)
    rows_all = jax.ShapeDtypeStruct((head_count, micro_count, capacity, share), BF16)
    out_shape = [
        rows_all,
        rows_all,
        jax.ShapeDtypeStruct((head_count, micro_count * 4, share), F32),
        jax.ShapeDtypeStruct((3, micro_count, capacity, full_width), BF16),
        jax.ShapeDtypeStruct((micro_count, capacity, head_dim), BF16),
        jax.ShapeDtypeStruct((micro_count, 3, capacity, 2 * head_dim), BF16),
        jax.ShapeDtypeStruct((micro_count, capacity, 3 * capacity), BF16),
        rows_all,
    ]
    if own_gather:
        out_shape += [
            jax.ShapeDtypeStruct((patch_count, shard_rows, weight_width), BF16),
            jax.ShapeDtypeStruct((head_count, patch_count, shard_rows, head_dim), BF16),
        ]

    def attend_body(*refs):
        refs = list(refs)
        if not own_gather:
            refs[13:13] = [refs[4], None]
        attend_kernel(patch_count, own_gather, *refs)

    gathered = pl.pallas_call(
        attend_body,
        out_shape=out_shape,
        in_specs=[vmem] * 5,
        out_specs=[vmem] * len(out_shape),
        scratch_shapes=[
            pltpu.VMEM((2, head_count, micro_count, capacity, share), BF16),
            pltpu.VMEM((micro_count, capacity, 3 * capacity), BF16),
            pltpu.SemaphoreType.DMA((64,)),
            pltpu.SemaphoreType.DMA((64,)),
        ],
        compiler_params=pltpu.CompilerParams(
            collective_id=0, has_side_effects=True, vmem_limit_bytes=56 << 20
        ),
        name="attend",
    )(node_state, out_grad, index_rows, modulation, low_cat)
    state_all, cot_all, mod_all, a_one, queries, key_value, prob_low, mixed_all = gathered[:8]
    if own_gather:
        weight_all, output_all = gathered[8:]
    else:
        weight_all = low_cat
        output_all = lax.all_gather(
            low_cat[:, :, 3 * head_dim : 4 * head_dim], "heads", axis=0, tiled=False
        )
    weight_full = weight_all.reshape(full_width, weight_width)
    w_proj_low, w_out_low, w_exp_low, w_con_low = jnp.split(
        weight_full, (3 * head_dim, 4 * head_dim, 4 * head_dim + hidden), axis=1
    )
    output_full = output_all.reshape(head_count, full_width, head_dim).transpose(1, 0, 2).reshape(full_width, full_width)

    def rows_of(blocks):
        return blocks.transpose(1, 2, 0, 3).reshape(micro_count * capacity, full_width)

    def own_columns(rows):
        return lax.dynamic_slice_in_dim(rows, head_index * share, share, axis=1)

    def per_batch(number):
        terms = mod_all.reshape(head_count, micro_count, 4, share)[:, :, number].transpose(1, 0, 2)
        return jnp.repeat(terms.reshape(micro_count, full_width), capacity, axis=0)

    slot_ids = lax.broadcasted_iota(jnp.int32, (micro_count, capacity), 1)
    live = (slot_ids < patch_sizes).astype(F32).reshape(micro_count * capacity, 1)
    state = rows_of(state_all).astype(F32)
    mixed = rows_of(mixed_all)
    hidden_one = state + mul(mixed, output_full, NT)
    norm_two, root_two = norm_rows(hidden_one)
    scale_two = 1.0 + per_batch(3)
    a_two = (norm_two * scale_two + per_batch(2)).astype(BF16)
    up = mul(a_two, w_exp_low)
    gate = jax.nn.sigmoid(up)
    act = (up * gate).astype(BF16)
    result = own_columns(hidden_one) + lax.psum_scatter(
        mul(act, w_con_low, NT), "heads", scatter_dimension=1, tiled=True
    )
    layer_output = (result * live).astype(BF16).reshape(micro_count, capacity, share)
    cot = rows_of(cot_all) * live.astype(BF16)
    grad_act = mul(cot, w_con_low)
    grad_contract = mul(cot, act, TN)
    grad_up = (grad_act * gate * (1.0 + up * (1.0 - gate))).astype(BF16)
    grad_expand = mul(a_two, grad_up, TN)
    grad_two = lax.psum(mul(grad_up, w_exp_low, NT), "heads")

    def norm_back(grad, normed, root):
        mean_grad = jnp.sum(grad, axis=-1, keepdims=True) / full_width
        mean_cross = jnp.sum(grad * normed, axis=-1, keepdims=True) / full_width
        return root * (grad - mean_grad - normed * mean_cross)

    grad_hidden = cot.astype(F32) + norm_back(grad_two * scale_two, norm_two, root_two)
    grad_attn = grad_hidden.astype(BF16)
    grad_mixed = mul(grad_attn, w_out_low).astype(BF16).reshape(micro_count, capacity, head_dim)
    own_mixed = lax.dynamic_index_in_dim(mixed_all, head_index, 0, keepdims=False)
    grad_output = mul(grad_attn, own_mixed.reshape(-1, head_dim), TN)
    keys = key_value[..., :head_dim].reshape(micro_count, 3 * capacity, head_dim)
    values = key_value[..., head_dim:].reshape(micro_count, 3 * capacity, head_dim)
    grad_prob = jnp.einsum("brd,bmd->brm", grad_mixed, values, preferred_element_type=F32)
    prob = prob_low.astype(F32)
    grad_score = prob * (grad_prob - jnp.sum(prob * grad_prob, axis=-1, keepdims=True))
    grad_score = (grad_score * inv_head).astype(BF16)
    grad_query = jnp.einsum("brm,bmd->brd", grad_score, keys, preferred_element_type=F32)
    grad_keys = jnp.einsum("brm,brd->bmd", grad_score, queries, preferred_element_type=F32)
    grad_values = jnp.einsum("brm,brd->bmd", prob_low, grad_mixed, preferred_element_type=F32)
    grad_ext = jnp.concatenate([grad_keys, grad_values], axis=-1).reshape(
        micro_count, 3, capacity, 2 * head_dim
    )
    up_perm = [(i, (i + 1) % patch_count) for i in range(patch_count)]
    down_perm = [(j, i) for i, j in up_perm]
    grad_kv = (
        grad_ext[:, 1]
        + lax.ppermute(grad_ext[:, 0].astype(BF16), "nodes", down_perm)
        + lax.ppermute(grad_ext[:, 2].astype(BF16), "nodes", up_perm)
    )
    grad_projected = (
        jnp.concatenate([grad_query, grad_kv], axis=-1).astype(BF16).reshape(-1, 3 * head_dim)
    )
    a_own = a_one[1].reshape(-1, full_width)
    grad_project = mul(a_own, grad_projected, TN)
    grad_one = lax.psum_scatter(
        mul(grad_projected, w_proj_low, NT), "heads", scatter_dimension=1, tiled=True
    )
    norm_one, root_one = norm_rows(state)
    norm_one = own_columns(norm_one)
    scale_one = own_columns(1.0 + per_batch(1))
    grad_in = grad_one * scale_one
    mean_grad, mean_cross = lax.psum(
        (jnp.sum(grad_in, axis=-1, keepdims=True), jnp.sum(grad_in * norm_one, axis=-1, keepdims=True)),
        "heads",
    )
    input_grad = own_columns(grad_hidden) + root_one * (
        grad_in - mean_grad / full_width - norm_one * mean_cross / full_width
    )
    grad_two_own, norm_two_own = own_columns(grad_two), own_columns(norm_two)

    def node_sum(rows):
        return jnp.sum(rows.reshape(micro_count, capacity, share), axis=1)

    mod_summed = lax.psum(
        jnp.stack(
            [
                node_sum(grad_one),
                node_sum(grad_one * norm_one),
                node_sum(grad_two_own),
                node_sum(grad_two_own * norm_two_own),
            ],
            axis=1,
        ),
        "nodes",
    )
    grad_modulate = jnp.einsum("bc,bjd->jcd", noise_embed, mod_summed, precision=HIGH)
    grad_bias = jnp.sum(mod_summed, axis=0)

    grad_cat = jnp.concatenate([grad_project, grad_output, grad_expand, grad_contract], axis=1)
    moment_cat = jnp.concatenate(
        [momentum_project, momentum_output.T, momentum_expand, momentum_contract.T], axis=1
    )
    moment_cat = MOMENTUM_DECAY * moment_cat + lax.psum_scatter(
        grad_cat, "nodes", scatter_dimension=0, tiled=True
    )
    whole = lax.all_gather(moment_cat.astype(BF16), ("nodes", "heads"), axis=0, tiled=False)
    whole = whole.reshape(patch_count, head_count, shard_rows, weight_width)
    whole = whole.transpose(0, 2, 1, 3).reshape(full_width, head_count, weight_width).astype(F32)
    cuts = (0, 3 * head_dim, 4 * head_dim, 4 * head_dim + hidden, weight_width)
    factors = (1.0, 1.0, 1.0, (head_count * hidden / full_width) ** 0.5)
    pieces = []
    for number in range(4):
        columns = cuts[number + 1] - cuts[number]
        matrix = whole[:, :, cuts[number] : cuts[number + 1]].reshape(full_width, head_count * columns)
        ortho = lax.dynamic_slice(
            orthogonal(matrix), (patch_index * shard_rows, head_index * columns), (shard_rows, columns)
        )
        pieces.append(factors[number] * ortho)
    new_cat = weight_cat * (1.0 - LR_MUON * DECAY_WEIGHT) - LR_MUON * jnp.concatenate(pieces, axis=1)

    def unpack(cat):
        project, output, expand, contract = (cat[:, cuts[i] : cuts[i + 1]] for i in range(4))
        return (project, output.T, expand, contract.T)

    first_mod, second_mod, new_mod = adam_step(
        w_modulate, first_modulate, second_modulate, grad_modulate
    )
    first_b, second_b, new_b = adam_step(b_modulate, first_bias, second_bias, grad_bias)
    return (
        layer_output,
        input_grad.reshape(micro_count, capacity, share),
        *unpack(moment_cat),
        *unpack(new_cat),
        first_mod,
        second_mod,
        new_mod,
        first_b,
        second_b,
        new_b,
    )


def solution(mesh):
    in_specs = (
        P(None, "nodes", "heads"),
        P(),
        P(None, "nodes", "heads"),
        P(None, "nodes", None),
        P(None, "nodes"),
        P("nodes", "heads"),
        P("heads", "nodes"),
        P("nodes", "heads"),
        P("heads", "nodes"),
        P("nodes", "heads"),
        P("heads", "nodes"),
        P("nodes", "heads"),
        P("heads", "nodes"),
        P(None, None, "heads"),
        P(None, "heads"),
        P(None, None, "heads"),
        P(None, None, "heads"),
        P(None, "heads"),
        P(None, "heads"),
    )
    out_specs = (
        P(None, "nodes", "heads"),
        P(None, "nodes", "heads"),
        P("nodes", "heads"),
        P("heads", "nodes"),
        P("nodes", "heads"),
        P("heads", "nodes"),
        P("nodes", "heads"),
        P("heads", "nodes"),
        P("nodes", "heads"),
        P("heads", "nodes"),
        P(None, None, "heads"),
        P(None, None, "heads"),
        P(None, None, "heads"),
        P(None, "heads"),
        P(None, "heads"),
        P(None, "heads"),
    )
    return jax.shard_map(
        per_device, mesh=mesh, in_specs=in_specs, out_specs=out_specs, check_vma=False
    )
```

```python
import functools

import jax
import jax.numpy as jnp
from jax import lax
from jax.experimental import pallas as pl
from jax.experimental.pallas import tpu as pltpu
from jax.sharding import PartitionSpec as P

NS_STEPS = 5
STEP = 10


EPS_NORM = 1e-06
NEWTON_A = 3.4445
NEWTON_B = -4.775
NEWTON_C = 2.0315
MOMENTUM_DECAY = 0.5
LR_MUON = 1.0
LR_ADAM = 0.04
DECAY_WEIGHT = 0.01
BETA_FIRST = 0.9
BETA_SECOND = 0.999
EPS_ADAM = 1e-08
HIGH = lax.Precision.HIGHEST
MESH = pl.DeviceIdType.MESH
F32 = jnp.float32
BF16 = jnp.bfloat16
NN = (((1,), (0,)), ((), ()))
NT = (((1,), (1,)), ((), ()))
TN = (((0,), (0,)), ((), ()))


def mul(left, right, dims=NN):
    return lax.dot_general(left, right, dims, preferred_element_type=F32)


class Links:
    def __init__(self, send_sems, recv_sems):
        self.send_sems, self.recv_sems = send_sems, recv_sems
        self.copies, self.finished = [], []

    def send(self, source, target, device):
        slot = len(self.copies)
        copy = pltpu.make_async_remote_copy(
            src_ref=source,
            dst_ref=target,
            send_sem=self.send_sems.at[slot],
            recv_sem=self.recv_sems.at[slot],
            device_id=device,
            device_id_type=MESH,
        )
        copy.start()
        self.copies.append(copy)
        return copy

    def finish(self, copy):
        copy.wait_send()
        self.finished.append(copy)

    def close(self):
        for copy in self.copies:
            if not any(copy is other for other in self.finished):
                copy.wait_send()


def meet(devices):
    barrier = pltpu.get_barrier_semaphore()
    for device in devices:
        pl.semaphore_signal(barrier, inc=1, device_id=device, device_id_type=MESH)
    pl.semaphore_wait(barrier, len(devices))


def norm_rows(values):
    width = values.shape[-1]
    row_mean = jnp.sum(values, axis=-1, keepdims=True) / width
    square_mean = jnp.sum(values * values, axis=-1, keepdims=True) / width
    inv_root = lax.rsqrt(square_mean - row_mean * row_mean + EPS_NORM)
    return ((values - row_mean) * inv_root, inv_root)


def wide(ref, *index):
    return jnp.concatenate([ref[(head, *index)] for head in range(ref.shape[0])], axis=-1)


def mod_row(mod_ref, batch, number):
    return wide(mod_ref, slice(batch * 4 + number, batch * 4 + number + 1), slice(None))


def attend_kernel(
    patch_count,
    own_gather,
    state_ref,
    cot_ref,
    index_ref,
    mod_ref,
    weight_ref,
    state_all,
    cot_all,
    mod_all,
    a_one,
    queries,
    key_value,
    prob_low,
    mixed_all,
    weight_all,
    output_all,
    halo,
    count,
    send_sems,
    recv_sems,
):
    node, head = lax.axis_index("nodes"), lax.axis_index("heads")
    after, before = lax.rem(node + 1, patch_count), lax.rem(node + patch_count - 1, patch_count)
    across, sibling = lax.rem(head + 2, 4), head + 1 - 2 * lax.rem(head, 2)
    to_across, to_sibling, to_diagonal = (node, across), (node, sibling), (node, 3 - head)
    to_after, to_before = (after, head), (before, head)
    partner = node + 1 - 2 * lax.rem(node, 2)
    peers = [(lax.rem(node + 2 * k, patch_count), head) for k in range(1, patch_count // 2)]
    met = [to_across, to_sibling, to_diagonal, to_after, to_before]
    meet(met + peers if own_gather else met)
    micro_count, capacity, share = state_ref.shape
    head_dim = queries.shape[-1]
    total = 3 * capacity
    links = Links(send_sems, recv_sems)

    state_across = links.send(state_ref, state_all.at[head], to_across)
    state_after = links.send(state_ref, halo.at[0, head], to_after)
    state_before = links.send(state_ref, halo.at[1, head], to_before)
    state_sibling = links.send(state_ref, state_all.at[head], to_sibling)
    mod_copies = [
        links.send(mod_ref, mod_all.at[head], to)
        for to in (to_across, to_sibling, to_diagonal)
    ]
    first_columns, other_columns = pl.ds(0, 3 * head_dim), pl.ds(3 * head_dim, weight_ref.shape[-1] - 3 * head_dim)

    def spread(columns):
        part = weight_ref.at[:, columns]
        into = weight_all.at[node, :, columns]
        return [links.send(part, into, to) for to in peers], [
            links.send(part, into, (partner, head))
        ]

    def pass_on(arriving, columns):
        passed = []
        for k, copy in enumerate(arriving):
            copy.wait_recv()
            owner = lax.rem(node + patch_count - 2 * (k + 1), patch_count)
            passed.append(
                links.send(
                    weight_all.at[owner, :, columns],
                    weight_all.at[owner, :, columns],
                    (partner, head),
                )
            )
        return passed

    if own_gather:
        first_peers, first_partner = spread(first_columns)
        weight_all[node] = weight_ref[...]
    state_all[head] = state_ref[...]
    cot_all[head] = cot_ref[...]
    mod_all[head] = mod_ref[...]

    group = index_ref.shape[-1] // 16
    blocks = total // share

    def count_group(batch, place):
        ids = index_ref[batch, pl.ds(place, 1), :]
        lanes = lax.broadcasted_iota(jnp.int32, ids.shape, 1)
        code = (ids >> 7) + 16 * (lanes >> 4)
        rows = lax.broadcasted_iota(jnp.int32, (blocks * group, ids.shape[1]), 0)
        pick = jnp.where(code == (rows // group) + 16 * (rows % group), 1.0, 0.0).astype(BF16)
        slots = lax.broadcasted_iota(jnp.int32, (share, ids.shape[1]), 0)
        spot = jnp.where((ids & 127) == slots, 1.0, 0.0).astype(BF16)
        found = mul(pick, spot, NT).astype(BF16)
        for block in range(blocks):
            count[batch, pl.ds(pl.multiple_of(place * group, group), group), block * share : (block + 1) * share] = found[
                block * group : (block + 1) * group
            ]

    for batch in range(micro_count):

        @pl.loop(0, capacity // group)
        def _(place):
            count_group(batch, place)

    state_across.wait_recv()
    pass_state = links.send(state_all.at[across], state_all.at[across], to_sibling)
    halo_across, halo_sibling = [], []
    for side, copy in ((0, state_after), (1, state_before)):
        copy.wait_recv()
        halo_across.append(links.send(halo.at[side, head], halo.at[side, head], to_across))
        halo_sibling.append(links.send(halo.at[side, head], halo.at[side, head], to_sibling))
    if own_gather:
        first_passed = pass_on(first_peers, first_columns)
        other_peers, other_partner = spread(other_columns)
    state_sibling.wait_recv()
    pass_state.wait_recv()
    for copy in mod_copies:
        copy.wait_recv()
    if own_gather:
        for copy in first_partner + first_passed:
            copy.wait_recv()
    inv_head = head_dim ** (-0.5)
    tile = capacity // 2

    def project(source, patch):
        for batch in range(micro_count):
            shift, scale = mod_row(mod_all, batch, 0), 1.0 + mod_row(mod_all, batch, 1)

            @pl.loop(0, capacity // tile)
            def _(step):
                rows = pl.ds(pl.multiple_of(step * tile, tile), tile)
                normed, _ = norm_rows(wide(source, batch, rows, slice(None)).astype(F32))
                a_rows = (normed * scale + shift).astype(BF16)
                a_one[patch, batch, rows, :] = a_rows
                first = 0 if patch == 1 else head_dim
                weight = weight_all[:, :, first : 3 * head_dim].reshape(4 * share, 3 * head_dim - first)
                out = mul(a_rows, weight).astype(BF16)
                if patch == 1:
                    queries[batch, rows, :] = out[:, :head_dim]
                key_value[batch, patch, rows, :] = out[:, out.shape[1] - 2 * head_dim :]

    project(state_all, 1)
    for side in range(2):
        halo_across[side].wait_recv()
        halo_sibling.append(links.send(halo.at[side, across], halo.at[side, across], to_sibling))
    cot_across = links.send(cot_ref, cot_all.at[head], to_across)
    cot_sibling = links.send(cot_ref, cot_all.at[head], to_sibling)
    for copy in halo_sibling:
        copy.wait_recv()
    project(halo.at[0], 0)
    project(halo.at[1], 2)
    if own_gather:
        other_passed = pass_on(other_peers, other_columns)

    attend_rows = 128
    mixed_copies = []
    for batch in range(micro_count):

        @pl.loop(0, capacity // attend_rows)
        def _(step):
            rows = pl.ds(pl.multiple_of(step * attend_rows, attend_rows), attend_rows)
            keys = key_value[batch, :, :, :head_dim].reshape(total, head_dim)
            values = key_value[batch, :, :, head_dim:].reshape(total, head_dim)
            scores = mul(queries[batch, rows, :], keys, NT) * inv_head
            times = count[batch, rows, :].astype(F32)
            scores = jnp.where(times > 0.0, scores, -1e30)
            exps = jnp.exp(scores - jnp.max(scores, axis=-1, keepdims=True)) * times
            prob = (exps * (1.0 / jnp.sum(exps, axis=-1, keepdims=True))).astype(BF16)
            prob_low[batch, rows, :] = prob
            mixed_all[head, batch, rows, :] = mul(prob, values).astype(BF16)

        part = mixed_all.at[head, batch]
        mixed_copies.append(
            (batch, links.send(part, part, to_across), links.send(part, part, to_sibling))
        )

    cot_across.wait_recv()
    last = [cot_sibling, links.send(cot_all.at[across], cot_all.at[across], to_sibling)]
    if own_gather:
        for copy in other_partner + other_passed:
            copy.wait_recv()
        output_columns = pl.ds(3 * head_dim, head_dim)
        output_all[head] = weight_all[:, :, 3 * head_dim : 4 * head_dim]
        output_part = weight_all.at[:, :, output_columns]
        output_across = links.send(output_part, output_all.at[head], to_across)
        last.append(links.send(output_part, output_all.at[head], to_sibling))
        output_across.wait_recv()
        last.append(links.send(output_all.at[across], output_all.at[across], to_sibling))
    for batch, copy, other in mixed_copies:
        copy.wait_recv()
        part = mixed_all.at[across, batch]
        last += [other, links.send(part, part, to_sibling)]
    for copy in last:
        copy.wait_recv()
    links.close()


def update_kernel(
    patch_count,
    own_gather,
    sizes_ref,
    state_all,
    cot_all,
    mod_all,
    a_one,
    queries,
    key_value,
    prob_low,
    mixed_all,
    weight_all,
    output_all,
    moment_ref,
    weight_ref,
    layer_output,
    input_grad,
    moment_new,
    weight_new,
    mod_sum,
    hidden_one,
    a_two,
    act,
    grad_up,
    part_two,
    part_core,
    part_low,
    part_across,
    total_two,
    out_low,
    out_core,
    out_keep,
    out_across,
    grad_hidden,
    grad_attn,
    grad_mixed,
    score_low,
    grad_own,
    grad_away,
    grad_back,
    grad_projected,
    mod_part,
    mod_in,
    grad_cat,
    grad_low,
    grad_core,
    grad_line,
    moment_low,
    matrix,
    gram_left,
    gram_right,
    factor_left,
    chain,
    turn_right,
    ortho_out,
    ortho_in,
    send_sems,
    recv_sems,
    turn_send,
    turn_recv,
):
    node, head = lax.axis_index("nodes"), lax.axis_index("heads")
    after, before = lax.rem(node + 1, patch_count), lax.rem(node + patch_count - 1, patch_count)
    across, sibling = lax.rem(head + 2, 4), head + 1 - 2 * lax.rem(head, 2)
    to_across, to_sibling = (node, across), (node, sibling)
    to_after, to_before = (after, head), (before, head)
    side, core = lax.div(head, 2), lax.rem(head, 2)
    plane, parity = lax.div(node, 2), lax.rem(node, 2)
    to_partner = (node + 1 - 2 * parity, head)
    met = [to_across, to_sibling]
    if own_gather:
        met += [(lax.rem(node + k, patch_count), head) for k in range(1, patch_count)]
    else:
        met += [to_after, to_before]
    meet(met)
    links = Links(send_sems, recv_sems)
    micro_count, capacity, head_dim = queries.shape
    full_width = a_one.shape[-1]
    total = 3 * capacity
    hidden = act.shape[-1]
    inv_head = head_dim ** (-0.5)
    cuts = (0, 3 * head_dim, 4 * head_dim, 4 * head_dim + hidden, 4 * head_dim + 2 * hidden)
    expand_columns, contract_columns = slice(cuts[2], cuts[3]), slice(cuts[3], cuts[4])
    tile = capacity // 2

    def weight(columns):
        return weight_all[:, :, columns].reshape(full_width, columns.stop - columns.start)

    def live_rows(batch, start, count):
        slots = lax.broadcasted_iota(jnp.int32, (count, 1), 0) + start
        return (slots < sizes_ref[batch, 0]).astype(F32)

    def rows_at(step, count):
        start = step * count if isinstance(step, int) else pl.multiple_of(step * count, count)
        return start, pl.ds(start, count)

    def feed_forward(batch, step):
        start, rows = rows_at(step, tile)
        mixed = wide(mixed_all, batch, rows, slice(None))
        mixer = jnp.concatenate(
            [output_all[k].reshape(full_width, head_dim) for k in range(output_all.shape[0])], axis=-1
        )
        hid = wide(state_all, batch, rows, slice(None)).astype(F32) + mul(mixed, mixer, NT)
        hidden_one[batch, rows, :] = hid
        normed, _ = norm_rows(hid)
        a_rows = (normed * (1.0 + mod_row(mod_all, batch, 3)) + mod_row(mod_all, batch, 2)).astype(BF16)
        a_two[batch, rows, :] = a_rows
        up = mul(a_rows, weight(expand_columns))
        gate = jax.nn.sigmoid(up)
        acted = (up * gate).astype(BF16)
        act[batch, rows, :] = acted
        live = live_rows(batch, start, tile)
        cot = (wide(cot_all, batch, rows, slice(None)).astype(F32) * live).astype(BF16)
        grad_act = mul(cot, weight(contract_columns))
        grad_rows = (grad_act * gate * (1.0 + up * (1.0 - gate))).astype(BF16)
        grad_up[batch, rows, :] = grad_rows
        back = mul(grad_rows, weight(expand_columns), NT)
        out = mul(acted, weight(contract_columns), NT)
        for k in range(4):
            block = slice(k * head_dim, (k + 1) * head_dim)
            part_two[batch, k % 2, k // 2, rows, :] = back[:, block]
            out_low[batch, k % 2, k // 2, rows, :] = out[:, block].astype(BF16)

    def to_core(batch):
        return links.send(part_two.at[batch, 1 - core], part_core.at[batch], to_sibling)

    def to_side(batch, copy):
        copy.wait_recv()
        for k in range(2):
            chip = part_two[batch, core, k] + part_core[batch, k]
            part_core[batch, k] = chip
            part_low[batch, k] = chip.astype(BF16)
        return links.send(part_low.at[batch], part_across.at[batch], to_across)

    def to_all(batch, copy):
        copy.wait_recv()
        for k in range(2):
            total_two[batch, core, k] = part_core[batch, k] + part_across[batch, k].astype(F32)
        return links.send(total_two.at[batch, core], total_two.at[batch, core], to_sibling)

    def total_rows(batch, rows):
        return jnp.concatenate(
            [total_two[batch, k % 2, k // 2, rows, :] for k in range(4)], axis=-1
        )

    def back_norm(grad, normed, root):
        mean_grad = jnp.sum(grad, axis=-1, keepdims=True) / full_width
        mean_cross = jnp.sum(grad * normed, axis=-1, keepdims=True) / full_width
        return root * (grad - mean_grad - normed * mean_cross)

    def add_mod(batch, number, values):
        sums = jnp.sum(values, axis=0, keepdims=True)
        place = batch * 4 + number
        for k in range(4):
            mod_part[k, place : place + 1, :] += sums[:, k * head_dim : (k + 1) * head_dim]

    for k in range(4):
        mod_part[k] = jnp.zeros(mod_part.shape[1:], F32)

    pl.loop(0, 2)(lambda step: feed_forward(0, step))
    core_first = to_core(0)
    feed_forward(1, 0)
    side_first = to_side(0, core_first)
    feed_forward(1, 1)
    core_second = to_core(1)

    def store_grad(step, columns, value):
        half = full_width // 8
        for k in range(2):
            part = value[k * half : (k + 1) * half]
            grad_cat[k, step, :, columns] = part
            grad_low[k, step, :, columns] = part.astype(BF16)

    def both(ref, columns):
        return ref[:, :, columns].reshape(micro_count * capacity, -1)

    def live_cot(batch, columns):
        return (cot_all[columns, batch].astype(F32) * live_rows(batch, 0, capacity)).astype(BF16)

    @pl.loop(0, 4)
    def _(step):
        columns = pl.ds(pl.multiple_of(step * head_dim, head_dim), head_dim)
        store_grad(step, expand_columns, mul(both(a_two, columns), grad_up[...].reshape(-1, hidden), TN))
        cot = jnp.concatenate([live_cot(b, step) for b in range(micro_count)], axis=0)
        store_grad(step, contract_columns, mul(cot, act[...].reshape(-1, hidden), TN))

    early, late = slice(cuts[2], cuts[4]), slice(0, cuts[2])

    def grad_pair(columns):
        return links.send(
            grad_low.at[1 - parity, :, :, columns], grad_core.at[:, :, columns], to_partner
        )

    def grad_planes(copy, columns):
        copy.wait_recv()
        for k in range(4):
            summed = grad_cat[parity, k, :, columns] + grad_core[k, :, columns].astype(F32)
            grad_cat[parity, k, :, columns] = summed
            grad_low[parity, k, :, columns] = summed.astype(BF16)
        sent = []
        for k in range(1, 4):
            target = lax.rem(plane + k, 4)
            sent.append(
                links.send(
                    grad_low.at[parity, target, :, columns],
                    grad_line.at[k - 1, :, columns],
                    (2 * target + parity, head),
                )
            )
        return sent

    def grad_finish(copies, columns):
        for copy in copies:
            copy.wait_recv()
        summed = grad_cat[parity, plane, :, columns]
        for k in range(3):
            summed = summed + grad_line[k, :, columns].astype(F32)
        moment_new[:, columns] = MOMENTUM_DECAY * moment_ref[:, columns] + summed

    if own_gather:
        early_pair = grad_pair(early)
    side_second = to_side(1, core_second)
    all_first = to_all(0, side_first)
    out_copies = [
        links.send(out_low.at[b, 1 - core], out_core.at[b], to_sibling) for b in range(micro_count)
    ]

    def norm_two_back(batch):
        @pl.loop(0, capacity // tile)
        def _(step):
            start, rows = rows_at(step, tile)
            normed, root = norm_rows(hidden_one[batch, rows, :])
            grad = total_rows(batch, rows)
            add_mod(batch, 2, grad)
            add_mod(batch, 3, grad * normed)
            cot = wide(cot_all, batch, rows, slice(None)).astype(F32) * live_rows(batch, start, tile)
            grad = cot + back_norm(grad * (1.0 + mod_row(mod_all, batch, 3)), normed, root)
            for k in range(4):
                grad_hidden[k, batch, rows, :] = grad[:, k * head_dim : (k + 1) * head_dim]
            low = grad.astype(BF16)
            grad_attn[batch, rows, :] = low
            grad_mixed[batch, rows, :] = mul(low, weight(slice(cuts[1], cuts[2]))).astype(BF16)

    def attend_back(batch):
        attend_rows = 128

        @pl.loop(0, capacity // attend_rows)
        def _(step):
            _, rows = rows_at(step, attend_rows)
            keys = key_value[batch, :, :, :head_dim].reshape(total, head_dim)
            values = key_value[batch, :, :, head_dim:].reshape(total, head_dim)
            prob = prob_low[batch, rows, :].astype(F32)
            grad_prob = mul(grad_mixed[batch, rows, :], values, NT)
            mean = jnp.sum(prob * grad_prob, axis=-1, keepdims=True)
            score = (prob * (grad_prob - mean) * inv_head).astype(BF16)
            score_low[rows, :] = score
            grad_projected[batch, rows, :head_dim] = mul(score, keys).astype(BF16)

        for patch in range(3):
            slots = slice(patch * capacity, (patch + 1) * capacity)
            grad_key = mul(score_low[:, slots], queries[batch], TN)
            grad_value = mul(prob_low[batch, :, slots], grad_mixed[batch], TN)
            if patch == 1:
                grad_own[batch, :, :head_dim] = grad_key
                grad_own[batch, :, head_dim:] = grad_value
            else:
                grad_away[batch, patch // 2, :, :head_dim] = grad_key.astype(BF16)
                grad_away[batch, patch // 2, :, head_dim:] = grad_value.astype(BF16)

    def send_back(batch):
        return [
            links.send(grad_away.at[batch, 0], grad_back.at[batch, 1], to_before),
            links.send(grad_away.at[batch, 1], grad_back.at[batch, 0], to_after),
        ]

    all_first.wait_recv()
    norm_two_back(0)
    attend_back(0)
    back_first = send_back(0)
    all_second = to_all(1, side_second)
    if own_gather:
        early_line = grad_planes(early_pair, early)
    out_across_copies = []
    for batch in range(micro_count):
        out_copies[batch].wait_recv()
        for k in range(2):
            chip = out_low[batch, core, k].astype(F32) + out_core[batch, k].astype(F32)
            out_keep[batch, k] = chip
            out_core[batch, k] = chip.astype(BF16)
        out_across_copies.append(
            links.send(out_core.at[batch, 1 - side], out_across.at[batch], to_across)
        )
    all_second.wait_recv()
    norm_two_back(1)
    attend_back(1)

    @pl.loop(0, 4)
    def _(step):
        columns = pl.ds(pl.multiple_of(step * head_dim, head_dim), head_dim)
        queries_part = mul(both(a_one.at[1], columns), both(grad_projected, slice(0, head_dim)), TN)
        store_grad(step, slice(0, head_dim), queries_part)
        rest = mul(both(a_one.at[1], columns), grad_own[...].reshape(-1, 2 * head_dim).astype(BF16), TN)
        for patch in (0, 2):
            away = grad_away[:, patch // 2].reshape(-1, 2 * head_dim)
            rest = rest + mul(both(a_one.at[patch], columns), away, TN)
        store_grad(step, slice(head_dim, cuts[1]), rest)
        own_mixed = mixed_all[head].reshape(-1, head_dim)
        store_grad(step, slice(cuts[1], cuts[2]), mul(both(grad_attn, columns), own_mixed, TN))

    if own_gather:
        late_pair = grad_pair(late)
    back_second = send_back(1)
    if own_gather:
        grad_finish(early_line, early)
        late_line = grad_planes(late_pair, late)
    for batch in range(micro_count):
        out_across_copies[batch].wait_recv()
        own = hidden_one[batch, :, pl.ds(pl.multiple_of(head * head_dim, head_dim), head_dim)]
        result = own + out_keep[batch, side] + out_across[batch].astype(F32)
        layer_output[batch] = (result * live_rows(batch, 0, capacity)).astype(BF16)

    def turn(source, target, device, send_slot, recv_slot):
        return pltpu.make_async_remote_copy(
            src_ref=source,
            dst_ref=target,
            send_sem=turn_send.at[send_slot],
            recv_sem=turn_recv.at[recv_slot],
            device_id=device,
            device_id_type=MESH,
        )

    widths = (3 * head_dim, head_dim, hidden, hidden)

    def to_owner(number):
        columns = slice(cuts[number], cuts[number + 1])
        return turn(
            moment_low.at[:, columns],
            matrix.at[head, parity, plane, :, : widths[number]],
            (2 * number + parity, head),
            number,
            plane,
        )

    if own_gather:
        grad_finish(late_line, late)
        moment_low[...] = moment_new[...].astype(BF16)
        for number in range(4):
            columns = slice(cuts[number], cuts[number + 1])

            @pl.when(plane != number)
            def _():
                to_owner(number).start()

            @pl.when(plane == number)
            def _():
                matrix[head, parity, plane, :, : widths[number]] = moment_low[:, columns]

        for number in range(4):

            @pl.when(plane == number)
            def _():
                for other in range(4):
                    if other != number:
                        turn(
                            moment_low.at[:, slice(cuts[number], cuts[number + 1])],
                            matrix.at[head, parity, other, :, : widths[number]],
                            (2 * number + parity, head),
                            number,
                            other,
                        ).wait_recv()

            @pl.when(plane != number)
            def _():
                to_owner(number).wait_send()

        def gather_plane(width):
            sends = []

            def give(block, pair, device):
                slot = 4 + len(sends)
                part = matrix.at[block, pair, :, :, :width]
                copy = turn(part, part, device, slot, slot)
                copy.start()
                sends.append(copy)
                return copy

            mirror = 1 - parity
            first_across = give(head, parity, to_across)
            first_partner = give(head, parity, to_partner)
            waits = [give(head, parity, to_sibling)]
            first_across.wait_recv()
            waits.append(give(across, parity, to_partner))
            waits.append(give(across, parity, to_sibling))
            first_partner.wait_recv()
            waits.append(give(head, mirror, to_sibling))
            waits[1].wait_recv()
            waits.append(give(across, mirror, to_sibling))
            for copy in waits[:1] + waits[2:]:
                copy.wait_recv()
            for copy in sends:
                copy.wait_send()
            half = full_width // 2

            @pl.loop(0, 2)
            def _(step):
                _, rows = rows_at(step, half)
                gram = jnp.zeros((half, full_width), F32)
                for k in range(4):
                    left = matrix[k, step, :, :, :width].reshape(half, width)
                    right = matrix[k, :, :, :, :width].reshape(full_width, width)
                    gram = gram + mul(left, right, NT)
                chain[rows, :] = gram

        for low, high, width in ((0, 1, widths[0]), (1, 2, widths[1]), (2, 4, hidden)):

            @pl.when((plane >= low) & (plane < high))
            def _():
                gather_plane(width)

        half = full_width // 2
        wide_shape = (half, full_width)

        def split(value):
            high = value.astype(BF16)
            return high, (value - high.astype(F32)).astype(BF16)

        def put_left(ref, rows, value):
            high, low = split(value)
            ref[rows, :full_width] = high
            ref[rows, full_width : 2 * full_width] = high
            ref[rows, 2 * full_width :] = low

        def put_right(ref, rows, value):
            high, low = split(value)
            ref[0, rows, :] = high
            ref[1, rows, :] = low
            ref[2, rows, :] = high

        def times(left, rows, right):
            return mul(left[rows, :], right[...].reshape(3 * full_width, full_width))

        def diagonal(start):
            rows = lax.broadcasted_iota(jnp.int32, wide_shape, 0) + start
            return rows == lax.broadcasted_iota(jnp.int32, wide_shape, 1)

        trace = jnp.zeros((1, 1), F32)
        for step in range(2):
            rows = slice(step * half, (step + 1) * half)
            kept = jnp.where(diagonal(step * half), chain[rows, :], 0.0)
            trace = trace + jnp.sum(jnp.sum(kept, axis=1, keepdims=True), axis=0, keepdims=True)
        scale = 1.0 / (jnp.sqrt(trace) + 1e-07)

        @pl.loop(0, 2)
        def _(step):
            _, rows = rows_at(step, half)
            gram = chain[rows, :] * (scale * scale)
            chain[rows, :] = gram
            put_left(gram_left, rows, gram)
            put_right(gram_right, rows, gram)

        def polynomial(repeat):
            @pl.loop(0, 2)
            def _(step):
                start, rows = rows_at(step, half)
                gram = chain[rows, :]
                factor = NEWTON_B * gram + NEWTON_C * times(gram_left, rows, gram_right)
                factor = factor + jnp.where(diagonal(start), NEWTON_A, 0.0)
                put_left(factor_left, rows, factor)

        done = 0
        for repeat in range(NS_STEPS):
            polynomial(repeat)
            if repeat == 0:

                @pl.loop(0, 2)
                def _(step):
                    _, rows = rows_at(step, half)
                    high, low = factor_left[rows, :full_width], factor_left[rows, 2 * full_width :]
                    turn_right[0, 0, rows, :] = high
                    turn_right[0, 1, rows, :] = low
                    turn_right[0, 2, rows, :] = high

            else:

                @pl.loop(0, 2)
                def _(step):
                    _, rows = rows_at(step, half)
                    product = times(factor_left, rows, turn_right.at[done])
                    put_right(turn_right.at[2 - done], rows, product)

                done = 2 - done

            if repeat < NS_STEPS - 1:

                @pl.loop(0, 2)
                def _(step):
                    _, rows = rows_at(step, half)
                    put_right(turn_right.at[1], rows, times(factor_left, rows, gram_right))

                @pl.loop(0, 2)
                def _(step):
                    _, rows = rows_at(step, half)
                    gram = times(factor_left, rows, turn_right.at[1])
                    chain[rows, :] = gram
                    put_left(gram_left, rows, gram)
                    put_right(gram_right, rows, gram)

        def spread_ortho(number):
            width = widths[number]
            left = jnp.concatenate(
                [turn_right[done, k, pl.ds(pl.multiple_of(parity * half, half), half), :] for k in range(2)], axis=-1
            )
            right = matrix[head, :, :, :, :width].reshape(full_width, width)
            right = jnp.concatenate([right, right], axis=0)
            value = (mul(left, right) * scale).astype(BF16)
            ortho_out[:, :, :width] = value.reshape(4, half // 4, width)
            ortho_in[number, :, :width] = ortho_out[plane, :, :width]
            for k in range(1, 4):
                ortho_copy(number, k).start()

        def ortho_copy(number, k):
            target = (number + k) % 4
            width = widths[number]
            return turn(
                ortho_out.at[target, :, :width],
                ortho_in.at[number, :, :width],
                (2 * target + parity, head),
                12 + k,
                12 + number,
            )

        for number in range(4):

            @pl.when(plane == number)
            def _():
                spread_ortho(number)

    for copy in (core_first, core_second, side_first, side_second, all_first, all_second):
        links.finish(copy)
    for batch, copies in enumerate((back_first, back_second)):
        for copy in copies:
            copy.wait_recv()
        whole = grad_own[batch] + grad_back[batch, 0].astype(F32) + grad_back[batch, 1].astype(F32)
        grad_projected[batch, :, head_dim:] = whole.astype(BF16)

        @pl.loop(0, capacity // tile)
        def _(step):
            _, rows = rows_at(step, tile)
            back = mul(grad_projected[batch, rows, :], weight(slice(0, cuts[1])), NT)
            for k in range(4):
                part_two[batch, k % 2, k // 2, rows, :] = back[:, k * head_dim : (k + 1) * head_dim]

    one_core = [to_core(b) for b in range(micro_count)]
    one_side = [to_side(b, one_core[b]) for b in range(micro_count)]
    one_all = [to_all(b, one_side[b]) for b in range(micro_count)]
    for batch in range(micro_count):
        one_all[batch].wait_recv()

        @pl.loop(0, capacity // tile)
        def _(step):
            _, rows = rows_at(step, tile)
            normed, root = norm_rows(wide(state_all, batch, rows, slice(None)).astype(F32))
            grad = total_rows(batch, rows)
            add_mod(batch, 0, grad)
            add_mod(batch, 1, grad * normed)
            grad = back_norm(grad * (1.0 + mod_row(mod_all, batch, 1)), normed, root)
            own = jnp.zeros((tile, head_dim), F32)
            for k in range(4):
                own = own + jnp.where(head == k, grad[:, k * head_dim : (k + 1) * head_dim], 0.0)
            input_grad[batch, rows, :] = own + grad_hidden[head, batch, rows, :]

    if own_gather:
        mod_copies = [
            links.send(mod_part.at[head], mod_in.at[k - 1], (lax.rem(node + k, patch_count), head))
            for k in range(1, patch_count)
        ]
        for number in range(4):

            @pl.when(plane != number)
            def _():
                ortho_copy(number, 1).wait_recv()

            columns = slice(cuts[number], cuts[number + 1])
            factor = (4.0 * hidden / full_width) ** 0.5 if number == 3 else 1.0
            weight_new[:, columns] = weight_ref[:, columns] * (1.0 - LR_MUON * DECAY_WEIGHT) - (
                LR_MUON * factor
            ) * ortho_in[number, :, : widths[number]].astype(F32)

            @pl.when(plane == number)
            def _():
                for k in range(1, 4):
                    ortho_copy(number, k).wait_send()

        summed = mod_part[head]
        for copy in mod_copies:
            copy.wait_recv()
        for k in range(patch_count - 1):
            summed = summed + mod_in[k]
        mod_sum[...] = summed
    else:
        mod_sum[...] = mod_part[head]
        for k in range(8):
            moment_new[k] = grad_cat[k % 2, k // 2]
    links.close()


def adam_step(weight, first_old, second_old, gradient):
    first_new = BETA_FIRST * first_old + (1.0 - BETA_FIRST) * gradient
    second_new = BETA_SECOND * second_old + (1.0 - BETA_SECOND) * gradient * gradient
    first_hat = first_new / (1.0 - BETA_FIRST**STEP)
    second_hat = second_new / (1.0 - BETA_SECOND**STEP)
    updated = weight * (1.0 - LR_ADAM * DECAY_WEIGHT) - LR_ADAM * first_hat / (
        jnp.sqrt(second_hat) + EPS_ADAM
    )
    return (first_new, second_new, updated)


def orthogonal(matrix):
    scale = 1.0 / (jnp.sqrt(jnp.sum(matrix * matrix)) + 1e-07)
    gram = jnp.dot(matrix, matrix.T, precision=HIGH) * (scale * scale)
    eye = jnp.eye(gram.shape[0], dtype=F32)
    chain = None
    for repeat in range(NS_STEPS):
        factor = NEWTON_A * eye + NEWTON_B * gram + NEWTON_C * jnp.dot(gram, gram, precision=HIGH)
        chain = factor if chain is None else jnp.dot(factor, chain, precision=HIGH)
        if repeat < NS_STEPS - 1:
            gram = jnp.dot(factor, jnp.dot(factor, gram, precision=HIGH), precision=HIGH)
    return jnp.dot(chain, matrix, precision=HIGH) * scale


def per_device(
    node_state,
    noise_embed,
    out_grad,
    neighbours,
    patch_sizes,
    w_project,
    w_output,
    w_expand,
    w_contract,
    momentum_project,
    momentum_output,
    momentum_expand,
    momentum_contract,
    w_modulate,
    b_modulate,
    first_modulate,
    second_modulate,
    first_bias,
    second_bias,
):
    micro_count, capacity, share = node_state.shape
    head_count = lax.axis_size("heads")
    patch_count = lax.axis_size("nodes")
    full_width = share * head_count
    head_dim = w_output.shape[0]
    total_rows = capacity * patch_count
    patch_index = lax.axis_index("nodes")
    head_index = lax.axis_index("heads")
    inv_head = head_dim ** (-0.5)
    hidden = w_expand.shape[1]
    shard_rows = w_project.shape[0]
    own_gather = patch_count == 8

    modulation = (
        jnp.einsum("bc,jcd->bjd", noise_embed, w_modulate, precision=HIGH) + b_modulate
    ).reshape(micro_count * 4, share)
    local_index = jnp.mod(neighbours - (patch_index - 1) * capacity, total_rows)
    index_rows = local_index.reshape(micro_count, capacity // 16, 256)
    weight_cat = jnp.concatenate([w_project, w_output.T, w_expand, w_contract.T], axis=1)
    low_cat = weight_cat.astype(BF16)
    weight_width = low_cat.shape[1]
    if not own_gather:
        low_cat = lax.all_gather(low_cat, "nodes", axis=0, tiled=True).reshape(8, full_width // 8, weight_width)
    vmem = pl.BlockSpec(memory_space=pltpu.VMEM)
    rows_all = jax.ShapeDtypeStruct((head_count, micro_count, capacity, share), BF16)
    out_shape = [
        rows_all,
        rows_all,
        jax.ShapeDtypeStruct((head_count, micro_count * 4, share), F32),
        jax.ShapeDtypeStruct((3, micro_count, capacity, full_width), BF16),
        jax.ShapeDtypeStruct((micro_count, capacity, head_dim), BF16),
        jax.ShapeDtypeStruct((micro_count, 3, capacity, 2 * head_dim), BF16),
        jax.ShapeDtypeStruct((micro_count, capacity, 3 * capacity), BF16),
        rows_all,
    ]
    if own_gather:
        out_shape += [
            jax.ShapeDtypeStruct((patch_count, shard_rows, weight_width), BF16),
            jax.ShapeDtypeStruct((head_count, patch_count, shard_rows, head_dim), BF16),
        ]

    def attend_body(*refs):
        refs = list(refs)
        if not own_gather:
            refs[13:13] = [refs[4], None]
        attend_kernel(patch_count, own_gather, *refs)

    gathered = pl.pallas_call(
        attend_body,
        out_shape=out_shape,
        in_specs=[vmem] * 5,
        out_specs=[vmem] * len(out_shape),
        scratch_shapes=[
            pltpu.VMEM((2, head_count, micro_count, capacity, share), BF16),
            pltpu.VMEM((micro_count, capacity, 3 * capacity), BF16),
            pltpu.SemaphoreType.DMA((64,)),
            pltpu.SemaphoreType.DMA((64,)),
        ],
        compiler_params=pltpu.CompilerParams(
            collective_id=0, has_side_effects=True, vmem_limit_bytes=56 << 20
        ),
        name="attend",
    )(node_state, out_grad, index_rows, modulation, low_cat)
    state_all, cot_all, mod_all, a_one, queries, key_value, prob_low, mixed_all = gathered[:8]
    if own_gather:
        weight_all, output_all = gathered[8:]
    else:
        weight_all = low_cat
        output_all = lax.all_gather(
            low_cat[:, :, 3 * head_dim : 4 * head_dim], "heads", axis=0, tiled=False
        )
    moment_cat = jnp.concatenate(
        [momentum_project, momentum_output.T, momentum_expand, momentum_contract.T], axis=1
    )

    def scratch(dtype, *shape):
        return pltpu.VMEM(shape, dtype)

    blocks = (micro_count, 2, 2, capacity, head_dim)
    half_blocks = (micro_count, 2, capacity, head_dim)
    rows_wide = (micro_count, capacity, full_width)
    rows_hidden = (micro_count, capacity, hidden)
    key_value_rows = (capacity, 2 * head_dim)
    eighth = full_width // 8
    scratches = [
        scratch(F32, *rows_wide),
        scratch(BF16, *rows_wide),
        scratch(BF16, *rows_hidden),
        scratch(BF16, *rows_hidden),
        scratch(F32, *blocks),
        scratch(F32, *half_blocks),
        scratch(BF16, *half_blocks),
        scratch(BF16, *half_blocks),
        scratch(F32, *blocks),
        scratch(BF16, *blocks),
        scratch(BF16, *half_blocks),
        scratch(F32, *half_blocks),
        scratch(BF16, micro_count, capacity, head_dim),
        scratch(F32, head_count, micro_count, capacity, head_dim),
        scratch(BF16, *rows_wide),
        scratch(BF16, micro_count, capacity, head_dim),
        scratch(BF16, capacity, 3 * capacity),
        scratch(F32, micro_count, *key_value_rows),
        scratch(BF16, micro_count, 2, *key_value_rows),
        scratch(BF16, micro_count, 2, *key_value_rows),
        scratch(BF16, micro_count, capacity, 3 * head_dim),
        scratch(F32, head_count, 4 * micro_count, share),
        scratch(F32, 8, 4 * micro_count, share),
        scratch(F32, 2, 4, eighth, weight_width),
        scratch(BF16, 2, 4, eighth, weight_width),
        scratch(BF16, 4, eighth, weight_width),
        scratch(BF16, 3, eighth, weight_width),
    ]
    if own_gather:
        scratches += [
            scratch(BF16, eighth, weight_width),
            scratch(BF16, head_count, 2, 4, eighth, hidden),
            scratch(BF16, full_width, 3 * full_width),
            scratch(BF16, 3, full_width, full_width),
            scratch(BF16, full_width, 3 * full_width),
            scratch(F32, full_width, full_width),
            scratch(BF16, 3, 3, full_width, full_width),
            scratch(BF16, 4, eighth, hidden),
            scratch(BF16, 4, eighth, hidden),
        ]
    semaphores = [pltpu.SemaphoreType.DMA((count,)) for count in (64, 64, 16, 16)]
    operands = [
        patch_sizes,
        state_all,
        cot_all,
        mod_all,
        a_one,
        queries,
        key_value,
        prob_low,
        mixed_all,
        weight_all,
        output_all.reshape(head_count, 8, eighth, head_dim),
    ]
    out_shape = [
        jax.ShapeDtypeStruct((micro_count, capacity, share), BF16),
        jax.ShapeDtypeStruct((micro_count, capacity, share), F32),
    ]
    summed_shape = jax.ShapeDtypeStruct((4 * micro_count, share), F32)
    if own_gather:
        operands += [moment_cat, weight_cat]
        shard = jax.ShapeDtypeStruct(weight_cat.shape, F32)
        out_shape += [shard, shard, summed_shape]
    else:
        out_shape += [jax.ShapeDtypeStruct((8, eighth, weight_width), F32), summed_shape]

    def update_body(*refs):
        refs = list(refs)
        if not own_gather:
            refs[11:11] = [None, None]
            refs[16:16] = [None]
            refs[-4:-4] = [None] * 9
        update_kernel(patch_count, own_gather, *refs)

    updated = pl.pallas_call(
        update_body,
        out_shape=out_shape,
        in_specs=[pl.BlockSpec(memory_space=pltpu.SMEM)] + [vmem] * (len(operands) - 1),
        out_specs=[vmem] * len(out_shape),
        scratch_shapes=scratches + semaphores,
        compiler_params=pltpu.CompilerParams(
            collective_id=1, has_side_effects=True, vmem_limit_bytes=60 << 20
        ),
        name="update",
    )(*operands)
    cuts = (0, 3 * head_dim, 4 * head_dim, 4 * head_dim + hidden, weight_width)
    if own_gather:
        layer_output, input_grad, moment_cat, new_cat, mod_summed = updated
    else:
        layer_output, input_grad, grad_cat, mod_summed = updated
        mod_summed = lax.psum(mod_summed, "nodes")
        moment_cat = MOMENTUM_DECAY * moment_cat + lax.psum_scatter(
            grad_cat.reshape(full_width, weight_width), "nodes", scatter_dimension=0, tiled=True
        )
        whole = lax.all_gather(moment_cat.astype(BF16), ("nodes", "heads"), axis=0, tiled=False)
        whole = whole.reshape(patch_count, head_count, shard_rows, weight_width)
        whole = whole.transpose(0, 2, 1, 3).reshape(full_width, head_count, weight_width).astype(F32)
        factors = (1.0, 1.0, 1.0, (head_count * hidden / full_width) ** 0.5)
        pieces = []
        for number in range(4):
            columns = cuts[number + 1] - cuts[number]
            matrix = whole[:, :, cuts[number] : cuts[number + 1]].reshape(full_width, head_count * columns)
            ortho = lax.dynamic_slice(
                orthogonal(matrix),
                (patch_index * shard_rows, head_index * columns),
                (shard_rows, columns),
            )
            pieces.append(factors[number] * ortho)
        new_cat = weight_cat * (1.0 - LR_MUON * DECAY_WEIGHT) - LR_MUON * jnp.concatenate(pieces, axis=1)

    def unpack(cat):
        project, output, expand, contract = (cat[:, cuts[i] : cuts[i + 1]] for i in range(4))
        return (project, output.T, expand, contract.T)

    mod_summed = mod_summed.reshape(micro_count, 4, share)
    grad_modulate = sum(
        noise_embed[b][None, :, None] * mod_summed[b][:, None, :] for b in range(micro_count)
    )
    grad_bias = jnp.sum(mod_summed, axis=0)
    first_mod, second_mod, new_mod = adam_step(
        w_modulate, first_modulate, second_modulate, grad_modulate
    )
    first_b, second_b, new_b = adam_step(b_modulate, first_bias, second_bias, grad_bias)
    return (
        layer_output,
        input_grad,
        *unpack(moment_cat),
        *unpack(new_cat),
        first_mod,
        second_mod,
        new_mod,
        first_b,
        second_b,
        new_b,
    )


def solution(mesh):
    in_specs = (
        P(None, "nodes", "heads"),
        P(),
        P(None, "nodes", "heads"),
        P(None, "nodes", None),
        P(None, "nodes"),
        P("nodes", "heads"),
        P("heads", "nodes"),
        P("nodes", "heads"),
        P("heads", "nodes"),
        P("nodes", "heads"),
        P("heads", "nodes"),
        P("nodes", "heads"),
        P("heads", "nodes"),
        P(None, None, "heads"),
        P(None, "heads"),
        P(None, None, "heads"),
        P(None, None, "heads"),
        P(None, "heads"),
        P(None, "heads"),
    )
    out_specs = (
        P(None, "nodes", "heads"),
        P(None, "nodes", "heads"),
        P("nodes", "heads"),
        P("heads", "nodes"),
        P("nodes", "heads"),
        P("heads", "nodes"),
        P("nodes", "heads"),
        P("heads", "nodes"),
        P("nodes", "heads"),
        P("heads", "nodes"),
        P(None, None, "heads"),
        P(None, None, "heads"),
        P(None, None, "heads"),
        P(None, "heads"),
        P(None, "heads"),
        P(None, "heads"),
    )
    return jax.shard_map(
        per_device, mesh=mesh, in_specs=in_specs, out_specs=out_specs, check_vma=False
    )
```

```python
import functools

import jax
import jax.numpy as jnp
from jax import lax
from jax.experimental import pallas as pl
from jax.experimental.pallas import tpu as pltpu
from jax.sharding import PartitionSpec as P

NS_STEPS = 5
STEP = 10


EPS_NORM = 1e-06
NEWTON_A = 3.4445
NEWTON_B = -4.775
NEWTON_C = 2.0315
MOMENTUM_DECAY = 0.5
LR_MUON = 1.0
LR_ADAM = 0.04
DECAY_WEIGHT = 0.01
BETA_FIRST = 0.9
BETA_SECOND = 0.999
EPS_ADAM = 1e-08
HIGH = lax.Precision.HIGHEST
MESH = pl.DeviceIdType.MESH
F32 = jnp.float32
BF16 = jnp.bfloat16
NN = (((1,), (0,)), ((), ()))
NT = (((1,), (1,)), ((), ()))
TN = (((0,), (0,)), ((), ()))


def mul(left, right, dims=NN):
    return lax.dot_general(left, right, dims, preferred_element_type=F32)


class Links:
    def __init__(self, send_sems, recv_sems):
        self.send_sems, self.recv_sems = send_sems, recv_sems
        self.copies, self.finished = [], []

    def send(self, source, target, device):
        slot = len(self.copies)
        copy = pltpu.make_async_remote_copy(
            src_ref=source,
            dst_ref=target,
            send_sem=self.send_sems.at[slot],
            recv_sem=self.recv_sems.at[slot],
            device_id=device,
            device_id_type=MESH,
        )
        copy.start()
        self.copies.append(copy)
        return copy

    def finish(self, copy):
        copy.wait_send()
        self.finished.append(copy)

    def close(self):
        for copy in self.copies:
            if not any(copy is other for other in self.finished):
                copy.wait_send()


def greet(devices):
    barrier = pltpu.get_barrier_semaphore()
    for device in devices:
        pl.semaphore_signal(barrier, inc=1, device_id=device, device_id_type=MESH)


def await_greetings(devices):
    pl.semaphore_wait(pltpu.get_barrier_semaphore(), len(devices))


def norm_rows(values):
    width = values.shape[-1]
    row_mean = jnp.sum(values, axis=-1, keepdims=True) / width
    square_mean = jnp.sum(values * values, axis=-1, keepdims=True) / width
    inv_root = lax.rsqrt(square_mean - row_mean * row_mean + EPS_NORM)
    return ((values - row_mean) * inv_root, inv_root)


def wide(ref, *index):
    return jnp.concatenate([ref[(head, *index)] for head in range(ref.shape[0])], axis=-1)


def mod_row(mod_ref, batch, number):
    return wide(mod_ref, slice(batch * 4 + number, batch * 4 + number + 1), slice(None))


def layer_kernel(
    patch_count,
    own_gather,
    sizes_ref,
    state_ref,
    cot_ref,
    index_ref,
    noise_ref,
    modulate_ref,
    bias_ref,
    weight_refs,
    moment_refs,
    layer_output,
    input_grad,
    moment_new,
    ortho_in,
    mod_sum,
    weight_low,
    weight_all,
    output_all,
    state_all,
    cot_all,
    mod_all,
    halo,
    a_one,
    queries,
    key_value,
    prob_low,
    mixed_all,
    hidden_one,
    a_two,
    act,
    grad_up,
    part_two,
    part_core,
    part_low,
    part_across,
    total_two,
    out_low,
    out_core,
    out_keep,
    out_across,
    grad_hidden,
    grad_attn,
    grad_mixed,
    score_low,
    grad_own,
    grad_away,
    grad_back,
    grad_projected,
    mod_part,
    mod_in,
    grad_cat,
    grad_low,
    grad_core,
    grad_line,
    grad_near,
    moment_low,
    matrix,
    gram,
    chain,
    ortho_out,
    send_sems,
    recv_sems,
    turn_send,
    turn_recv,
):
    node, head = lax.axis_index("nodes"), lax.axis_index("heads")
    after, before = lax.rem(node + 1, patch_count), lax.rem(node + patch_count - 1, patch_count)
    across, sibling = lax.rem(head + 2, 4), head + 1 - 2 * lax.rem(head, 2)
    to_across, to_sibling, to_diagonal = (node, across), (node, sibling), (node, 3 - head)
    to_after, to_before = (after, head), (before, head)
    side, core = lax.div(head, 2), lax.rem(head, 2)
    plane, parity = lax.div(node, 2), lax.rem(node, 2)
    mirror = 1 - parity
    partner = node + 1 - 2 * parity
    to_partner = (partner, head)
    micro_count, capacity, share = state_ref.shape
    head_dim = queries.shape[-1]
    full_width = a_one.shape[-1]
    hidden = act.shape[-1]
    total = 3 * capacity
    inv_head = head_dim ** (-0.5)
    cuts = (0, 3 * head_dim, 4 * head_dim, 4 * head_dim + hidden, 4 * head_dim + 2 * hidden)
    widths = (3 * head_dim, head_dim, hidden, hidden)
    expand_columns, contract_columns = slice(cuts[2], cuts[3]), slice(cuts[3], cuts[4])
    tile = capacity // 2
    batches = range(micro_count)
    peers = [(lax.rem(node + 2 * k, patch_count), head) for k in range(1, patch_count // 2)]
    met = [to_across, to_sibling, to_diagonal]
    if own_gather:
        met += [(lax.rem(node + k, patch_count), head) for k in range(1, patch_count)]
        met += [(partner, across)]
    else:
        met += [to_after, to_before]
    greet(met)
    for number in range(modulate_ref.shape[0]):
        terms = lax.dot_general(
            noise_ref[...], modulate_ref[number], NN, precision=HIGH, preferred_element_type=F32
        )
        terms = terms + bias_ref[number : number + 1, :]
        for b in batches:
            place = b * modulate_ref.shape[0] + number
            mod_all[head, place : place + 1, :] = terms[b : b + 1]
    if own_gather:
        for number, ref in enumerate(weight_refs):
            weight_low[:, cuts[number] : cuts[number + 1]] = ref[...].astype(BF16)
    await_greetings(met)
    links = Links(send_sems, recv_sems)

    def weight(columns):
        return weight_all[:, :, columns].reshape(full_width, columns.stop - columns.start)

    def live_rows(batch, start, count):
        slots = lax.broadcasted_iota(jnp.int32, (count, 1), 0) + start
        return (slots < sizes_ref[batch, 0]).astype(F32)

    def rows_at(step, count):
        start = step * count if isinstance(step, int) else pl.multiple_of(step * count, count)
        return start, pl.ds(start, count)

    first_columns = pl.ds(0, cuts[2])
    other_columns = pl.ds(cuts[2], cuts[4] - cuts[2])

    def spread(columns):
        part = weight_low.at[:, columns]
        into = weight_all.at[node, :, columns]
        return [links.send(part, into, to) for to in peers], (part, into)

    def pass_on(arriving, columns):
        passed = []
        for k, copy in enumerate(arriving):
            copy.wait_recv()
            owner = lax.rem(node + patch_count - 2 * (k + 1), patch_count)
            part = weight_all.at[owner, :, columns]
            passed.append(links.send(part, part, to_partner))
        return passed

    mod_copies = [
        links.send(mod_all.at[head], mod_all.at[head], to) for to in (to_across, to_sibling, to_diagonal)
    ]
    if own_gather:
        first_peers, first_partner = spread(first_columns)
        first_partner = [links.send(*first_partner, to_partner)]
    state_across, state_after, state_before, state_sibling = [], [], [], []
    for b in batches:
        state_across.append(links.send(state_ref.at[b], state_all.at[head, b], to_across))
        state_after.append(links.send(state_ref.at[b], halo.at[0, head, b], to_after))
        state_before.append(links.send(state_ref.at[b], halo.at[1, head, b], to_before))
        state_sibling.append(links.send(state_ref.at[b], state_all.at[head, b], to_sibling))
    if own_gather:
        other_peers, other_partner = spread(other_columns)
    cot_across = [links.send(cot_ref.at[0], cot_all.at[head, 0], to_across)]
    if own_gather:
        weight_all[node] = weight_low[...]
    state_all[head] = state_ref[...]
    cot_all[head] = cot_ref[...]

    group = index_ref.shape[-1] // 16
    blocks = total // share

    def count_group(batch, place):
        ids = index_ref[batch, pl.ds(place, 1), :]
        lanes = lax.broadcasted_iota(jnp.int32, ids.shape, 1)
        code = (ids >> 7) + 16 * (lanes >> 4)
        rows = lax.broadcasted_iota(jnp.int32, (blocks * group, ids.shape[1]), 0)
        pick = jnp.where(code == (rows // group) + 16 * (rows % group), 1.0, 0.0).astype(BF16)
        slots = lax.broadcasted_iota(jnp.int32, (share, ids.shape[1]), 0)
        spot = jnp.where((ids & 127) == slots, 1.0, 0.0).astype(BF16)
        found = mul(pick, spot, NT).astype(BF16)
        into = pl.ds(pl.multiple_of(place * group, group), group)
        for block in range(blocks):
            prob_low[batch, into, block * share : (block + 1) * share] = found[
                block * group : (block + 1) * group
            ]

    def count(batch):
        pl.loop(0, capacity // group, unroll=4)(lambda place: count_group(batch, place))

    pass_state, halo_across, halo_sibling = [], [], []

    def second_hops(b):
        state_across[b].wait_recv()
        part = state_all.at[across, b]
        pass_state.append(links.send(part, part, to_sibling))
        to_chip, to_core = [], []
        for k, copy in ((0, state_after[b]), (1, state_before[b])):
            copy.wait_recv()
            part = halo.at[k, head, b]
            to_chip.append(links.send(part, part, to_across))
            to_core.append(links.send(part, part, to_sibling))
        halo_across.append(to_chip)
        halo_sibling.append(to_core)

    count(0)
    second_hops(0)
    if own_gather:
        first_passed = pass_on(first_peers, first_columns)
    count(1)
    second_hops(1)
    if own_gather:
        other_partner = [links.send(*other_partner, to_partner)]
    cot_across += [links.send(cot_ref.at[b], cot_all.at[head, b], to_across) for b in batches[1:]]
    cot_sibling = links.send(cot_ref, cot_all.at[head], to_sibling)

    def project(source, patch, batch):
        shift, scale = mod_row(mod_all, batch, 0), 1.0 + mod_row(mod_all, batch, 1)

        @pl.loop(0, capacity // tile)
        def _(step):
            _, rows = rows_at(step, tile)
            normed, _ = norm_rows(wide(source, batch, rows, slice(None)).astype(F32))
            a_rows = (normed * scale + shift).astype(BF16)
            a_one[patch * micro_count + batch, rows, :] = a_rows
            first = 0 if patch == 1 else head_dim
            out = mul(a_rows, weight(slice(first, cuts[1]))).astype(BF16)
            if patch == 1:
                queries[batch, rows, :] = out[:, :head_dim]
            key_value[batch, patch, rows, :] = out[:, out.shape[1] - 2 * head_dim :]

    def project_all(b):
        state_sibling[b].wait_recv()
        pass_state[b].wait_recv()
        project(state_all, 1, b)
        for k in range(2):
            halo_across[b][k].wait_recv()
            part = halo.at[k, across, b]
            halo_sibling[b].append(links.send(part, part, to_sibling))
        for copy in halo_sibling[b]:
            copy.wait_recv()
        project(halo.at[0], 0, b)
        project(halo.at[1], 2, b)

    def attend(batch):
        attend_rows = 128

        @pl.loop(0, capacity // attend_rows)
        def _(step):
            _, rows = rows_at(step, attend_rows)
            keys = key_value[batch, :, :, :head_dim].reshape(total, head_dim)
            values = key_value[batch, :, :, head_dim:].reshape(total, head_dim)
            scores = mul(queries[batch, rows, :], keys, NT) * inv_head
            times = prob_low[batch, rows, :].astype(F32)
            scores = jnp.where(times > 0.0, scores, -1e30)
            exps = jnp.exp(scores - jnp.max(scores, axis=-1, keepdims=True)) * times
            prob = (exps * (1.0 / jnp.sum(exps, axis=-1, keepdims=True))).astype(BF16)
            prob_low[batch, rows, :] = prob
            mixed_all[head, batch, rows, :] = mul(prob, values).astype(BF16)

        part = mixed_all.at[head, batch]
        return links.send(part, part, to_across), links.send(part, part, to_sibling)

    def pass_mixed(batch, copies):
        copies[0].wait_recv()
        part = mixed_all.at[across, batch]
        return [copies[1], links.send(part, part, to_sibling)]

    def wait_all(copies):
        for copy in copies:
            copy.wait_recv()

    wait_all(mod_copies)
    ready = [cot_sibling]
    if own_gather:
        wait_all(first_partner + first_passed)
        output_all[head] = weight_all[:, :, cuts[1] : cuts[2]]
        output_part = weight_all.at[:, :, pl.ds(cuts[1], head_dim)]
        output_across = links.send(output_part, output_all.at[head], to_across)
        ready.append(links.send(output_part, output_all.at[head], to_sibling))
    project_all(0)
    mixed_first = attend(0)
    if own_gather:
        other_passed = pass_on(other_peers, other_columns)
    project_all(1)
    mixed_first = pass_mixed(0, mixed_first)
    wait_all(cot_across)
    ready.append(links.send(cot_all.at[across], cot_all.at[across], to_sibling))
    if own_gather:
        output_across.wait_recv()
        ready.append(links.send(output_all.at[across], output_all.at[across], to_sibling))
    mixed_second = attend(1)
    if own_gather:
        ready += other_partner + other_passed
    wait_all(ready + mixed_first)

    def feed_forward(batch, step):
        start, rows = rows_at(step, tile)
        mixed = wide(mixed_all, batch, rows, slice(None))
        mixer = jnp.concatenate(
            [output_all[k].reshape(full_width, head_dim) for k in range(output_all.shape[0])], axis=-1
        )
        hid = wide(state_all, batch, rows, slice(None)).astype(F32) + mul(mixed, mixer, NT)
        hidden_one[batch, rows, :] = hid
        normed, _ = norm_rows(hid)
        a_rows = (normed * (1.0 + mod_row(mod_all, batch, 3)) + mod_row(mod_all, batch, 2)).astype(BF16)
        a_two[batch, rows, :] = a_rows
        up = mul(a_rows, weight(expand_columns))
        gate = jax.nn.sigmoid(up)
        acted = (up * gate).astype(BF16)
        act[batch, rows, :] = acted
        live = live_rows(batch, start, tile)
        cot = (wide(cot_all, batch, rows, slice(None)).astype(F32) * live).astype(BF16)
        grad_act = mul(cot, weight(contract_columns))
        grad_rows = (grad_act * gate * (1.0 + up * (1.0 - gate))).astype(BF16)
        grad_up[batch, rows, :] = grad_rows
        back = mul(grad_rows, weight(expand_columns), NT)
        out = mul(acted, weight(contract_columns), NT)
        for k in range(4):
            block = slice(k * head_dim, (k + 1) * head_dim)
            part_two[batch, k % 2, k // 2, rows, :] = back[:, block]
            out_low[batch, k % 2, k // 2, rows, :] = out[:, block].astype(BF16)

    def to_core(batch):
        return links.send(part_two.at[batch, 1 - core], part_core.at[batch], to_sibling)

    def to_side(batch, copy):
        copy.wait_recv()
        for k in range(2):
            chip = part_two[batch, core, k] + part_core[batch, k]
            part_core[batch, k] = chip
            part_low[batch, k] = chip.astype(BF16)
        return links.send(part_low.at[batch], part_across.at[batch], to_across)

    def to_all(batch, copy):
        copy.wait_recv()
        for k in range(2):
            total_two[batch, core, k] = part_core[batch, k] + part_across[batch, k].astype(F32)
        return links.send(total_two.at[batch, core], total_two.at[batch, core], to_sibling)

    def total_rows(batch, rows):
        return jnp.concatenate(
            [total_two[batch, k % 2, k // 2, rows, :] for k in range(4)], axis=-1
        )

    def back_norm(grad, normed, root):
        mean_grad = jnp.sum(grad, axis=-1, keepdims=True) / full_width
        mean_cross = jnp.sum(grad * normed, axis=-1, keepdims=True) / full_width
        return root * (grad - mean_grad - normed * mean_cross)

    def add_mod(batch, number, values):
        sums = jnp.sum(values, axis=0, keepdims=True)
        place = batch * 4 + number
        for k in range(4):
            mod_part[k, place : place + 1, :] += sums[:, k * head_dim : (k + 1) * head_dim]

    def own_block(values):
        own = jnp.zeros((values.shape[0], head_dim), F32)
        for k in range(4):
            own = own + jnp.where(head == k, values[:, k * head_dim : (k + 1) * head_dim], 0.0)
        return own

    for k in range(4):
        mod_part[k] = jnp.zeros(mod_part.shape[1:], F32)

    pl.loop(0, 2)(lambda step: feed_forward(0, step))
    core_first = to_core(0)
    mixed_second = pass_mixed(1, mixed_second)
    side_first = to_side(0, core_first)
    wait_all(mixed_second)
    pl.loop(0, 2)(lambda step: feed_forward(1, step))
    core_second = to_core(1)

    def store_grad(step, columns, value):
        half = full_width // 8
        for k in range(2):
            part = value[k * half : (k + 1) * half]
            grad_cat[k, step, :, columns] = part
            grad_low[k, step, :, columns] = part.astype(BF16)

    def both(ref, columns):
        return ref[:, :, columns].reshape(micro_count * capacity, -1)

    def one_pair(patch, columns):
        pair = a_one[patch * micro_count : (patch + 1) * micro_count, :, columns]
        return pair.reshape(micro_count * capacity, -1)

    def live_cot(batch, columns):
        return (cot_all[columns, batch].astype(F32) * live_rows(batch, 0, capacity)).astype(BF16)

    late = slice(0, cuts[2])

    def grad_pair(columns):
        return links.send(
            grad_low.at[1 - parity, :, :, columns], grad_core.at[:, :, columns], to_partner
        )

    def grad_planes(copy, columns):
        copy.wait_recv()
        for k in range(4):
            summed = grad_cat[parity, k, :, columns] + grad_core[k, :, columns].astype(F32)
            grad_cat[parity, k, :, columns] = summed
            grad_low[parity, k, :, columns] = summed.astype(BF16)
        sent = []
        for k in range(1, 4):
            target = lax.rem(plane + k, 4)
            sent.append(
                links.send(
                    grad_low.at[parity, target, :, columns],
                    grad_line.at[k - 1, :, columns],
                    (2 * target + parity, head),
                )
            )
        return sent

    def grad_finish(copies, columns):
        wait_all(copies)
        summed = grad_cat[parity, plane, :, columns]
        for k in range(3):
            summed = summed + grad_line[k, :, columns].astype(F32)
        store_moment(summed, columns)

    def grad_direct(columns):
        sent = []
        for k in range(1, patch_count):
            target = lax.rem(node + k, patch_count)
            sent.append(
                links.send(
                    grad_low.at[lax.rem(target, 2), lax.div(target, 2), :, columns],
                    grad_near.at[k - 1],
                    (target, head),
                )
            )
        return sent

    def grad_direct_finish(copies, columns):
        summed = grad_cat[parity, plane, :, columns]
        for k, copy in enumerate(copies):
            copy.wait_recv()
            summed = summed + grad_near[k].astype(F32)
        store_moment(summed, columns)

    def store_moment(summed, columns):
        for number, ref in enumerate(moment_refs):
            if columns.start <= cuts[number] < columns.stop:
                own = slice(cuts[number], cuts[number + 1])
                part = summed[:, cuts[number] - columns.start : cuts[number + 1] - columns.start]
                moment = MOMENTUM_DECAY * ref[...] + part
                moment_new[:, own] = moment
                moment_low[:, own] = moment.astype(BF16)

    @pl.loop(0, 4)
    def _(step):
        columns = pl.ds(pl.multiple_of(step * head_dim, head_dim), head_dim)
        store_grad(step, expand_columns, mul(both(a_two, columns), grad_up[...].reshape(-1, hidden), TN))

    if own_gather:
        expand_pair = grad_pair(expand_columns)

    @pl.loop(0, 4)
    def _(step):
        cot = jnp.concatenate([live_cot(b, step) for b in batches], axis=0)
        store_grad(step, contract_columns, mul(cot, act[...].reshape(-1, hidden), TN))

    if own_gather:
        contract_pair = grad_pair(contract_columns)
    side_second = to_side(1, core_second)
    all_first = to_all(0, side_first)
    out_copies = [links.send(out_low.at[b, 1 - core], out_core.at[b], to_sibling) for b in batches]

    def norm_two_back(batch):
        @pl.loop(0, capacity // tile)
        def _(step):
            start, rows = rows_at(step, tile)
            normed, root = norm_rows(hidden_one[batch, rows, :])
            grad = total_rows(batch, rows)
            add_mod(batch, 2, grad)
            add_mod(batch, 3, grad * normed)
            cot = wide(cot_all, batch, rows, slice(None)).astype(F32) * live_rows(batch, start, tile)
            grad = cot + back_norm(grad * (1.0 + mod_row(mod_all, batch, 3)), normed, root)
            grad_hidden[batch, rows, :] = own_block(grad)
            low = grad.astype(BF16)
            grad_attn[batch, rows, :] = low
            grad_mixed[batch, rows, :] = mul(low, weight(slice(cuts[1], cuts[2]))).astype(BF16)

    def attend_back(batch):
        attend_rows = 128

        @pl.loop(0, capacity // attend_rows)
        def _(step):
            _, rows = rows_at(step, attend_rows)
            keys = key_value[batch, :, :, :head_dim].reshape(total, head_dim)
            values = key_value[batch, :, :, head_dim:].reshape(total, head_dim)
            prob = prob_low[batch, rows, :].astype(F32)
            grad_prob = mul(grad_mixed[batch, rows, :], values, NT)
            mean = jnp.sum(prob * grad_prob, axis=-1, keepdims=True)
            score = (prob * (grad_prob - mean) * inv_head).astype(BF16)
            score_low[rows, :] = score
            grad_projected[batch, rows, :head_dim] = mul(score, keys).astype(BF16)

        for patch in range(3):
            slots = slice(patch * capacity, (patch + 1) * capacity)
            grad_key = mul(score_low[:, slots], queries[batch], TN)
            grad_value = mul(prob_low[batch, :, slots], grad_mixed[batch], TN)
            if patch == 1:
                grad_own[batch, :, :head_dim] = grad_key
                grad_own[batch, :, head_dim:] = grad_value
            else:
                grad_away[batch, patch // 2, :, :head_dim] = grad_key.astype(BF16)
                grad_away[batch, patch // 2, :, head_dim:] = grad_value.astype(BF16)

    def send_back(batch):
        return [
            links.send(grad_away.at[batch, 0], grad_back.at[batch, 1], to_before),
            links.send(grad_away.at[batch, 1], grad_back.at[batch, 0], to_after),
        ]

    owners = (1, 2, 0, 3)

    def turn(source, target, device, send_slot, recv_slot):
        return pltpu.make_async_remote_copy(
            src_ref=source,
            dst_ref=target,
            send_sem=turn_send.at[send_slot],
            recv_sem=turn_recv.at[recv_slot],
            device_id=device,
            device_id_type=MESH,
        )

    def to_owner(number, sender):
        return turn(
            moment_low.at[:, slice(cuts[number], cuts[number + 1])],
            matrix.at[head, parity, sender, :, : widths[number]],
            (2 * owners[number] + parity, head),
            number,
            sender,
        )

    def give(width, number):
        block, pair, device = (
            (head, parity, to_across),
            (head, parity, to_partner),
            (head, parity, (partner, across)),
            (head, parity, to_sibling),
            (across, parity, to_sibling),
            (head, mirror, to_sibling),
            (across, mirror, to_sibling),
        )[number]
        part = matrix.at[block, pair, :, :, :width]
        return turn(part, part, device, 4 + number, 4 + number)

    def own_to_owner(numbers):
        for number in numbers:

            @pl.when(plane != owners[number])
            def _():
                to_owner(number, plane).start()

            @pl.when(plane == owners[number])
            def _():
                matrix[head, parity, plane, :, : widths[number]] = moment_low[
                    :, cuts[number] : cuts[number + 1]
                ]

    def own_arrive(numbers):
        for number in numbers:

            @pl.when(plane == owners[number])
            def _():
                for other in range(4):
                    if other != owners[number]:
                        to_owner(number, other).wait_recv()
                for k in range(4):
                    give(widths[number], k).start()

            @pl.when(plane != owners[number])
            def _():
                to_owner(number, plane).wait_send()

    all_first.wait_recv()
    if own_gather:
        expand_line = grad_planes(expand_pair, expand_columns)
    norm_two_back(0)
    attend_back(0)
    back_first = send_back(0)
    all_second = to_all(1, side_second)
    if own_gather:
        contract_line = grad_planes(contract_pair, contract_columns)
    out_across_copies = []
    for batch in batches:
        out_copies[batch].wait_recv()
        for k in range(2):
            chip = out_low[batch, core, k].astype(F32) + out_core[batch, k].astype(F32)
            out_keep[batch, k] = chip
            out_core[batch, k] = chip.astype(BF16)
        out_across_copies.append(
            links.send(out_core.at[batch, 1 - side], out_across.at[batch], to_across)
        )
    all_second.wait_recv()
    norm_two_back(1)
    attend_back(1)

    @pl.loop(0, 4)
    def _(step):
        columns = pl.ds(pl.multiple_of(step * head_dim, head_dim), head_dim)
        queries_part = mul(one_pair(1, columns), both(grad_projected, slice(0, head_dim)), TN)
        store_grad(step, slice(0, head_dim), queries_part)
        rest = mul(one_pair(1, columns), grad_own[...].reshape(-1, 2 * head_dim).astype(BF16), TN)
        for patch in (0, 2):
            away = grad_away[:, patch // 2].reshape(-1, 2 * head_dim)
            rest = rest + mul(one_pair(patch, columns), away, TN)
        store_grad(step, slice(head_dim, cuts[1]), rest)
        own_mixed = mixed_all[head].reshape(-1, head_dim)
        store_grad(step, slice(cuts[1], cuts[2]), mul(both(grad_attn, columns), own_mixed, TN))

    if own_gather:
        late_direct = grad_direct(late)
    back_second = send_back(1)
    if own_gather:
        grad_finish(expand_line, expand_columns)
        grad_finish(contract_line, contract_columns)
        own_to_owner((2, 3))
    for batch in batches:
        out_across_copies[batch].wait_recv()
        own = hidden_one[batch, :, pl.ds(pl.multiple_of(head * head_dim, head_dim), head_dim)]
        result = own + out_keep[batch, side] + out_across[batch].astype(F32)
        layer_output[batch] = (result * live_rows(batch, 0, capacity)).astype(BF16)

    for copy in (core_first, core_second, side_first, side_second, all_first, all_second):
        links.finish(copy)

    def rows_back(batch, copies):
        wait_all(copies)
        whole = grad_own[batch] + grad_back[batch, 0].astype(F32) + grad_back[batch, 1].astype(F32)
        grad_projected[batch, :, head_dim:] = whole.astype(BF16)

        @pl.loop(0, capacity // tile)
        def _(step):
            _, rows = rows_at(step, tile)
            back = mul(grad_projected[batch, rows, :], weight(slice(0, cuts[1])), NT)
            for k in range(4):
                part_two[batch, k % 2, k // 2, rows, :] = back[:, k * head_dim : (k + 1) * head_dim]

        return to_core(batch)

    def rows_end(batch, copy):
        copy.wait_recv()

        @pl.loop(0, capacity // tile)
        def _(step):
            _, rows = rows_at(step, tile)
            normed, root = norm_rows(wide(state_all, batch, rows, slice(None)).astype(F32))
            grad = total_rows(batch, rows)
            add_mod(batch, 0, grad)
            add_mod(batch, 1, grad * normed)
            grad = back_norm(grad * (1.0 + mod_row(mod_all, batch, 1)), normed, root)
            input_grad[batch, rows, :] = own_block(grad) + grad_hidden[batch, rows, :]

    one_core = [rows_back(0, back_first)]

    if not own_gather:
        one_core.append(rows_back(1, back_second))
        one_side = [to_side(b, one_core[b]) for b in batches]
        one_all = [to_all(b, one_side[b]) for b in batches]
        for b in batches:
            rows_end(b, one_all[b])
        mod_sum[...] = mod_part[head]
        for k in range(8):
            moment_new[k] = grad_cat[k % 2, k // 2]
        links.close()
        return

    grad_direct_finish(late_direct, late)
    own_to_owner((0, 1))
    own_arrive((2, 3))
    one_core.append(rows_back(1, back_second))
    own_arrive((0, 1))
    one_side = [to_side(b, one_core[b]) for b in batches]
    half = full_width // 2

    def gather_plane(width):
        for k in range(3):
            give(width, k).wait_recv()
            give(width, 4 + k).start()
        for k in range(3, 7):
            give(width, k).wait_recv()
        for k in range(7):
            give(width, k).wait_send()

        @pl.loop(0, 2)
        def _(step):
            _, rows = rows_at(step, half)
            summed = jnp.zeros((half, full_width), F32)
            for k in range(4):
                left = matrix[k, step, :, :, :width].reshape(half, width)
                right = matrix[k, :, :, :, :width].reshape(full_width, width)
                summed = summed + mul(left, right, NT)
            gram[rows, :] = summed

    for first, second, width in ((1, 1, widths[0]), (2, 2, widths[1]), (0, 3, hidden)):

        @pl.when((plane == first) | (plane == second))
        def _():
            gather_plane(width)

    gram_pair, factor_pair, turn_pair = (a_one.at[pl.ds(k, 2)] for k in (0, 2, 4))

    def put_pair(ref, value, rows=slice(None)):
        high = value.astype(BF16)
        ref[0, rows, :] = high
        ref[1, rows, :] = (value - high.astype(F32)).astype(BF16)

    def times(left, right, rows=slice(None)):
        left_high, left_low = left[0, rows, :], left[1, rows, :]
        right_high, right_low = right[0], right[1]
        return mul(
            jnp.concatenate([left_high, left_high, left_low], axis=1),
            jnp.concatenate([right_high, right_low, right_high], axis=0),
        )

    def diagonal(count, start=0):
        rows = lax.broadcasted_iota(jnp.int32, (count, full_width), 0) + start
        return rows == lax.broadcasted_iota(jnp.int32, (count, full_width), 1)

    trace = jnp.zeros((1, 1), F32)
    for step in range(2):
        kept = jnp.where(diagonal(half, step * half), gram[step * half : (step + 1) * half, :], 0.0)
        trace = trace + jnp.sum(jnp.sum(kept, axis=1, keepdims=True), axis=0, keepdims=True)
    scale = 1.0 / (jnp.sqrt(trace) + 1e-07)
    gram[...] = gram[...] * (scale * scale)
    put_pair(gram_pair, gram[...])
    own = pl.ds(pl.multiple_of(parity * half, half), half)

    one_all = []
    for repeat in range(NS_STEPS - 1):
        factor = NEWTON_B * gram[...] + NEWTON_C * times(gram_pair, gram_pair)
        factor = factor + jnp.where(diagonal(full_width), NEWTON_A, 0.0)
        put_pair(factor_pair, factor)
        if repeat == 0:
            put_pair(chain.at[0], factor)
        else:
            put_pair(chain.at[repeat % 2], times(factor_pair, chain.at[(repeat + 1) % 2]))
        put_pair(turn_pair, times(factor_pair, gram_pair))
        gram[...] = times(factor_pair, turn_pair)
        put_pair(gram_pair, gram[...])
        if repeat in (1, 2):
            one_all.append(to_all(repeat - 1, one_side[repeat - 1]))
    factor = NEWTON_B * gram[own, :] + NEWTON_C * times(gram_pair, gram_pair, own)
    factor = factor + jnp.where(diagonal(half, parity * half), NEWTON_A, 0.0)
    put_pair(factor_pair, factor, own)
    final = times(factor_pair, chain.at[(NS_STEPS - 2) % 2], own)

    put_pair(chain.at[0], final, slice(0, half))

    def ortho_copy(number, k):
        target = (owners[number] + k) % 4
        width = widths[number]
        return turn(
            ortho_out.at[target, :, :width],
            ortho_in.at[number, :, :width],
            (2 * target + parity, head),
            11 + k,
            11 + number,
        )

    for number in range(4):

        @pl.when(plane == owners[number])
        def _():
            width = widths[number]
            left = jnp.concatenate([chain[0, k, :half, :] for k in range(2)], axis=-1)
            right = matrix[head, :, :, :, :width].reshape(full_width, width)
            value = mul(left, jnp.concatenate([right, right], axis=0)) * scale
            ortho_out[:, :, :width] = value.astype(BF16).reshape(4, half // 4, width)
            for k in range(1, 4):
                ortho_copy(number, k).start()
            ortho_in[number, :, :width] = ortho_out[plane, :, :width]

    for b in batches:
        rows_end(b, one_all[b])
    mod_copies = [
        links.send(mod_part.at[head], mod_in.at[k - 1], (lax.rem(node + k, patch_count), head))
        for k in range(1, patch_count)
    ]
    for number in range(4):

        @pl.when(plane != owners[number])
        def _():
            ortho_copy(number, 1).wait_recv()

        @pl.when(plane == owners[number])
        def _():
            for k in range(1, 4):
                ortho_copy(number, k).wait_send()

    summed = mod_part[head]
    wait_all(mod_copies)
    for k in range(patch_count - 1):
        summed = summed + mod_in[k]
    mod_sum[...] = summed
    links.close()


def finish_kernel(
    cuts,
    factors,
    layer_ref,
    input_ref,
    moment_ref,
    ortho_ref,
    mod_ref,
    noise_ref,
    weight_refs,
    adam_refs,
    layer_out,
    input_out,
    moment_outs,
    weight_outs,
    adam_outs,
    sems,
):
    copies = [
        pltpu.make_async_copy(source, target, sems.at[k])
        for k, (source, target) in enumerate(((layer_ref, layer_out), (input_ref, input_out)))
    ]
    for copy in copies:
        copy.start()
    for number in range(4):
        columns = slice(cuts[number], cuts[number + 1])
        moment_outs[number][...] = moment_ref[:, columns]
        ortho = ortho_ref[number, :, : cuts[number + 1] - cuts[number]].astype(F32)
        weight_outs[number][...] = (
            weight_refs[number][...] * (1.0 - LR_MUON * DECAY_WEIGHT) - (LR_MUON * factors[number]) * ortho
        )
    weight, first, second, bias, first_bias, second_bias = adam_refs
    micro_count = noise_ref.shape[0]
    for number in range(4):
        rows = [mod_ref[b * 4 + number : b * 4 + number + 1, :] for b in range(micro_count)]
        grad = lax.dot_general(
            noise_ref[...], jnp.concatenate(rows, axis=0), TN, precision=HIGH, preferred_element_type=F32
        )
        place = slice(number, number + 1)
        stepped = adam_step(weight[number], first[number], second[number], grad)
        for ref, value in zip(adam_outs[:3], stepped):
            ref[number] = value
        stepped = adam_step(bias[place, :], first_bias[place, :], second_bias[place, :], sum(rows))
        for ref, value in zip(adam_outs[3:], stepped):
            ref[place, :] = value
    for copy in copies:
        copy.wait()


def adam_step(weight, first_old, second_old, gradient):
    first_new = BETA_FIRST * first_old + (1.0 - BETA_FIRST) * gradient
    second_new = BETA_SECOND * second_old + (1.0 - BETA_SECOND) * gradient * gradient
    first_hat = first_new / (1.0 - BETA_FIRST**STEP)
    second_hat = second_new / (1.0 - BETA_SECOND**STEP)
    updated = weight * (1.0 - LR_ADAM * DECAY_WEIGHT) - LR_ADAM * first_hat / (
        jnp.sqrt(second_hat) + EPS_ADAM
    )
    return (first_new, second_new, updated)


def orthogonal(matrix):
    scale = 1.0 / (jnp.sqrt(jnp.sum(matrix * matrix)) + 1e-07)
    gram = jnp.dot(matrix, matrix.T, precision=HIGH) * (scale * scale)
    eye = jnp.eye(gram.shape[0], dtype=F32)
    chain = None
    for repeat in range(NS_STEPS):
        factor = NEWTON_A * eye + NEWTON_B * gram + NEWTON_C * jnp.dot(gram, gram, precision=HIGH)
        chain = factor if chain is None else jnp.dot(factor, chain, precision=HIGH)
        if repeat < NS_STEPS - 1:
            gram = jnp.dot(factor, jnp.dot(factor, gram, precision=HIGH), precision=HIGH)
    return jnp.dot(chain, matrix, precision=HIGH) * scale


def per_device(
    node_state,
    noise_embed,
    out_grad,
    neighbours,
    patch_sizes,
    w_project,
    w_output,
    w_expand,
    w_contract,
    momentum_project,
    momentum_output,
    momentum_expand,
    momentum_contract,
    w_modulate,
    b_modulate,
    first_modulate,
    second_modulate,
    first_bias,
    second_bias,
):
    micro_count, capacity, share = node_state.shape
    head_count = lax.axis_size("heads")
    patch_count = lax.axis_size("nodes")
    full_width = share * head_count
    head_dim = w_output.shape[0]
    total_rows = capacity * patch_count
    patch_index = lax.axis_index("nodes")
    head_index = lax.axis_index("heads")
    inv_head = head_dim ** (-0.5)
    hidden = w_expand.shape[1]
    shard_rows = w_project.shape[0]
    own_gather = patch_count == 8

    local_index = jnp.mod(neighbours - (patch_index - 1) * capacity, total_rows)
    index_rows = local_index.reshape(micro_count, capacity // 16, 256)
    weights = [w_project, w_output.T, w_expand, w_contract.T]
    moments = [momentum_project, momentum_output.T, momentum_expand, momentum_contract.T]
    cuts = (0, 3 * head_dim, 4 * head_dim, 4 * head_dim + hidden, 4 * head_dim + 2 * hidden)
    factors = (1.0, 1.0, 1.0, (head_count * hidden / full_width) ** 0.5)
    weight_width = cuts[4]
    vmem = pl.BlockSpec(memory_space=pltpu.VMEM)
    def scratch(dtype, *shape):
        return pltpu.VMEM(shape, dtype)

    rows_all = (head_count, micro_count, capacity, share)
    blocks = (micro_count, 2, 2, capacity, head_dim)
    half_blocks = (micro_count, 2, capacity, head_dim)
    rows_wide = (micro_count, capacity, full_width)
    rows_hidden = (micro_count, capacity, hidden)
    rows_own = (micro_count, capacity, head_dim)
    key_value_rows = (capacity, 2 * head_dim)
    eighth = full_width // 8
    scratches = [
        scratch(BF16, eighth, weight_width),
        scratch(BF16, 8, eighth, weight_width),
        scratch(BF16, head_count, 8, eighth, head_dim),
    ]
    scratches = scratches if own_gather else []
    scratches += [
        scratch(BF16, *rows_all),
        scratch(BF16, *rows_all),
        scratch(F32, head_count, 4 * micro_count, share),
        scratch(BF16, 2, *rows_all),
        scratch(BF16, 3 * micro_count, capacity, full_width),
        scratch(BF16, *rows_own),
        scratch(BF16, micro_count, 3, *key_value_rows),
        scratch(BF16, micro_count, capacity, 3 * capacity),
        scratch(BF16, *rows_all),
        scratch(F32, *rows_wide),
        scratch(BF16, *rows_wide),
        scratch(BF16, *rows_hidden),
        scratch(BF16, *rows_hidden),
        scratch(F32, *blocks),
        scratch(F32, *half_blocks),
        scratch(BF16, *half_blocks),
        scratch(BF16, *half_blocks),
        scratch(F32, *blocks),
        scratch(BF16, *blocks),
        scratch(BF16, *half_blocks),
        scratch(F32, *half_blocks),
        scratch(BF16, *rows_own),
        scratch(F32, *rows_own),
        scratch(BF16, *rows_wide),
        scratch(BF16, *rows_own),
        scratch(BF16, capacity, 3 * capacity),
        scratch(F32, micro_count, *key_value_rows),
        scratch(BF16, micro_count, 2, *key_value_rows),
        scratch(BF16, micro_count, 2, *key_value_rows),
        scratch(BF16, micro_count, capacity, 3 * head_dim),
        scratch(F32, head_count, 4 * micro_count, share),
        scratch(F32, 8, 4 * micro_count, share),
        scratch(F32, 2, 4, eighth, weight_width),
        scratch(BF16, 2, 4, eighth, weight_width),
        scratch(BF16, 4, eighth, weight_width),
        scratch(BF16, 3, eighth, weight_width),
        scratch(BF16, 7, eighth, 4 * head_dim),
    ]
    last = [
        scratch(BF16, eighth, weight_width),
        scratch(BF16, head_count, 2, 4, eighth, hidden),
        scratch(F32, full_width, full_width),
        scratch(BF16, 2, 2, full_width, full_width),
        scratch(BF16, 4, eighth, hidden),
    ]
    semaphores = [pltpu.SemaphoreType.DMA((count,)) for count in (96, 96, 16, 16)]
    operands = [patch_sizes, node_state, out_grad, index_rows, noise_embed, w_modulate, b_modulate]
    out_shape = [
        jax.ShapeDtypeStruct((micro_count, capacity, share), BF16),
        jax.ShapeDtypeStruct((micro_count, capacity, share), F32),
    ]
    summed_shape = jax.ShapeDtypeStruct((4 * micro_count, share), F32)
    if own_gather:
        operands += weights + moments
        out_shape += [
            jax.ShapeDtypeStruct((eighth, weight_width), F32),
            jax.ShapeDtypeStruct((4, eighth, hidden), BF16),
            summed_shape,
        ]
        scratches += last
    else:
        low_cat = jnp.concatenate(weights, axis=1).astype(BF16)
        low_cat = lax.all_gather(low_cat, "nodes", axis=0, tiled=True)
        low_cat = low_cat.reshape(8, eighth, weight_width)
        output_all = lax.all_gather(
            low_cat[:, :, 3 * head_dim : 4 * head_dim], "heads", axis=0, tiled=False
        )
        operands += [low_cat, output_all]
        out_shape += [jax.ShapeDtypeStruct((8, eighth, weight_width), F32), summed_shape]

    def layer_body(*refs):
        refs = list(refs)
        if own_gather:
            refs[7:15] = [refs[7:11], refs[11:15]]
        else:
            gathered = refs[7:9]
            refs[7:9] = [None, None]
            refs[12:12] = [None]
            refs[14:14] = [None] + gathered
            refs[-4:-4] = [None] * len(last)
        layer_kernel(patch_count, own_gather, *refs)

    updated = pl.pallas_call(
        layer_body,
        out_shape=out_shape,
        in_specs=[pl.BlockSpec(memory_space=pltpu.SMEM)] + [vmem] * (len(operands) - 1),
        out_specs=[vmem] * len(out_shape),
        scratch_shapes=scratches + semaphores,
        compiler_params=pltpu.CompilerParams(
            collective_id=0, has_side_effects=True, vmem_limit_bytes=60 << 20
        ),
        name="layer",
    )(*operands)
    if own_gather:
        layer_output, input_grad, moment_cat, ortho_all, mod_summed = updated
    else:
        layer_output, input_grad, grad_cat, mod_summed = updated
        mod_summed = lax.psum(mod_summed, "nodes")
        moment_cat = MOMENTUM_DECAY * jnp.concatenate(moments, axis=1) + lax.psum_scatter(
            grad_cat.reshape(full_width, weight_width), "nodes", scatter_dimension=0, tiled=True
        )
        whole = lax.all_gather(moment_cat.astype(BF16), ("nodes", "heads"), axis=0, tiled=False)
        whole = whole.reshape(patch_count, head_count, shard_rows, weight_width)
        whole = whole.transpose(0, 2, 1, 3).reshape(full_width, head_count, weight_width).astype(F32)
        pieces = []
        for number in range(4):
            columns = cuts[number + 1] - cuts[number]
            matrix = whole[:, :, cuts[number] : cuts[number + 1]].reshape(full_width, head_count * columns)
            ortho = lax.dynamic_slice(
                orthogonal(matrix),
                (patch_index * shard_rows, head_index * columns),
                (shard_rows, columns),
            )
            pieces.append(jnp.pad(ortho, ((0, 0), (0, hidden - columns))))
        ortho_all = jnp.stack(pieces)
    adam = [w_modulate, first_modulate, second_modulate, b_modulate, first_bias, second_bias]
    anywhere = pl.BlockSpec(memory_space=pl.ANY)

    def finish_body(*refs):
        finish_kernel(
            cuts, factors, *refs[:6], refs[6:10], refs[10:16], *refs[16:18], refs[18:22], refs[22:26], refs[26:32], refs[32]
        )

    shards = [jax.ShapeDtypeStruct(weight.shape, F32) for weight in weights]
    finished = pl.pallas_call(
        finish_body,
        out_shape=[
            jax.ShapeDtypeStruct(layer_output.shape, BF16),
            jax.ShapeDtypeStruct(input_grad.shape, F32),
            *shards,
            *shards,
            *[jax.ShapeDtypeStruct(array.shape, F32) for array in adam],
        ],
        in_specs=[anywhere] * 2 + [vmem] * 14,
        out_specs=[anywhere] * 2 + [vmem] * 14,
        scratch_shapes=[pltpu.SemaphoreType.DMA((2,))],
        compiler_params=pltpu.CompilerParams(vmem_limit_bytes=60 << 20),
        name="finish",
    )(layer_output, input_grad, moment_cat, ortho_all, mod_summed, noise_embed, *weights, *adam)

    def unpack(project, output, expand, contract):
        return (project, output.T, expand, contract.T)

    return (*finished[:2], *unpack(*finished[2:6]), *unpack(*finished[6:10]), *finished[10:])


def solution(mesh):
    in_specs = (
        P(None, "nodes", "heads"),
        P(),
        P(None, "nodes", "heads"),
        P(None, "nodes", None),
        P(None, "nodes"),
        P("nodes", "heads"),
        P("heads", "nodes"),
        P("nodes", "heads"),
        P("heads", "nodes"),
        P("nodes", "heads"),
        P("heads", "nodes"),
        P("nodes", "heads"),
        P("heads", "nodes"),
        P(None, None, "heads"),
        P(None, "heads"),
        P(None, None, "heads"),
        P(None, None, "heads"),
        P(None, "heads"),
        P(None, "heads"),
    )
    out_specs = (
        P(None, "nodes", "heads"),
        P(None, "nodes", "heads"),
        P("nodes", "heads"),
        P("heads", "nodes"),
        P("nodes", "heads"),
        P("heads", "nodes"),
        P("nodes", "heads"),
        P("heads", "nodes"),
        P("nodes", "heads"),
        P("heads", "nodes"),
        P(None, None, "heads"),
        P(None, None, "heads"),
        P(None, None, "heads"),
        P(None, "heads"),
        P(None, "heads"),
        P(None, "heads"),
    )
    return jax.shard_map(
        per_device, mesh=mesh, in_specs=in_specs, out_specs=out_specs, check_vma=False
    )
```

```python
import functools

import jax
import jax.numpy as jnp
from jax import lax
from jax.experimental import pallas as pl
from jax.experimental.pallas import tpu as pltpu
from jax.sharding import PartitionSpec as P

NS_STEPS = 5
STEP = 10


EPS_NORM = 1e-06
NEWTON_A = 3.4445
NEWTON_B = -4.775
NEWTON_C = 2.0315
MOMENTUM_DECAY = 0.5
LR_MUON = 1.0
LR_ADAM = 0.04
DECAY_WEIGHT = 0.01
BETA_FIRST = 0.9
BETA_SECOND = 0.999
EPS_ADAM = 1e-08
HIGH = lax.Precision.HIGHEST
MESH = pl.DeviceIdType.MESH
F32 = jnp.float32
BF16 = jnp.bfloat16
NN = (((1,), (0,)), ((), ()))
NT = (((1,), (1,)), ((), ()))
TN = (((0,), (0,)), ((), ()))


def mul(left, right, dims=NN):
    return lax.dot_general(left, right, dims, preferred_element_type=F32)


class Links:
    def __init__(self, send_sems, recv_sems):
        self.send_sems, self.recv_sems = send_sems, recv_sems
        self.copies, self.finished = [], []

    def send(self, source, target, device):
        slot = len(self.copies)
        copy = pltpu.make_async_remote_copy(
            src_ref=source,
            dst_ref=target,
            send_sem=self.send_sems.at[slot],
            recv_sem=self.recv_sems.at[slot],
            device_id=device,
            device_id_type=MESH,
        )
        copy.start()
        self.copies.append(copy)
        return copy

    def finish(self, copy):
        copy.wait_send()
        self.finished.append(copy)

    def close(self):
        for copy in self.copies:
            if not any(copy is other for other in self.finished):
                copy.wait_send()


def greet(devices):
    barrier = pltpu.get_barrier_semaphore()
    for device in devices:
        pl.semaphore_signal(barrier, inc=1, device_id=device, device_id_type=MESH)


def await_greetings(devices):
    pl.semaphore_wait(pltpu.get_barrier_semaphore(), len(devices))


def norm_rows(values):
    width = values.shape[-1]
    row_mean = jnp.sum(values, axis=-1, keepdims=True) / width
    square_mean = jnp.sum(values * values, axis=-1, keepdims=True) / width
    inv_root = lax.rsqrt(square_mean - row_mean * row_mean + EPS_NORM)
    return ((values - row_mean) * inv_root, inv_root)


def wide(ref, *index):
    return jnp.concatenate([ref[(head, *index)] for head in range(ref.shape[0])], axis=-1)


def mod_row(mod_ref, batch, number):
    return wide(mod_ref, slice(batch * 4 + number, batch * 4 + number + 1), slice(None))


def layer_kernel(
    patch_count,
    own_gather,
    sizes_ref,
    state_ref,
    cot_ref,
    index_ref,
    noise_ref,
    modulate_ref,
    bias_ref,
    weight_refs,
    moment_refs,
    layer_output,
    input_grad,
    moment_new,
    ortho_in,
    mod_sum,
    weight_low,
    weight_all,
    output_all,
    state_all,
    cot_all,
    mod_all,
    halo,
    a_one,
    queries,
    key_value,
    prob_low,
    mixed_all,
    hidden_one,
    a_two,
    act,
    grad_up,
    part_two,
    part_core,
    part_low,
    part_across,
    total_two,
    out_low,
    out_core,
    out_keep,
    out_across,
    grad_hidden,
    grad_attn,
    grad_mixed,
    score_low,
    grad_own,
    grad_away,
    grad_back,
    grad_projected,
    mod_part,
    mod_in,
    grad_cat,
    grad_low,
    grad_core,
    grad_line,
    grad_wide,
    moment_low,
    matrix,
    gram,
    chain,
    ortho_out,
    send_sems,
    recv_sems,
    turn_send,
    turn_recv,
):
    node, head = lax.axis_index("nodes"), lax.axis_index("heads")
    after, before = lax.rem(node + 1, patch_count), lax.rem(node + patch_count - 1, patch_count)
    across, sibling = lax.rem(head + 2, 4), head + 1 - 2 * lax.rem(head, 2)
    to_across, to_sibling, to_diagonal = (node, across), (node, sibling), (node, 3 - head)
    to_after, to_before = (after, head), (before, head)
    side, core = lax.div(head, 2), lax.rem(head, 2)
    plane, parity = lax.div(node, 2), lax.rem(node, 2)
    mirror = 1 - parity
    partner = node + 1 - 2 * parity
    to_partner = (partner, head)
    micro_count, capacity, share = state_ref.shape
    head_dim = queries.shape[-1]
    full_width = a_one.shape[-1]
    hidden = act.shape[-1]
    total = 3 * capacity
    inv_head = head_dim ** (-0.5)
    cuts = (0, 3 * head_dim, 4 * head_dim, 4 * head_dim + hidden, 4 * head_dim + 2 * hidden)
    widths = (3 * head_dim, head_dim, hidden, hidden)
    expand_columns, contract_columns = slice(cuts[2], cuts[3]), slice(cuts[3], cuts[4])
    tile = capacity // 2
    batches = range(micro_count)
    peers = [(lax.rem(node + 2 * k, patch_count), head) for k in range(1, patch_count // 2)]
    met = [to_across, to_sibling, to_diagonal]
    if own_gather:
        met += [(lax.rem(node + k, patch_count), head) for k in range(1, patch_count)]
        met += [(partner, across)]
    else:
        met += [to_after, to_before]
    greet(met)
    for number in range(modulate_ref.shape[0]):
        terms = lax.dot_general(
            noise_ref[...], modulate_ref[number], NN, precision=HIGH, preferred_element_type=F32
        )
        terms = terms + bias_ref[number : number + 1, :]
        for b in batches:
            place = b * modulate_ref.shape[0] + number
            mod_all[head, place : place + 1, :] = terms[b : b + 1]
    if own_gather:
        for number, ref in enumerate(weight_refs):
            weight_low[:, cuts[number] : cuts[number + 1]] = ref[...].astype(BF16)
    await_greetings(met)
    links = Links(send_sems, recv_sems)

    def weight(columns):
        return weight_all[:, :, columns].reshape(full_width, columns.stop - columns.start)

    def live_rows(batch, start, count):
        slots = lax.broadcasted_iota(jnp.int32, (count, 1), 0) + start
        return (slots < sizes_ref[0:1, batch : batch + 1]).astype(F32)

    def rows_at(step, count):
        start = step * count if isinstance(step, int) else pl.multiple_of(step * count, count)
        return start, pl.ds(start, count)

    first_columns = pl.ds(0, cuts[2])
    other_columns = pl.ds(cuts[2], cuts[4] - cuts[2])

    def spread(columns):
        part = weight_low.at[:, columns]
        into = weight_all.at[node, :, columns]
        return [links.send(part, into, to) for to in peers], (part, into)

    def pass_on(arriving, columns, which=(0, 1, 2)):
        passed = []
        for k in which:
            arriving[k].wait_recv()
            owner = lax.rem(node + patch_count - 2 * (k + 1), patch_count)
            part = weight_all.at[owner, :, columns]
            passed.append(links.send(part, part, to_partner))
        return passed

    mod_copies = [
        links.send(mod_all.at[head], mod_all.at[head], to) for to in (to_across, to_sibling, to_diagonal)
    ]
    if own_gather:
        first_peers, first_partner = spread(first_columns)
        first_partner = [links.send(*first_partner, to_partner)]
    state_across, state_after, state_before, state_sibling = [], [], [], []
    for b in batches:
        state_across.append(links.send(state_ref.at[b], state_all.at[head, b], to_across))
        state_after.append(links.send(state_ref.at[b], halo.at[0, head, b], to_after))
        state_before.append(links.send(state_ref.at[b], halo.at[1, head, b], to_before))
        state_sibling.append(links.send(state_ref.at[b], state_all.at[head, b], to_sibling))
    if own_gather:
        weight_all[node] = weight_low[...]
    state_all[head] = state_ref[...]
    cot_all[head] = cot_ref[...]

    group = index_ref.shape[-1] // 16
    blocks = total // share

    def count_group(batch, place):
        ids = index_ref[batch, pl.ds(place, 1), :]
        lanes = lax.broadcasted_iota(jnp.int32, ids.shape, 1)
        code = (ids >> 7) + 16 * (lanes >> 4)
        rows = lax.broadcasted_iota(jnp.int32, (blocks * group, ids.shape[1]), 0)
        pick = jnp.where(code == (rows // group) + 16 * (rows % group), 1.0, 0.0).astype(BF16)
        slots = lax.broadcasted_iota(jnp.int32, (share, ids.shape[1]), 0)
        spot = jnp.where((ids & 127) == slots, 1.0, 0.0).astype(BF16)
        found = mul(pick, spot, NT).astype(BF16)
        into = pl.ds(pl.multiple_of(place * group, group), group)
        for block in range(blocks):
            prob_low[batch, into, block * share : (block + 1) * share] = found[
                block * group : (block + 1) * group
            ]

    def count(batch):
        pl.loop(0, capacity // group, unroll=4)(lambda place: count_group(batch, place))

    pass_state, halo_across, halo_sibling = [], [], []

    def second_hops(b):
        state_across[b].wait_recv()
        part = state_all.at[across, b]
        pass_state.append(links.send(part, part, to_sibling))
        to_chip, to_core = [], []
        for k, copy in ((0, state_after[b]), (1, state_before[b])):
            copy.wait_recv()
            part = halo.at[k, head, b]
            to_chip.append(links.send(part, part, to_across))
            to_core.append(links.send(part, part, to_sibling))
        halo_across.append(to_chip)
        halo_sibling.append(to_core)

    if own_gather:
        other_peers, other_partner = spread(other_columns)
    for b in batches:
        count(b)
    second_hops(0)
    if own_gather:
        first_passed = pass_on(first_peers, first_columns)
    cot_across = [links.send(cot_ref.at[0], cot_all.at[head, 0], to_across)]
    second_hops(1)
    if own_gather:
        other_partner = [links.send(*other_partner, to_partner)]
    cot_across += [links.send(cot_ref.at[b], cot_all.at[head, b], to_across) for b in batches[1:]]
    cot_sibling = links.send(cot_ref, cot_all.at[head], to_sibling)

    def project(source, patch, batch):
        shift, scale = mod_row(mod_all, batch, 0), 1.0 + mod_row(mod_all, batch, 1)

        @pl.loop(0, capacity // tile)
        def _(step):
            _, rows = rows_at(step, tile)
            normed, _ = norm_rows(wide(source, batch, rows, slice(None)).astype(F32))
            a_rows = (normed * scale + shift).astype(BF16)
            a_one[patch * micro_count + batch, rows, :] = a_rows
            first = 0 if patch == 1 else head_dim
            out = mul(a_rows, weight(slice(first, cuts[1]))).astype(BF16)
            if patch == 1:
                queries[batch, rows, :] = out[:, :head_dim]
            key_value[batch, patch, rows, :] = out[:, out.shape[1] - 2 * head_dim :]

    def project_all(b):
        state_sibling[b].wait_recv()
        pass_state[b].wait_recv()
        project(state_all, 1, b)
        for k in range(2):
            halo_across[b][k].wait_recv()
            part = halo.at[k, across, b]
            halo_sibling[b].append(links.send(part, part, to_sibling))
        for copy in halo_sibling[b]:
            copy.wait_recv()
        project(halo.at[0], 0, b)
        project(halo.at[1], 2, b)

    def attend(batch):
        attend_rows = 128

        @pl.loop(0, capacity // attend_rows)
        def _(step):
            _, rows = rows_at(step, attend_rows)
            keys = key_value[batch, :, :, :head_dim].reshape(total, head_dim)
            values = key_value[batch, :, :, head_dim:].reshape(total, head_dim)
            scores = mul(queries[batch, rows, :], keys, NT) * inv_head
            times = prob_low[batch, rows, :].astype(F32)
            scores = jnp.where(times > 0.0, scores, -1e30)
            exps = jnp.exp(scores - jnp.max(scores, axis=-1, keepdims=True)) * times
            prob = (exps * (1.0 / jnp.sum(exps, axis=-1, keepdims=True))).astype(BF16)
            prob_low[batch, rows, :] = prob
            mixed_all[head, batch, rows, :] = mul(prob, values).astype(BF16)

        part = mixed_all.at[head, batch]
        return links.send(part, part, to_across), links.send(part, part, to_sibling)

    def pass_mixed(batch, copies):
        copies[0].wait_recv()
        part = mixed_all.at[across, batch]
        return [copies[1], links.send(part, part, to_sibling)]

    def wait_all(copies):
        for copy in copies:
            copy.wait_recv()

    wait_all(mod_copies)
    ready = [cot_sibling]
    if own_gather:
        wait_all(first_partner + first_passed)
        output_all[head] = weight_all[:, :, cuts[1] : cuts[2]]
        output_part = weight_all.at[:, :, pl.ds(cuts[1], head_dim)]
        output_across = links.send(output_part, output_all.at[head], to_across)
        ready.append(links.send(output_part, output_all.at[head], to_sibling))
        other_passed = pass_on(other_peers, other_columns, (0,))
    project_all(0)
    if own_gather:
        other_passed += pass_on(other_peers, other_columns, (1,))
    mixed_first = attend(0)
    if own_gather:
        other_passed += pass_on(other_peers, other_columns, (2,))
    project_all(1)
    mixed_first = pass_mixed(0, mixed_first)
    wait_all(cot_across)
    ready.append(links.send(cot_all.at[across], cot_all.at[across], to_sibling))
    if own_gather:
        output_across.wait_recv()
        ready.append(links.send(output_all.at[across], output_all.at[across], to_sibling))
    mixed_second = attend(1)
    if own_gather:
        ready += other_partner + other_passed
    wait_all(ready + mixed_first)

    def feed_forward(batch, step):
        start, rows = rows_at(step, tile)
        mixed = wide(mixed_all, batch, rows, slice(None))
        mixer = jnp.concatenate(
            [output_all[k].reshape(full_width, head_dim) for k in range(output_all.shape[0])], axis=-1
        )
        hid = wide(state_all, batch, rows, slice(None)).astype(F32) + mul(mixed, mixer, NT)
        hidden_one[batch, rows, :] = hid
        normed, _ = norm_rows(hid)
        a_rows = (normed * (1.0 + mod_row(mod_all, batch, 3)) + mod_row(mod_all, batch, 2)).astype(BF16)
        a_two[batch, rows, :] = a_rows
        up = mul(a_rows, weight(expand_columns))
        gate = jax.nn.sigmoid(up)
        acted = (up * gate).astype(BF16)
        act[batch, rows, :] = acted
        live = live_rows(batch, start, tile)
        cot = (wide(cot_all, batch, rows, slice(None)).astype(F32) * live).astype(BF16)
        grad_act = mul(cot, weight(contract_columns))
        grad_rows = (grad_act * gate * (1.0 + up * (1.0 - gate))).astype(BF16)
        grad_up[batch, rows, :] = grad_rows
        back = mul(grad_rows, weight(expand_columns), NT)
        out = mul(acted, weight(contract_columns), NT)
        for k in range(4):
            block = slice(k * head_dim, (k + 1) * head_dim)
            part_two[batch, k % 2, k // 2, rows, :] = back[:, block]
            out_low[batch, k % 2, k // 2, rows, :] = out[:, block].astype(BF16)

    def to_core(batch):
        return links.send(part_two.at[batch, 1 - core], part_core.at[batch], to_sibling)

    def to_side(batch, copy):
        copy.wait_recv()
        for k in range(2):
            chip = part_two[batch, core, k] + part_core[batch, k]
            part_core[batch, k] = chip
            part_low[batch, k] = chip.astype(BF16)
        return links.send(part_low.at[batch], part_across.at[batch], to_across)

    def to_all(batch, copy):
        copy.wait_recv()
        for k in range(2):
            total_two[batch, core, k] = part_core[batch, k] + part_across[batch, k].astype(F32)
        return links.send(total_two.at[batch, core], total_two.at[batch, core], to_sibling)

    def total_rows(batch, rows):
        return jnp.concatenate(
            [total_two[batch, k % 2, k // 2, rows, :] for k in range(4)], axis=-1
        )

    def back_norm(grad, normed, root):
        mean_grad = jnp.sum(grad, axis=-1, keepdims=True) / full_width
        mean_cross = jnp.sum(grad * normed, axis=-1, keepdims=True) / full_width
        return root * (grad - mean_grad - normed * mean_cross)

    def add_mod(batch, number, values):
        sums = jnp.sum(values, axis=0, keepdims=True)
        place = batch * 4 + number
        for k in range(4):
            mod_part[k, place : place + 1, :] += sums[:, k * head_dim : (k + 1) * head_dim]

    def own_block(values):
        own = jnp.zeros((values.shape[0], head_dim), F32)
        for k in range(4):
            own = own + jnp.where(head == k, values[:, k * head_dim : (k + 1) * head_dim], 0.0)
        return own

    for k in range(4):
        mod_part[k] = jnp.zeros(mod_part.shape[1:], F32)

    def store_grad(step, columns, value, add=False):
        half = full_width // 8
        for k in range(2):
            part = value[k * half : (k + 1) * half]
            if add:
                part = grad_cat[k, step, :, columns] + part
            grad_cat[k, step, :, columns] = part
            grad_low[k, step, :, columns] = part.astype(BF16)

    def both(ref, columns):
        return ref[:, :, columns].reshape(micro_count * capacity, -1)

    def one_pair(patch, columns):
        pair = a_one[patch * micro_count : (patch + 1) * micro_count, :, columns]
        return pair.reshape(micro_count * capacity, -1)

    def live_cot(batch, columns):
        return (cot_all[columns, batch].astype(F32) * live_rows(batch, 0, capacity)).astype(BF16)

    def expand_grad(batch, step):
        columns = pl.ds(pl.multiple_of(step * head_dim, head_dim), head_dim)
        value = mul(a_two[batch, :, columns], grad_up[batch], TN)
        store_grad(step, expand_columns, value, batch > 0)

    def contract_grad(batch, step):
        store_grad(step, contract_columns, mul(live_cot(batch, step), act[batch], TN), batch > 0)

    pl.loop(0, 2)(lambda step: feed_forward(0, step))
    core_first = to_core(0)
    mixed_second = pass_mixed(1, mixed_second)
    side_first = to_side(0, core_first)

    @pl.loop(0, 4)
    def _(step):
        expand_grad(0, step)
        contract_grad(0, step)

    wait_all(mixed_second)
    pl.loop(0, 2)(lambda step: feed_forward(1, step))
    core_second = to_core(1)

    late_one, late_two = slice(0, 2 * head_dim), slice(2 * head_dim, cuts[2])

    def grad_pair(columns):
        return links.send(
            grad_low.at[1 - parity, :, :, columns], grad_core.at[:, :, columns], to_partner
        )

    def grad_planes(copy, columns):
        copy.wait_recv()
        for k in range(4):
            summed = grad_cat[parity, k, :, columns] + grad_core[k, :, columns].astype(F32)
            grad_cat[parity, k, :, columns] = summed
            grad_low[parity, k, :, columns] = summed.astype(BF16)
        sent = []
        for k in range(1, 4):
            target = lax.rem(plane + k, 4)
            sent.append(
                links.send(
                    grad_low.at[parity, target, :, columns],
                    grad_line.at[k - 1, :, columns],
                    (2 * target + parity, head),
                )
            )
        return sent

    def grad_finish(copies, columns):
        wait_all(copies)
        summed = grad_cat[parity, plane, :, columns]
        for k in range(3):
            summed = summed + grad_line[k, :, columns].astype(F32)
        moment_new[:, columns] = summed

    def grad_wide_planes(columns):
        sent = []
        for k in range(1, 4):
            target = lax.rem(plane + k, 4)
            sent.append(
                links.send(
                    grad_low.at[:, target, :, columns],
                    grad_wide.at[k - 1, :, :, columns],
                    (2 * target + parity, head),
                )
            )
        return sent

    def grad_wide_pair(copies, columns):
        wait_all(copies)
        for pair in range(2):
            summed = grad_cat[pair, plane, :, columns]
            for k in range(3):
                summed = summed + grad_wide[k, pair, :, columns].astype(F32)
            grad_cat[pair, plane, :, columns] = summed
            grad_low[pair, plane, :, columns] = summed.astype(BF16)
        return links.send(
            grad_low.at[mirror, plane, :, columns], grad_core.at[plane, :, columns], to_partner
        )

    def grad_wide_finish(copy, columns):
        copy.wait_recv()
        summed = grad_cat[parity, plane, :, columns] + grad_core[plane, :, columns].astype(F32)
        moment_new[:, columns] = summed

    def store_moment(numbers):
        for number in numbers:
            own = slice(cuts[number], cuts[number + 1])
            moment = MOMENTUM_DECAY * moment_refs[number][...] + moment_new[:, own]
            moment_new[:, own] = moment
            moment_low[:, own] = moment.astype(BF16)

    pl.loop(0, 4)(lambda step: expand_grad(1, step))
    if own_gather:
        expand_pair = grad_pair(expand_columns)
    pl.loop(0, 4)(lambda step: contract_grad(1, step))
    if own_gather:
        contract_wide = grad_wide_planes(contract_columns)
    side_second = to_side(1, core_second)
    all_first = to_all(0, side_first)
    out_copies = [links.send(out_low.at[b, 1 - core], out_core.at[b], to_sibling) for b in batches]

    def norm_two_back(batch):
        @pl.loop(0, capacity // tile)
        def _(step):
            start, rows = rows_at(step, tile)
            normed, root = norm_rows(hidden_one[batch, rows, :])
            grad = total_rows(batch, rows)
            add_mod(batch, 2, grad)
            add_mod(batch, 3, grad * normed)
            cot = wide(cot_all, batch, rows, slice(None)).astype(F32) * live_rows(batch, start, tile)
            grad = cot + back_norm(grad * (1.0 + mod_row(mod_all, batch, 3)), normed, root)
            grad_hidden[batch, rows, :] = own_block(grad)
            low = grad.astype(BF16)
            grad_attn[batch, rows, :] = low
            grad_mixed[batch, rows, :] = mul(low, weight(slice(cuts[1], cuts[2]))).astype(BF16)

    def attend_back(batch, between=lambda: None):
        attend_rows = 128

        @pl.loop(0, capacity // attend_rows)
        def _(step):
            _, rows = rows_at(step, attend_rows)
            keys = key_value[batch, :, :, :head_dim].reshape(total, head_dim)
            values = key_value[batch, :, :, head_dim:].reshape(total, head_dim)
            prob = prob_low[batch, rows, :].astype(F32)
            grad_prob = mul(grad_mixed[batch, rows, :], values, NT)
            mean = jnp.sum(prob * grad_prob, axis=-1, keepdims=True)
            score = (prob * (grad_prob - mean) * inv_head).astype(BF16)
            score_low[rows, :] = score
            grad_projected[batch, rows, :head_dim] = mul(score, keys).astype(BF16)

        between()
        for patch in range(3):
            slots = slice(patch * capacity, (patch + 1) * capacity)
            grad_key = mul(score_low[:, slots], queries[batch], TN)
            grad_value = mul(prob_low[batch, :, slots], grad_mixed[batch], TN)
            if patch == 1:
                grad_own[batch, :, :head_dim] = grad_key
                grad_own[batch, :, head_dim:] = grad_value
            else:
                grad_away[batch, patch // 2, :, :head_dim] = grad_key.astype(BF16)
                grad_away[batch, patch // 2, :, head_dim:] = grad_value.astype(BF16)

    def send_back(batch):
        return [
            links.send(grad_away.at[batch, 0], grad_back.at[batch, 1], to_before),
            links.send(grad_away.at[batch, 1], grad_back.at[batch, 0], to_after),
        ]

    owners = (1, 2, 0, 3)

    def turn(source, target, device, send_slot, recv_slot):
        return pltpu.make_async_remote_copy(
            src_ref=source,
            dst_ref=target,
            send_sem=turn_send.at[send_slot],
            recv_sem=turn_recv.at[recv_slot],
            device_id=device,
            device_id_type=MESH,
        )

    def to_owner(number, sender):
        return turn(
            moment_low.at[:, slice(cuts[number], cuts[number + 1])],
            matrix.at[head, parity, sender, :, : widths[number]],
            (2 * owners[number] + parity, head),
            number,
            sender,
        )

    def give(width, number):
        block, pair, device = (
            (head, parity, to_across),
            (head, parity, to_partner),
            (head, parity, (partner, across)),
            (head, parity, to_sibling),
            (across, parity, to_sibling),
            (head, mirror, to_sibling),
            (across, mirror, to_sibling),
        )[number]
        part = matrix.at[block, pair, :, :, :width]
        return turn(part, part, device, 4 + number, 4 + number)

    def own_to_owner(numbers):
        for number in numbers:

            @pl.when(plane != owners[number])
            def _():
                to_owner(number, plane).start()

            @pl.when(plane == owners[number])
            def _():
                matrix[head, parity, plane, :, : widths[number]] = moment_low[
                    :, cuts[number] : cuts[number + 1]
                ]

    def own_arrive(numbers):
        for number in numbers:

            @pl.when(plane == owners[number])
            def _():
                for other in range(4):
                    if other != owners[number]:
                        to_owner(number, other).wait_recv()
                for k in range(4):
                    give(widths[number], k).start()

            @pl.when(plane != owners[number])
            def _():
                to_owner(number, plane).wait_send()

    all_first.wait_recv()
    norm_two_back(0)
    if own_gather:
        expand_line = grad_planes(expand_pair, expand_columns)
    all_second = []
    attend_back(0, lambda: all_second.append(to_all(1, side_second)))
    all_second = all_second[0]
    back_first = send_back(0)
    out_across_copies = []
    for batch in batches:
        out_copies[batch].wait_recv()
        for k in range(2):
            chip = out_low[batch, core, k].astype(F32) + out_core[batch, k].astype(F32)
            out_keep[batch, k] = chip
            out_core[batch, k] = chip.astype(BF16)
        out_across_copies.append(
            links.send(out_core.at[batch, 1 - side], out_across.at[batch], to_across)
        )
    all_second.wait_recv()
    norm_two_back(1)
    attend_back(1)
    if own_gather:
        contract_pair = grad_wide_pair(contract_wide, contract_columns)

    @pl.loop(0, 4)
    def _(step):
        columns = pl.ds(pl.multiple_of(step * head_dim, head_dim), head_dim)
        own = jnp.concatenate(
            [both(grad_projected, slice(0, head_dim)), grad_own[...].reshape(-1, 2 * head_dim).astype(BF16)], axis=1
        )
        own = mul(one_pair(1, columns), own, TN)
        store_grad(step, slice(0, head_dim), own[:, :head_dim])
        rest = own[:, head_dim:]
        for patch in (0, 2):
            away = grad_away[:, patch // 2].reshape(-1, 2 * head_dim)
            rest = rest + mul(one_pair(patch, columns), away, TN)
        store_grad(step, slice(head_dim, cuts[1]), rest)
        own_mixed = mixed_all[head].reshape(-1, head_dim)
        store_grad(step, slice(cuts[1], cuts[2]), mul(both(grad_attn, columns), own_mixed, TN))

    if own_gather:
        late_wide = grad_wide_planes(late_two)
        late_pair = grad_pair(late_one)
    back_second = send_back(1)
    if own_gather:
        grad_finish(expand_line, expand_columns)
        grad_wide_finish(contract_pair, contract_columns)
        store_moment((2, 3))
        own_to_owner((2, 3))
        late_line = grad_planes(late_pair, late_one)
        late_pair = grad_wide_pair(late_wide, late_two)
    for batch in batches:
        out_across_copies[batch].wait_recv()
        own = hidden_one[batch, :, pl.ds(pl.multiple_of(head * head_dim, head_dim), head_dim)]
        result = own + out_keep[batch, side] + out_across[batch].astype(F32)
        layer_output[batch] = (result * live_rows(batch, 0, capacity)).astype(BF16)

    for copy in (core_first, core_second, side_first, side_second, all_first, all_second):
        links.finish(copy)

    def rows_back(batch, copies):
        wait_all(copies)
        whole = grad_own[batch] + grad_back[batch, 0].astype(F32) + grad_back[batch, 1].astype(F32)
        grad_projected[batch, :, head_dim:] = whole.astype(BF16)

        @pl.loop(0, capacity // tile)
        def _(step):
            _, rows = rows_at(step, tile)
            back = mul(grad_projected[batch, rows, :], weight(slice(0, cuts[1])), NT)
            for k in range(4):
                part_two[batch, k % 2, k // 2, rows, :] = back[:, k * head_dim : (k + 1) * head_dim]

        return to_core(batch)

    def rows_end(batch, copy):
        copy.wait_recv()

        @pl.loop(0, capacity // tile)
        def _(step):
            _, rows = rows_at(step, tile)
            normed, root = norm_rows(wide(state_all, batch, rows, slice(None)).astype(F32))
            grad = total_rows(batch, rows)
            add_mod(batch, 0, grad)
            add_mod(batch, 1, grad * normed)
            grad = back_norm(grad * (1.0 + mod_row(mod_all, batch, 1)), normed, root)
            input_grad[batch, rows, :] = own_block(grad) + grad_hidden[batch, rows, :]

    one_core = [rows_back(0, back_first)]

    if not own_gather:
        one_core.append(rows_back(1, back_second))
        one_side = [to_side(b, one_core[b]) for b in batches]
        one_all = [to_all(b, one_side[b]) for b in batches]
        for b in batches:
            rows_end(b, one_all[b])
        mod_sum[...] = mod_part[head]
        for k in range(8):
            moment_new[k] = grad_cat[k % 2, k // 2]
        links.close()
        return

    own_arrive((2, 3))
    grad_wide_finish(late_pair, late_two)
    grad_finish(late_line, late_one)
    store_moment((0, 1))
    own_to_owner((0, 1))
    one_core.append(rows_back(1, back_second))
    own_arrive((0, 1))
    one_side = [to_side(b, one_core[b]) for b in batches]
    half = full_width // 2

    def gather_plane(width):
        for k in range(3):
            give(width, k).wait_recv()
            give(width, 4 + k).start()
        for k in range(3, 7):
            give(width, k).wait_recv()
        for k in range(7):
            give(width, k).wait_send()

        @pl.loop(0, 2)
        def _(step):
            _, rows = rows_at(step, half)
            summed = jnp.zeros((half, full_width), F32)
            for k in range(4):
                left = matrix[k, step, :, :, :width].reshape(half, width)
                right = matrix[k, :, :, :, :width].reshape(full_width, width)
                summed = summed + mul(left, right, NT)
            gram[rows, :] = summed

    for first, second, width in ((1, 1, widths[0]), (2, 2, widths[1]), (0, 3, hidden)):

        @pl.when((plane == first) | (plane == second))
        def _():
            gather_plane(width)

    gram_pair, factor_pair, turn_pair = (a_one.at[pl.ds(k, 2)] for k in (0, 2, 4))

    def put_pair(ref, value, rows=slice(None)):
        high = value.astype(BF16)
        ref[0, rows, :] = high
        ref[1, rows, :] = (value - high.astype(F32)).astype(BF16)

    def times(left, right, rows=slice(None)):
        left_high, left_low = left[0, rows, :], left[1, rows, :]
        right_high, right_low = right[0], right[1]
        return mul(
            jnp.concatenate([left_high, left_high, left_low], axis=1),
            jnp.concatenate([right_high, right_low, right_high], axis=0),
        )

    def diagonal(count, start=0):
        rows = lax.broadcasted_iota(jnp.int32, (count, full_width), 0) + start
        return rows == lax.broadcasted_iota(jnp.int32, (count, full_width), 1)

    trace = jnp.zeros((1, 1), F32)
    for step in range(2):
        kept = jnp.where(diagonal(half, step * half), gram[step * half : (step + 1) * half, :], 0.0)
        trace = trace + jnp.sum(jnp.sum(kept, axis=1, keepdims=True), axis=0, keepdims=True)
    scale = 1.0 / (jnp.sqrt(trace) + 1e-07)
    gram[...] = gram[...] * (scale * scale)
    put_pair(gram_pair, gram[...])
    own = pl.ds(pl.multiple_of(parity * half, half), half)

    one_all = []
    for repeat in range(NS_STEPS - 1):
        factor = NEWTON_B * gram[...] + NEWTON_C * times(gram_pair, gram_pair)
        factor = factor + jnp.where(diagonal(full_width), NEWTON_A, 0.0)
        put_pair(factor_pair, factor)
        if repeat == 0:
            put_pair(chain.at[0], factor)
        else:
            put_pair(chain.at[repeat % 2], times(factor_pair, chain.at[(repeat + 1) % 2]))
        put_pair(turn_pair, times(factor_pair, gram_pair))
        gram[...] = times(factor_pair, turn_pair)
        put_pair(gram_pair, gram[...])
        if repeat in (1, 2):
            one_all.append(to_all(repeat - 1, one_side[repeat - 1]))
    factor = NEWTON_B * gram[own, :] + NEWTON_C * times(gram_pair, gram_pair, own)
    factor = factor + jnp.where(diagonal(half, parity * half), NEWTON_A, 0.0)
    put_pair(factor_pair, factor, own)
    final = times(factor_pair, chain.at[(NS_STEPS - 2) % 2], own)

    put_pair(chain.at[0], final, slice(0, half))

    def ortho_copy(number, k):
        target = (owners[number] + k) % 4
        width = widths[number]
        return turn(
            ortho_out.at[target, :, :width],
            ortho_in.at[number, :, :width],
            (2 * target + parity, head),
            11 + k,
            11 + number,
        )

    for number in range(4):

        @pl.when(plane == owners[number])
        def _():
            width = widths[number]
            left = jnp.concatenate([chain[0, k, :half, :] for k in range(2)], axis=-1)
            right = matrix[head, :, :, :, :width].reshape(full_width, width)
            value = mul(left, jnp.concatenate([right, right], axis=0)) * scale
            ortho_out[:, :, :width] = value.astype(BF16).reshape(4, half // 4, width)
            for k in range(1, 4):
                ortho_copy(number, k).start()
            ortho_in[number, :, :width] = ortho_out[plane, :, :width]

    for b in batches:
        rows_end(b, one_all[b])
    mod_copies = [
        links.send(mod_part.at[head], mod_in.at[k - 1], (lax.rem(node + k, patch_count), head))
        for k in range(1, patch_count)
    ]
    for number in range(4):

        @pl.when(plane != owners[number])
        def _():
            ortho_copy(number, 1).wait_recv()

        @pl.when(plane == owners[number])
        def _():
            for k in range(1, 4):
                ortho_copy(number, k).wait_send()

    summed = mod_part[head]
    wait_all(mod_copies)
    for k in range(patch_count - 1):
        summed = summed + mod_in[k]
    mod_sum[...] = summed
    links.close()


def finish_kernel(
    cuts,
    factors,
    layer_ref,
    input_ref,
    moment_ref,
    ortho_ref,
    mod_ref,
    noise_ref,
    weight_refs,
    adam_refs,
    layer_out,
    input_out,
    moment_outs,
    weight_outs,
    adam_outs,
):
    layer_out[...] = layer_ref[...]
    input_out[...] = input_ref[...]
    for number in range(4):
        columns = slice(cuts[number], cuts[number + 1])
        moment_outs[number][...] = moment_ref[:, columns]
        ortho = ortho_ref[number, :, : cuts[number + 1] - cuts[number]].astype(F32)
        weight_outs[number][...] = (
            weight_refs[number][...] * (1.0 - LR_MUON * DECAY_WEIGHT) - (LR_MUON * factors[number]) * ortho
        )
    weight, first, second, bias, first_bias, second_bias = adam_refs
    micro_count = noise_ref.shape[0]
    for number in range(4):
        rows = [mod_ref[b * 4 + number : b * 4 + number + 1, :] for b in range(micro_count)]
        grad = lax.dot_general(
            noise_ref[...], jnp.concatenate(rows, axis=0), TN, precision=HIGH, preferred_element_type=F32
        )
        place = slice(number, number + 1)
        stepped = adam_step(weight[number], first[number], second[number], grad)
        for ref, value in zip(adam_outs[:3], stepped):
            ref[number] = value
        stepped = adam_step(bias[place, :], first_bias[place, :], second_bias[place, :], sum(rows))
        for ref, value in zip(adam_outs[3:], stepped):
            ref[place, :] = value


def adam_step(weight, first_old, second_old, gradient):
    first_new = BETA_FIRST * first_old + (1.0 - BETA_FIRST) * gradient
    second_new = BETA_SECOND * second_old + (1.0 - BETA_SECOND) * gradient * gradient
    first_hat = first_new / (1.0 - BETA_FIRST**STEP)
    second_hat = second_new / (1.0 - BETA_SECOND**STEP)
    updated = weight * (1.0 - LR_ADAM * DECAY_WEIGHT) - LR_ADAM * first_hat / (
        jnp.sqrt(second_hat) + EPS_ADAM
    )
    return (first_new, second_new, updated)


def orthogonal(matrix):
    scale = 1.0 / (jnp.sqrt(jnp.sum(matrix * matrix)) + 1e-07)
    gram = jnp.dot(matrix, matrix.T, precision=HIGH) * (scale * scale)
    eye = jnp.eye(gram.shape[0], dtype=F32)
    chain = None
    for repeat in range(NS_STEPS):
        factor = NEWTON_A * eye + NEWTON_B * gram + NEWTON_C * jnp.dot(gram, gram, precision=HIGH)
        chain = factor if chain is None else jnp.dot(factor, chain, precision=HIGH)
        if repeat < NS_STEPS - 1:
            gram = jnp.dot(factor, jnp.dot(factor, gram, precision=HIGH), precision=HIGH)
    return jnp.dot(chain, matrix, precision=HIGH) * scale


def per_device(
    node_state,
    noise_embed,
    out_grad,
    neighbours,
    patch_sizes,
    w_project,
    w_output,
    w_expand,
    w_contract,
    momentum_project,
    momentum_output,
    momentum_expand,
    momentum_contract,
    w_modulate,
    b_modulate,
    first_modulate,
    second_modulate,
    first_bias,
    second_bias,
):
    micro_count, capacity, share = node_state.shape
    head_count = lax.axis_size("heads")
    patch_count = lax.axis_size("nodes")
    full_width = share * head_count
    head_dim = w_output.shape[0]
    total_rows = capacity * patch_count
    patch_index = lax.axis_index("nodes")
    head_index = lax.axis_index("heads")
    inv_head = head_dim ** (-0.5)
    hidden = w_expand.shape[1]
    shard_rows = w_project.shape[0]
    own_gather = patch_count == 8

    local_index = jnp.mod(neighbours - (patch_index - 1) * capacity, total_rows)
    index_rows = local_index.reshape(micro_count, capacity // 16, 256)
    weights = [w_project, w_output.T, w_expand, w_contract.T]
    moments = [momentum_project, momentum_output.T, momentum_expand, momentum_contract.T]
    cuts = (0, 3 * head_dim, 4 * head_dim, 4 * head_dim + hidden, 4 * head_dim + 2 * hidden)
    factors = (1.0, 1.0, 1.0, (head_count * hidden / full_width) ** 0.5)
    weight_width = cuts[4]
    vmem = pl.BlockSpec(memory_space=pltpu.VMEM)
    def scratch(dtype, *shape):
        return pltpu.VMEM(shape, dtype)

    rows_all = (head_count, micro_count, capacity, share)
    blocks = (micro_count, 2, 2, capacity, head_dim)
    half_blocks = (micro_count, 2, capacity, head_dim)
    rows_wide = (micro_count, capacity, full_width)
    rows_hidden = (micro_count, capacity, hidden)
    rows_own = (micro_count, capacity, head_dim)
    key_value_rows = (capacity, 2 * head_dim)
    eighth = full_width // 8
    scratches = [
        scratch(BF16, eighth, weight_width),
        scratch(BF16, 8, eighth, weight_width),
        scratch(BF16, head_count, 8, eighth, head_dim),
    ]
    scratches = scratches if own_gather else []
    scratches += [
        scratch(BF16, *rows_all),
        scratch(BF16, *rows_all),
        scratch(F32, head_count, 4 * micro_count, share),
        scratch(BF16, 2, *rows_all),
        scratch(BF16, 3 * micro_count, capacity, full_width),
        scratch(BF16, *rows_own),
        scratch(BF16, micro_count, 3, *key_value_rows),
        scratch(BF16, micro_count, capacity, 3 * capacity),
        scratch(BF16, *rows_all),
        scratch(F32, *rows_wide),
        scratch(BF16, *rows_wide),
        scratch(BF16, *rows_hidden),
        scratch(BF16, *rows_hidden),
        scratch(F32, *blocks),
        scratch(F32, *half_blocks),
        scratch(BF16, *half_blocks),
        scratch(BF16, *half_blocks),
        scratch(F32, *blocks),
        scratch(BF16, *blocks),
        scratch(BF16, *half_blocks),
        scratch(F32, *half_blocks),
        scratch(BF16, *rows_own),
        scratch(F32, *rows_own),
        scratch(BF16, *rows_wide),
        scratch(BF16, *rows_own),
        scratch(BF16, capacity, 3 * capacity),
        scratch(F32, micro_count, *key_value_rows),
        scratch(BF16, micro_count, 2, *key_value_rows),
        scratch(BF16, micro_count, 2, *key_value_rows),
        scratch(BF16, micro_count, capacity, 3 * head_dim),
        scratch(F32, head_count, 4 * micro_count, share),
        scratch(F32, 8, 4 * micro_count, share),
        scratch(F32, 2, 4, eighth, weight_width),
        scratch(BF16, 2, 4, eighth, weight_width),
        scratch(BF16, 4, eighth, weight_width),
        scratch(BF16, 3, eighth, weight_width),
        scratch(BF16, 3, 2, eighth, weight_width),
    ]
    last = [
        scratch(BF16, eighth, weight_width),
        scratch(BF16, head_count, 2, 4, eighth, hidden),
        scratch(F32, full_width, full_width),
        scratch(BF16, 2, 2, full_width, full_width),
        scratch(BF16, 4, eighth, hidden),
    ]
    semaphores = [pltpu.SemaphoreType.DMA((count,)) for count in (96, 96, 16, 16)]
    operands = [patch_sizes.T, node_state, out_grad, index_rows, noise_embed, w_modulate, b_modulate]
    out_shape = [
        jax.ShapeDtypeStruct((micro_count, capacity, share), BF16),
        jax.ShapeDtypeStruct((micro_count, capacity, share), F32),
    ]
    summed_shape = jax.ShapeDtypeStruct((4 * micro_count, share), F32)
    if own_gather:
        operands += weights + moments
        out_shape += [
            jax.ShapeDtypeStruct((eighth, weight_width), F32),
            jax.ShapeDtypeStruct((4, eighth, hidden), BF16),
            summed_shape,
        ]
        scratches += last
    else:
        low_cat = jnp.concatenate(weights, axis=1).astype(BF16)
        low_cat = lax.all_gather(low_cat, "nodes", axis=0, tiled=True)
        low_cat = low_cat.reshape(8, eighth, weight_width)
        output_all = lax.all_gather(
            low_cat[:, :, 3 * head_dim : 4 * head_dim], "heads", axis=0, tiled=False
        )
        operands += [low_cat, output_all]
        out_shape += [jax.ShapeDtypeStruct((8, eighth, weight_width), F32), summed_shape]

    def layer_body(*refs):
        refs = list(refs)
        if own_gather:
            refs[7:15] = [refs[7:11], refs[11:15]]
        else:
            gathered = refs[7:9]
            refs[7:9] = [None, None]
            refs[12:12] = [None]
            refs[14:14] = [None] + gathered
            refs[-4:-4] = [None] * len(last)
        layer_kernel(patch_count, own_gather, *refs)

    updated = pl.pallas_call(
        layer_body,
        out_shape=out_shape,
        in_specs=[vmem] * len(operands),
        out_specs=[vmem] * len(out_shape),
        scratch_shapes=scratches + semaphores,
        compiler_params=pltpu.CompilerParams(
            collective_id=0, has_side_effects=True, vmem_limit_bytes=60 << 20
        ),
        name="layer",
    )(*operands)
    if own_gather:
        layer_output, input_grad, moment_cat, ortho_all, mod_summed = updated
    else:
        layer_output, input_grad, grad_cat, mod_summed = updated
        mod_summed = lax.psum(mod_summed, "nodes")
        moment_cat = MOMENTUM_DECAY * jnp.concatenate(moments, axis=1) + lax.psum_scatter(
            grad_cat.reshape(full_width, weight_width), "nodes", scatter_dimension=0, tiled=True
        )
        whole = lax.all_gather(moment_cat.astype(BF16), ("nodes", "heads"), axis=0, tiled=False)
        whole = whole.reshape(patch_count, head_count, shard_rows, weight_width)
        whole = whole.transpose(0, 2, 1, 3).reshape(full_width, head_count, weight_width).astype(F32)
        pieces = []
        for number in range(4):
            columns = cuts[number + 1] - cuts[number]
            matrix = whole[:, :, cuts[number] : cuts[number + 1]].reshape(full_width, head_count * columns)
            ortho = lax.dynamic_slice(
                orthogonal(matrix),
                (patch_index * shard_rows, head_index * columns),
                (shard_rows, columns),
            )
            pieces.append(jnp.pad(ortho, ((0, 0), (0, hidden - columns))))
        ortho_all = jnp.stack(pieces)
    adam = [w_modulate, first_modulate, second_modulate, b_modulate, first_bias, second_bias]

    def finish_body(*refs):
        finish_kernel(
            cuts, factors, *refs[:6], refs[6:10], refs[10:16], *refs[16:18], refs[18:22], refs[22:26], refs[26:32]
        )

    shards = [jax.ShapeDtypeStruct(weight.shape, F32) for weight in weights]
    finished = pl.pallas_call(
        finish_body,
        out_shape=[
            jax.ShapeDtypeStruct(layer_output.shape, BF16),
            jax.ShapeDtypeStruct(input_grad.shape, F32),
            *shards,
            *shards,
            *[jax.ShapeDtypeStruct(array.shape, F32) for array in adam],
        ],
        in_specs=[vmem] * 16,
        out_specs=[vmem] * 16,
        compiler_params=pltpu.CompilerParams(vmem_limit_bytes=60 << 20),
        name="finish",
    )(layer_output, input_grad, moment_cat, ortho_all, mod_summed, noise_embed, *weights, *adam)

    def unpack(project, output, expand, contract):
        return (project, output.T, expand, contract.T)

    return (*finished[:2], *unpack(*finished[2:6]), *unpack(*finished[6:10]), *finished[10:])


def solution(mesh):
    in_specs = (
        P(None, "nodes", "heads"),
        P(),
        P(None, "nodes", "heads"),
        P(None, "nodes", None),
        P(None, "nodes"),
        P("nodes", "heads"),
        P("heads", "nodes"),
        P("nodes", "heads"),
        P("heads", "nodes"),
        P("nodes", "heads"),
        P("heads", "nodes"),
        P("nodes", "heads"),
        P("heads", "nodes"),
        P(None, None, "heads"),
        P(None, "heads"),
        P(None, None, "heads"),
        P(None, None, "heads"),
        P(None, "heads"),
        P(None, "heads"),
    )
    out_specs = (
        P(None, "nodes", "heads"),
        P(None, "nodes", "heads"),
        P("nodes", "heads"),
        P("heads", "nodes"),
        P("nodes", "heads"),
        P("heads", "nodes"),
        P("nodes", "heads"),
        P("heads", "nodes"),
        P("nodes", "heads"),
        P("heads", "nodes"),
        P(None, None, "heads"),
        P(None, None, "heads"),
        P(None, None, "heads"),
        P(None, "heads"),
        P(None, "heads"),
        P(None, "heads"),
    )
    return jax.shard_map(
        per_device, mesh=mesh, in_specs=in_specs, out_specs=out_specs, check_vma=False
    )
```

```python
import functools

import jax
import jax.numpy as jnp
from jax import lax
from jax.experimental import pallas as pl
from jax.experimental.pallas import tpu as pltpu
from jax.sharding import PartitionSpec as P

NS_STEPS = 5
STEP = 10


EPS_NORM = 1e-06
NEWTON_A = 3.4445
NEWTON_B = -4.775
NEWTON_C = 2.0315
MOMENTUM_DECAY = 0.5
LR_MUON = 1.0
LR_ADAM = 0.04
DECAY_WEIGHT = 0.01
BETA_FIRST = 0.9
BETA_SECOND = 0.999
EPS_ADAM = 1e-08
HIGH = lax.Precision.HIGHEST
MESH = pl.DeviceIdType.MESH
F32 = jnp.float32
BF16 = jnp.bfloat16
NN = (((1,), (0,)), ((), ()))
NT = (((1,), (1,)), ((), ()))
TN = (((0,), (0,)), ((), ()))


def mul(left, right, dims=NN):
    return lax.dot_general(left, right, dims, preferred_element_type=F32)


class Links:
    def __init__(self, send_sems, recv_sems):
        self.send_sems, self.recv_sems = send_sems, recv_sems
        self.copies, self.finished = [], []

    def send(self, source, target, device):
        slot = len(self.copies)
        copy = pltpu.make_async_remote_copy(
            src_ref=source,
            dst_ref=target,
            send_sem=self.send_sems.at[slot],
            recv_sem=self.recv_sems.at[slot],
            device_id=device,
            device_id_type=MESH,
        )
        copy.start()
        self.copies.append(copy)
        return copy

    def finish(self, copy):
        copy.wait_send()
        self.finished.append(copy)

    def close(self):
        for copy in self.copies:
            if not any(copy is other for other in self.finished):
                copy.wait_send()


def greet(devices):
    barrier = pltpu.get_barrier_semaphore()
    for device in devices:
        pl.semaphore_signal(barrier, inc=1, device_id=device, device_id_type=MESH)


def await_greetings(devices):
    pl.semaphore_wait(pltpu.get_barrier_semaphore(), len(devices))


def norm_rows(values):
    width = values.shape[-1]
    row_mean = jnp.sum(values, axis=-1, keepdims=True) / width
    square_mean = jnp.sum(values * values, axis=-1, keepdims=True) / width
    inv_root = lax.rsqrt(square_mean - row_mean * row_mean + EPS_NORM)
    return ((values - row_mean) * inv_root, inv_root)


def wide(ref, *index):
    return jnp.concatenate([ref[(head, *index)] for head in range(ref.shape[0])], axis=-1)


def mod_row(mod_ref, batch, number):
    return wide(mod_ref, slice(batch * 4 + number, batch * 4 + number + 1), slice(None))


def layer_kernel(
    patch_count,
    own_gather,
    sizes_ref,
    state_ref,
    cot_ref,
    index_ref,
    noise_ref,
    modulate_ref,
    bias_ref,
    weight_refs,
    moment_refs,
    layer_out,
    input_out,
    moment_out,
    ortho_in,
    mod_sum,
    layer_output,
    input_grad,
    moment_new,
    moment_in,
    weight_low,
    weight_all,
    output_all,
    state_all,
    cot_all,
    mod_all,
    halo,
    a_one,
    queries,
    key_value,
    prob_low,
    mixed_all,
    hidden_one,
    a_two,
    act,
    grad_up,
    part_two,
    part_core,
    part_low,
    part_across,
    total_two,
    out_low,
    out_core,
    out_keep,
    out_across,
    grad_hidden,
    grad_attn,
    grad_mixed,
    score_low,
    grad_own,
    grad_away,
    grad_back,
    grad_projected,
    mod_part,
    mod_in,
    grad_cat,
    grad_low,
    grad_core,
    grad_line,
    grad_wide,
    moment_low,
    matrix,
    gram,
    chain,
    ortho_out,
    send_sems,
    recv_sems,
    turn_send,
    turn_recv,
    local_sems,
):
    node, head = lax.axis_index("nodes"), lax.axis_index("heads")
    after, before = lax.rem(node + 1, patch_count), lax.rem(node + patch_count - 1, patch_count)
    across, sibling = lax.rem(head + 2, 4), head + 1 - 2 * lax.rem(head, 2)
    to_across, to_sibling, to_diagonal = (node, across), (node, sibling), (node, 3 - head)
    to_after, to_before = (after, head), (before, head)
    side, core = lax.div(head, 2), lax.rem(head, 2)
    plane, parity = lax.div(node, 2), lax.rem(node, 2)
    mirror = 1 - parity
    partner = node + 1 - 2 * parity
    to_partner = (partner, head)
    micro_count, capacity, share = state_ref.shape
    head_dim = queries.shape[-1]
    full_width = a_one.shape[-1]
    hidden = act.shape[-1]
    total = 3 * capacity
    inv_head = head_dim ** (-0.5)
    cuts = (0, 3 * head_dim, 4 * head_dim, 4 * head_dim + hidden, 4 * head_dim + 2 * hidden)
    widths = (3 * head_dim, head_dim, hidden, hidden)
    expand_columns, contract_columns = slice(cuts[2], cuts[3]), slice(cuts[3], cuts[4])
    tile = capacity // 2
    batches = range(micro_count)
    peers = [(lax.rem(node + 2 * k, patch_count), head) for k in range(1, patch_count // 2)]
    met = [to_across, to_sibling, to_diagonal]
    if own_gather:
        met += [(lax.rem(node + k, patch_count), head) for k in range(1, patch_count)]
        met += [(partner, across)]
    else:
        met += [to_after, to_before]
    greet(met)
    own_copies = {}

    def move(name, source, target):
        copy = pltpu.make_async_copy(source, target, local_sems.at[len(own_copies)])
        copy.start()
        own_copies[name] = copy

    if own_gather:
        for number, ref in enumerate(moment_refs):
            move(number, ref, moment_in.at[:, cuts[number] : cuts[number + 1]])
    for number in range(modulate_ref.shape[0]):
        terms = lax.dot_general(
            noise_ref[...], modulate_ref[number], NN, precision=HIGH, preferred_element_type=F32
        )
        terms = terms + bias_ref[number : number + 1, :]
        for b in batches:
            place = b * modulate_ref.shape[0] + number
            mod_all[head, place : place + 1, :] = terms[b : b + 1]
    if own_gather:
        for number, ref in enumerate(weight_refs):
            weight_low[:, cuts[number] : cuts[number + 1]] = ref[...].astype(BF16)
    await_greetings(met)
    links = Links(send_sems, recv_sems)

    def weight(columns):
        return weight_all[:, :, columns].reshape(full_width, columns.stop - columns.start)

    def live_rows(batch, start, count):
        slots = lax.broadcasted_iota(jnp.int32, (count, 1), 0) + start
        return (slots < sizes_ref[0:1, batch : batch + 1]).astype(F32)

    def rows_at(step, count):
        start = step * count if isinstance(step, int) else pl.multiple_of(step * count, count)
        return start, pl.ds(start, count)

    first_columns = pl.ds(0, cuts[2])
    other_columns = pl.ds(cuts[2], cuts[4] - cuts[2])

    def spread(columns):
        part = weight_low.at[:, columns]
        into = weight_all.at[node, :, columns]
        return [links.send(part, into, to) for to in peers], (part, into)

    def pass_on(arriving, columns, which=(0, 1, 2)):
        passed = []
        for k in which:
            arriving[k].wait_recv()
            owner = lax.rem(node + patch_count - 2 * (k + 1), patch_count)
            part = weight_all.at[owner, :, columns]
            passed.append(links.send(part, part, to_partner))
        return passed

    mod_copies = [
        links.send(mod_all.at[head], mod_all.at[head], to) for to in (to_across, to_sibling, to_diagonal)
    ]
    if own_gather:
        first_peers, first_partner = spread(first_columns)
        first_partner = [links.send(*first_partner, to_partner)]
    state_across, state_after, state_before, state_sibling = [], [], [], []
    for b in batches:
        state_across.append(links.send(state_ref.at[b], state_all.at[head, b], to_across))
        state_after.append(links.send(state_ref.at[b], halo.at[0, head, b], to_after))
        state_before.append(links.send(state_ref.at[b], halo.at[1, head, b], to_before))
        state_sibling.append(links.send(state_ref.at[b], state_all.at[head, b], to_sibling))
    if own_gather:
        weight_all[node] = weight_low[...]
    state_all[head] = state_ref[...]
    cot_all[head] = cot_ref[...]

    group = index_ref.shape[-1] // 16
    blocks = total // share

    def count_group(batch, place):
        ids = index_ref[batch, pl.ds(place, 1), :] - (node - 1) * capacity
        ids = jnp.where(ids < 0, ids + patch_count * capacity, ids)
        ids = jnp.where(ids >= patch_count * capacity, ids - patch_count * capacity, ids)
        lanes = lax.broadcasted_iota(jnp.int32, ids.shape, 1)
        code = (ids >> 7) + 16 * (lanes >> 4)
        rows = lax.broadcasted_iota(jnp.int32, (blocks * group, ids.shape[1]), 0)
        pick = jnp.where(code == (rows // group) + 16 * (rows % group), 1.0, 0.0).astype(BF16)
        slots = lax.broadcasted_iota(jnp.int32, (share, ids.shape[1]), 0)
        spot = jnp.where((ids & 127) == slots, 1.0, 0.0).astype(BF16)
        found = mul(pick, spot, NT).astype(BF16)
        into = pl.ds(pl.multiple_of(place * group, group), group)
        for block in range(blocks):
            prob_low[batch, into, block * share : (block + 1) * share] = found[
                block * group : (block + 1) * group
            ]

    def count(batch):
        pl.loop(0, capacity // group, unroll=4)(lambda place: count_group(batch, place))

    pass_state, halo_across, halo_sibling = [], [], []

    def second_hops(b):
        state_across[b].wait_recv()
        part = state_all.at[across, b]
        pass_state.append(links.send(part, part, to_sibling))
        to_chip, to_core = [], []
        for k, copy in ((0, state_after[b]), (1, state_before[b])):
            copy.wait_recv()
            part = halo.at[k, head, b]
            to_chip.append(links.send(part, part, to_across))
            to_core.append(links.send(part, part, to_sibling))
        halo_across.append(to_chip)
        halo_sibling.append(to_core)

    if own_gather:
        other_peers, other_partner = spread(other_columns)
    for b in batches:
        count(b)
    second_hops(0)
    if own_gather:
        first_passed = pass_on(first_peers, first_columns)
    cot_across = [links.send(cot_ref.at[0], cot_all.at[head, 0], to_across)]
    second_hops(1)
    if own_gather:
        other_partner = [links.send(*other_partner, to_partner)]
    cot_sibling = links.send(cot_ref, cot_all.at[head], to_sibling)

    def project(source, patch, batch):
        shift, scale = mod_row(mod_all, batch, 0), 1.0 + mod_row(mod_all, batch, 1)

        @pl.loop(0, capacity // tile, unroll=2)
        def _(step):
            _, rows = rows_at(step, tile)
            normed, _ = norm_rows(wide(source, batch, rows, slice(None)).astype(F32))
            a_rows = (normed * scale + shift).astype(BF16)
            a_one[patch * micro_count + batch, rows, :] = a_rows
            first = 0 if patch == 1 else head_dim
            out = mul(a_rows, weight(slice(first, cuts[1]))).astype(BF16)
            if patch == 1:
                queries[batch, rows, :] = out[:, :head_dim]
            key_value[batch, patch, rows, :] = out[:, out.shape[1] - 2 * head_dim :]

    def project_all(b):
        state_sibling[b].wait_recv()
        pass_state[b].wait_recv()
        project(state_all, 1, b)
        for k in range(2):
            halo_across[b][k].wait_recv()
            part = halo.at[k, across, b]
            halo_sibling[b].append(links.send(part, part, to_sibling))
        for copy in halo_sibling[b]:
            copy.wait_recv()
        project(halo.at[0], 0, b)
        project(halo.at[1], 2, b)

    def attend(batch):
        attend_rows = 128

        @pl.loop(0, capacity // attend_rows, unroll=4)
        def _(step):
            _, rows = rows_at(step, attend_rows)
            keys = key_value[batch, :, :, :head_dim].reshape(total, head_dim)
            values = key_value[batch, :, :, head_dim:].reshape(total, head_dim)
            scores = mul(queries[batch, rows, :], keys, NT) * inv_head
            times = prob_low[batch, rows, :].astype(F32)
            scores = jnp.where(times > 0.0, scores, -1e30)
            exps = jnp.exp(scores - jnp.max(scores, axis=-1, keepdims=True)) * times
            prob = (exps * (1.0 / jnp.sum(exps, axis=-1, keepdims=True))).astype(BF16)
            prob_low[batch, rows, :] = prob
            mixed_all[head, batch, rows, :] = mul(prob, values).astype(BF16)

        part = mixed_all.at[head, batch]
        return links.send(part, part, to_across), links.send(part, part, to_sibling)

    def pass_mixed(batch, copies):
        copies[0].wait_recv()
        part = mixed_all.at[across, batch]
        return [copies[1], links.send(part, part, to_sibling)]

    def wait_all(copies):
        for copy in copies:
            copy.wait_recv()

    wait_all(mod_copies)
    ready = [cot_sibling]
    if own_gather:
        wait_all(first_partner + first_passed)
        output_all[head] = weight_all[:, :, cuts[1] : cuts[2]]
        output_part = weight_all.at[:, :, pl.ds(cuts[1], head_dim)]
        output_across = links.send(output_part, output_all.at[head], to_across)
        ready.append(links.send(output_part, output_all.at[head], to_sibling))
        other_passed = pass_on(other_peers, other_columns, (0,))
    project_all(0)
    if own_gather:
        other_passed += pass_on(other_peers, other_columns, (1,))
    mixed_first = attend(0)
    cot_across += [links.send(cot_ref.at[b], cot_all.at[head, b], to_across) for b in batches[1:]]
    if own_gather:
        other_passed += pass_on(other_peers, other_columns, (2,))
    project_all(1)
    mixed_first = pass_mixed(0, mixed_first)
    wait_all(cot_across)
    ready.append(links.send(cot_all.at[across], cot_all.at[across], to_sibling))
    if own_gather:
        output_across.wait_recv()
        ready.append(links.send(output_all.at[across], output_all.at[across], to_sibling))
    mixed_second = attend(1)
    if own_gather:
        ready += other_partner + other_passed
    wait_all(ready + mixed_first)

    def feed_forward(batch, step):
        start, rows = rows_at(step, tile)
        mixed = wide(mixed_all, batch, rows, slice(None))
        mixer = jnp.concatenate(
            [output_all[k].reshape(full_width, head_dim) for k in range(output_all.shape[0])], axis=-1
        )
        hid = wide(state_all, batch, rows, slice(None)).astype(F32) + mul(mixed, mixer, NT)
        hidden_one[batch, rows, :] = hid
        normed, _ = norm_rows(hid)
        a_rows = (normed * (1.0 + mod_row(mod_all, batch, 3)) + mod_row(mod_all, batch, 2)).astype(BF16)
        a_two[batch, rows, :] = a_rows
        up = mul(a_rows, weight(expand_columns))
        gate = jax.nn.sigmoid(up)
        acted = (up * gate).astype(BF16)
        act[batch, rows, :] = acted
        live = live_rows(batch, start, tile)
        cot = (wide(cot_all, batch, rows, slice(None)).astype(F32) * live).astype(BF16)
        grad_act = mul(cot, weight(contract_columns))
        grad_rows = (grad_act * gate * (1.0 + up * (1.0 - gate))).astype(BF16)
        grad_up[batch, rows, :] = grad_rows
        back = mul(grad_rows, weight(expand_columns), NT)
        out = mul(acted, weight(contract_columns), NT)
        for k in range(4):
            block = slice(k * head_dim, (k + 1) * head_dim)
            part_two[batch, k % 2, k // 2, rows, :] = back[:, block]
            out_low[batch, k % 2, k // 2, rows, :] = out[:, block].astype(BF16)

    def to_core(batch):
        return links.send(part_two.at[batch, 1 - core], part_core.at[batch], to_sibling)

    def to_side(batch, copy):
        copy.wait_recv()
        for k in range(2):
            chip = part_two[batch, core, k] + part_core[batch, k]
            part_core[batch, k] = chip
            part_low[batch, k] = chip.astype(BF16)
        return links.send(part_low.at[batch], part_across.at[batch], to_across)

    def to_all(batch, copy):
        copy.wait_recv()
        for k in range(2):
            total_two[batch, core, k] = part_core[batch, k] + part_across[batch, k].astype(F32)
        return links.send(total_two.at[batch, core], total_two.at[batch, core], to_sibling)

    def total_rows(batch, rows):
        return jnp.concatenate(
            [total_two[batch, k % 2, k // 2, rows, :] for k in range(4)], axis=-1
        )

    def back_norm(grad, normed, root):
        mean_grad = jnp.sum(grad, axis=-1, keepdims=True) / full_width
        mean_cross = jnp.sum(grad * normed, axis=-1, keepdims=True) / full_width
        return root * (grad - mean_grad - normed * mean_cross)

    def add_mod(batch, number, values):
        sums = jnp.sum(values, axis=0, keepdims=True)
        place = batch * 4 + number
        for k in range(4):
            mod_part[k, place : place + 1, :] += sums[:, k * head_dim : (k + 1) * head_dim]

    def own_block(values):
        own = jnp.zeros((values.shape[0], head_dim), F32)
        for k in range(4):
            own = own + jnp.where(head == k, values[:, k * head_dim : (k + 1) * head_dim], 0.0)
        return own

    for k in range(4):
        mod_part[k] = jnp.zeros(mod_part.shape[1:], F32)

    def store_grad(step, columns, value, add=False):
        half = full_width // 8
        for k in range(2):
            part = value[k * half : (k + 1) * half]
            if add:
                part = grad_cat[k, step, :, columns] + part
            grad_cat[k, step, :, columns] = part
            grad_low[k, step, :, columns] = part.astype(BF16)

    def both(ref, columns):
        return ref[:, :, columns].reshape(micro_count * capacity, -1)

    def one_pair(patch, columns):
        pair = a_one[patch * micro_count : (patch + 1) * micro_count, :, columns]
        return pair.reshape(micro_count * capacity, -1)

    def live_cot(batch, columns):
        return (cot_all[columns, batch].astype(F32) * live_rows(batch, 0, capacity)).astype(BF16)

    def expand_grad(batch, step):
        columns = pl.ds(pl.multiple_of(step * head_dim, head_dim), head_dim)
        value = mul(a_two[batch, :, columns], grad_up[batch], TN)
        store_grad(step, expand_columns, value, batch > 0)

    def contract_grad(batch, step):
        store_grad(step, contract_columns, mul(live_cot(batch, step), act[batch], TN), batch > 0)

    pl.loop(0, 2, unroll=2)(lambda step: feed_forward(0, step))
    core_first = to_core(0)
    mixed_second = pass_mixed(1, mixed_second)
    side_first = to_side(0, core_first)

    @pl.loop(0, 4, unroll=4)
    def _(step):
        expand_grad(0, step)
        contract_grad(0, step)

    wait_all(mixed_second)
    pl.loop(0, 2, unroll=2)(lambda step: feed_forward(1, step))
    core_second = to_core(1)

    late_one, late_two = slice(0, 2 * head_dim), slice(2 * head_dim, cuts[1])
    output_columns = slice(cuts[1], cuts[2])

    def grad_pair(columns):
        return links.send(
            grad_low.at[1 - parity, :, :, columns], grad_core.at[:, :, columns], to_partner
        )

    def grad_planes(copy, columns):
        copy.wait_recv()
        for k in range(4):
            summed = grad_cat[parity, k, :, columns] + grad_core[k, :, columns].astype(F32)
            grad_cat[parity, k, :, columns] = summed
            grad_low[parity, k, :, columns] = summed.astype(BF16)
        sent = []
        for k in range(1, 4):
            target = lax.rem(plane + k, 4)
            sent.append(
                links.send(
                    grad_low.at[parity, target, :, columns],
                    grad_line.at[k - 1, :, columns],
                    (2 * target + parity, head),
                )
            )
        return sent

    def grad_finish(copies, columns):
        wait_all(copies)
        summed = grad_cat[parity, plane, :, columns]
        for k in range(3):
            summed = summed + grad_line[k, :, columns].astype(F32)
        moment_new[:, columns] = summed

    def grad_wide_planes(columns):
        sent = []
        for k in range(1, 4):
            target = lax.rem(plane + k, 4)
            sent.append(
                links.send(
                    grad_low.at[:, target, :, columns],
                    grad_wide.at[k - 1, :, :, columns],
                    (2 * target + parity, head),
                )
            )
        return sent

    def grad_wide_pair(copies, columns):
        wait_all(copies)
        for pair in range(2):
            summed = grad_cat[pair, plane, :, columns]
            for k in range(3):
                summed = summed + grad_wide[k, pair, :, columns].astype(F32)
            grad_cat[pair, plane, :, columns] = summed
            grad_low[pair, plane, :, columns] = summed.astype(BF16)
        return links.send(
            grad_low.at[mirror, plane, :, columns], grad_core.at[plane, :, columns], to_partner
        )

    def grad_wide_finish(copy, columns):
        copy.wait_recv()
        summed = grad_cat[parity, plane, :, columns] + grad_core[plane, :, columns].astype(F32)
        moment_new[:, columns] = summed

    def store_moment(numbers):
        for number in numbers:
            own = slice(cuts[number], cuts[number + 1])
            own_copies[number].wait()
            moment = MOMENTUM_DECAY * moment_in[:, own] + moment_new[:, own]
            moment_new[:, own] = moment
            moment_low[:, own] = moment.astype(BF16)

    pl.loop(0, 4, unroll=4)(lambda step: expand_grad(1, step))
    if own_gather:
        expand_pair = grad_pair(expand_columns)
    pl.loop(0, 4, unroll=4)(lambda step: contract_grad(1, step))
    if own_gather:
        contract_wide = grad_wide_planes(contract_columns)
    side_second = to_side(1, core_second)
    all_first = to_all(0, side_first)
    out_copies = [links.send(out_low.at[b, 1 - core], out_core.at[b], to_sibling) for b in batches]

    def norm_two_back(batch):
        @pl.loop(0, capacity // tile, unroll=2)
        def _(step):
            start, rows = rows_at(step, tile)
            normed, root = norm_rows(hidden_one[batch, rows, :])
            grad = total_rows(batch, rows)
            add_mod(batch, 2, grad)
            add_mod(batch, 3, grad * normed)
            cot = wide(cot_all, batch, rows, slice(None)).astype(F32) * live_rows(batch, start, tile)
            grad = cot + back_norm(grad * (1.0 + mod_row(mod_all, batch, 3)), normed, root)
            grad_hidden[batch, rows, :] = own_block(grad)
            low = grad.astype(BF16)
            grad_attn[batch, rows, :] = low
            grad_mixed[batch, rows, :] = mul(low, weight(slice(cuts[1], cuts[2]))).astype(BF16)

    def attend_back(batch, between=lambda: None):
        attend_rows = 128

        @pl.loop(0, capacity // attend_rows, unroll=4)
        def _(step):
            _, rows = rows_at(step, attend_rows)
            keys = key_value[batch, :, :, :head_dim].reshape(total, head_dim)
            values = key_value[batch, :, :, head_dim:].reshape(total, head_dim)
            prob = prob_low[batch, rows, :].astype(F32)
            grad_prob = mul(grad_mixed[batch, rows, :], values, NT)
            mean = jnp.sum(prob * grad_prob, axis=-1, keepdims=True)
            score = (prob * (grad_prob - mean) * inv_head).astype(BF16)
            score_low[rows, :] = score
            grad_projected[batch, rows, :head_dim] = mul(score, keys).astype(BF16)

        between()
        for patch in range(3):
            slots = slice(patch * capacity, (patch + 1) * capacity)
            grad_key = mul(score_low[:, slots], queries[batch], TN)
            grad_value = mul(prob_low[batch, :, slots], grad_mixed[batch], TN)
            if patch == 1:
                grad_own[batch, :, :head_dim] = grad_key
                grad_own[batch, :, head_dim:] = grad_value
            else:
                grad_away[batch, patch // 2, :, :head_dim] = grad_key.astype(BF16)
                grad_away[batch, patch // 2, :, head_dim:] = grad_value.astype(BF16)

    def send_back(batch):
        return [
            links.send(grad_away.at[batch, 0], grad_back.at[batch, 1], to_before),
            links.send(grad_away.at[batch, 1], grad_back.at[batch, 0], to_after),
        ]

    owners = (1, 2, 0, 3)

    def turn(source, target, device, send_slot, recv_slot):
        return pltpu.make_async_remote_copy(
            src_ref=source,
            dst_ref=target,
            send_sem=turn_send.at[send_slot],
            recv_sem=turn_recv.at[recv_slot],
            device_id=device,
            device_id_type=MESH,
        )

    def to_owner(number, sender):
        return turn(
            moment_low.at[:, slice(cuts[number], cuts[number + 1])],
            matrix.at[head, parity, sender, :, : widths[number]],
            (2 * owners[number] + parity, head),
            number,
            sender,
        )

    def give(width, number):
        block, pair, device = (
            (head, parity, to_across),
            (head, parity, to_partner),
            (head, parity, (partner, across)),
            (head, parity, to_sibling),
            (across, parity, to_sibling),
            (head, mirror, to_sibling),
            (across, mirror, to_sibling),
        )[number]
        part = matrix.at[block, pair, :, :, :width]
        return turn(part, part, device, 4 + number, 4 + number)

    def own_to_owner(numbers):
        for number in numbers:

            @pl.when(plane != owners[number])
            def _():
                to_owner(number, plane).start()

            @pl.when(plane == owners[number])
            def _():
                matrix[head, parity, plane, :, : widths[number]] = moment_low[
                    :, cuts[number] : cuts[number + 1]
                ]

    def own_arrive(numbers):
        for number in numbers:

            @pl.when(plane == owners[number])
            def _():
                for other in range(4):
                    if other != owners[number]:
                        to_owner(number, other).wait_recv()
                for k in range(4):
                    give(widths[number], k).start()

            @pl.when(plane != owners[number])
            def _():
                to_owner(number, plane).wait_send()

    all_first.wait_recv()
    norm_two_back(0)
    if own_gather:
        expand_line = grad_planes(expand_pair, expand_columns)
    all_second = []
    attend_back(0, lambda: all_second.append(to_all(1, side_second)))
    all_second = all_second[0]
    back_first = send_back(0)
    out_across_copies = []
    for batch in batches:
        out_copies[batch].wait_recv()
        for k in range(2):
            chip = out_low[batch, core, k].astype(F32) + out_core[batch, k].astype(F32)
            out_keep[batch, k] = chip
            out_core[batch, k] = chip.astype(BF16)
        out_across_copies.append(
            links.send(out_core.at[batch, 1 - side], out_across.at[batch], to_across)
        )
    all_second.wait_recv()
    norm_two_back(1)
    attend_back(1)
    if own_gather:
        contract_pair = grad_wide_pair(contract_wide, contract_columns)

    @pl.loop(0, 4, unroll=4)
    def _(step):
        columns = pl.ds(pl.multiple_of(step * head_dim, head_dim), head_dim)
        own = jnp.concatenate(
            [both(grad_projected, slice(0, head_dim)), grad_own[...].reshape(-1, 2 * head_dim).astype(BF16)], axis=1
        )
        own = mul(one_pair(1, columns), own, TN)
        store_grad(step, slice(0, head_dim), own[:, :head_dim])
        rest = own[:, head_dim:]
        for patch in (0, 2):
            away = grad_away[:, patch // 2].reshape(-1, 2 * head_dim)
            rest = rest + mul(one_pair(patch, columns), away, TN)
        store_grad(step, slice(head_dim, cuts[1]), rest)

    if own_gather:
        late_wide = grad_wide_planes(late_two)
        late_pair = grad_pair(late_one)

    @pl.loop(0, 4, unroll=4)
    def _(step):
        columns = pl.ds(pl.multiple_of(step * head_dim, head_dim), head_dim)
        own_mixed = mixed_all[head].reshape(-1, head_dim)
        store_grad(step, output_columns, mul(both(grad_attn, columns), own_mixed, TN))

    if own_gather:
        output_wide = grad_wide_planes(output_columns)
    if own_gather:
        late_line = grad_planes(late_pair, late_one)
        late_pair = grad_wide_pair(late_wide, late_two)
        output_pair = grad_wide_pair(output_wide, output_columns)
    back_second = send_back(1)
    if own_gather:
        grad_finish(expand_line, expand_columns)
        grad_wide_finish(contract_pair, contract_columns)
        store_moment((2, 3))
        own_to_owner((2, 3))
    for copy in out_across_copies:
        copy.wait_recv()
    for copy in (core_first, core_second, side_first, side_second, all_first, all_second):
        links.finish(copy)

    def rows_back(batch, copies):
        wait_all(copies)
        whole = grad_own[batch] + grad_back[batch, 0].astype(F32) + grad_back[batch, 1].astype(F32)
        grad_projected[batch, :, head_dim:] = whole.astype(BF16)

        @pl.loop(0, capacity // tile, unroll=2)
        def _(step):
            _, rows = rows_at(step, tile)
            back = mul(grad_projected[batch, rows, :], weight(slice(0, cuts[1])), NT)
            for k in range(4):
                part_two[batch, k % 2, k // 2, rows, :] = back[:, k * head_dim : (k + 1) * head_dim]

        return to_core(batch)

    def rows_end(batch, copy):
        copy.wait_recv()

        @pl.loop(0, capacity // tile, unroll=2)
        def _(step):
            _, rows = rows_at(step, tile)
            normed, root = norm_rows(wide(state_all, batch, rows, slice(None)).astype(F32))
            grad = total_rows(batch, rows)
            add_mod(batch, 0, grad)
            add_mod(batch, 1, grad * normed)
            grad = back_norm(grad * (1.0 + mod_row(mod_all, batch, 1)), normed, root)
            input_grad[batch, rows, :] = own_block(grad) + grad_hidden[batch, rows, :]

        move(("input", batch), input_grad.at[batch], input_out.at[batch])

    one_core = [rows_back(0, back_first)]
    for batch in batches:
        own = hidden_one[batch, :, pl.ds(pl.multiple_of(head * head_dim, head_dim), head_dim)]
        result = own + out_keep[batch, side] + out_across[batch].astype(F32)
        layer_output[batch] = (result * live_rows(batch, 0, capacity)).astype(BF16)
    move("layer", layer_output, layer_out)


    if not own_gather:
        one_core.append(rows_back(1, back_second))
        one_side = [to_side(b, one_core[b]) for b in batches]
        one_all = [to_all(b, one_side[b]) for b in batches]
        for b in batches:
            rows_end(b, one_all[b])
        mod_sum[...] = mod_part[head]
        for k in range(8):
            moment_out[k] = grad_cat[k % 2, k // 2]
        links.close()
        for name in ("layer", ("input", 0), ("input", 1)):
            own_copies[name].wait()
        return

    one_side = [to_side(0, one_core[0])]
    own_arrive((2, 3))
    grad_wide_finish(late_pair, late_two)
    grad_finish(late_line, late_one)
    store_moment((0,))
    own_to_owner((0,))
    grad_wide_finish(output_pair, output_columns)
    store_moment((1,))
    own_to_owner((1,))
    move("moment", moment_new, moment_out)
    one_core.append(rows_back(1, back_second))
    own_arrive((0, 1))
    one_side.append(to_side(1, one_core[1]))
    one_all = [to_all(0, one_side[0])]
    rows_end(0, one_all[0])
    half = full_width // 2

    def gather_plane(width):
        for k in range(3):
            give(width, k).wait_recv()
            give(width, 4 + k).start()
        for k in range(3, 7):
            give(width, k).wait_recv()
        for k in range(7):
            give(width, k).wait_send()

        @pl.loop(0, 2)
        def _(step):
            _, rows = rows_at(step, half)
            summed = jnp.zeros((half, full_width), F32)
            for k in range(4):
                left = matrix[k, step, :, :, :width].reshape(half, width)
                right = matrix[k, :, :, :, :width].reshape(full_width, width)
                summed = summed + mul(left, right, NT)
            gram[rows, :] = summed

    for first, second, width in ((1, 1, widths[0]), (2, 2, widths[1]), (0, 3, hidden)):

        @pl.when((plane == first) | (plane == second))
        def _():
            gather_plane(width)

    gram_pair, factor_pair, turn_pair = (a_one.at[pl.ds(k, 2)] for k in (0, 2, 4))

    everything, top, bottom = slice(None), slice(0, half), slice(half, full_width)

    def put_pair(ref, value, rows=everything, columns=everything):
        high = value.astype(BF16)
        ref[0, rows, columns] = high
        ref[1, rows, columns] = (value - high.astype(F32)).astype(BF16)

    def times(left, right, rows=everything, columns=everything):
        left_high, left_low = left[0, rows, :], left[1, rows, :]
        right_high, right_low = right[0, :, columns], right[1, :, columns]
        return mul(
            jnp.concatenate([left_high, left_high, left_low], axis=1),
            jnp.concatenate([right_high, right_low, right_high], axis=0),
        )

    def upper(left, right):
        return times(left, right, top), times(left, right, bottom, bottom)

    def put_upper(ref, parts):
        put_pair(ref, parts[0], top)
        put_pair(ref, parts[1], bottom, bottom)
        put_pair(ref, parts[0][:, half:].T, bottom, top)

    def diagonal(count, start=0):
        rows = lax.broadcasted_iota(jnp.int32, (count, full_width), 0) + start
        return rows == lax.broadcasted_iota(jnp.int32, (count, full_width), 1)

    trace = jnp.zeros((1, 1), F32)
    for step in range(2):
        kept = jnp.where(diagonal(half, step * half), gram[step * half : (step + 1) * half, :], 0.0)
        trace = trace + jnp.sum(jnp.sum(kept, axis=1, keepdims=True), axis=0, keepdims=True)
    scale = 1.0 / (jnp.sqrt(trace) + 1e-07)
    gram[...] = gram[...] * (scale * scale)
    put_pair(gram_pair, gram[...])
    own = pl.ds(pl.multiple_of(parity * half, half), half)

    for repeat in range(NS_STEPS - 1):
        square = upper(gram_pair, gram_pair)
        unit = diagonal(full_width)
        factor = (
            NEWTON_B * gram[top, :] + NEWTON_C * square[0] + jnp.where(unit[top], NEWTON_A, 0.0),
            NEWTON_B * gram[bottom, bottom]
            + NEWTON_C * square[1]
            + jnp.where(unit[bottom, bottom], NEWTON_A, 0.0),
        )
        put_upper(factor_pair, factor)
        if repeat == 0:
            put_upper(chain.at[0], factor)
        else:
            put_upper(chain.at[repeat % 2], upper(factor_pair, chain.at[(repeat + 1) % 2]))
        put_upper(turn_pair, upper(factor_pair, gram_pair))
        product = upper(factor_pair, turn_pair)
        put_upper(gram_pair, product)
        gram[top, :] = product[0]
        gram[bottom, bottom] = product[1]
        if repeat == NS_STEPS - 2:
            gram[bottom, top] = product[0][:, half:].T
        if repeat == 1:
            one_all.append(to_all(1, one_side[1]))
    factor = NEWTON_B * gram[own, :] + NEWTON_C * times(gram_pair, gram_pair, own)
    factor = factor + jnp.where(diagonal(half, parity * half), NEWTON_A, 0.0)
    put_pair(factor_pair, factor, own)
    final = times(factor_pair, chain.at[(NS_STEPS - 2) % 2], own)

    put_pair(chain.at[0], final, slice(0, half))

    def ortho_copy(number, k):
        target = (owners[number] + k) % 4
        width = widths[number]
        return turn(
            ortho_out.at[target, :, :width],
            ortho_in.at[number, :, :width],
            (2 * target + parity, head),
            11 + k,
            11 + number,
        )

    for number in range(4):

        @pl.when(plane == owners[number])
        def _():
            width = widths[number]
            left = jnp.concatenate([chain[0, k, :half, :] for k in range(2)], axis=-1)
            right = matrix[head, :, :, :, :width].reshape(full_width, width)
            value = mul(left, jnp.concatenate([right, right], axis=0)) * scale
            ortho_out[:, :, :width] = value.astype(BF16).reshape(4, half // 4, width)
            for k in range(1, 4):
                ortho_copy(number, k).start()
            ortho_in[number, :, :width] = ortho_out[plane, :, :width]

    rows_end(1, one_all[1])
    mod_copies = [
        links.send(mod_part.at[head], mod_in.at[k - 1], (lax.rem(node + k, patch_count), head))
        for k in range(1, patch_count)
    ]
    for number in range(4):

        @pl.when(plane != owners[number])
        def _():
            ortho_copy(number, 1).wait_recv()

        @pl.when(plane == owners[number])
        def _():
            for k in range(1, 4):
                ortho_copy(number, k).wait_send()

    summed = mod_part[head]
    wait_all(mod_copies)
    for k in range(patch_count - 1):
        summed = summed + mod_in[k]
    mod_sum[...] = summed
    links.close()
    for name in ("layer", "moment", ("input", 0), ("input", 1)):
        own_copies[name].wait()


def finish_kernel(cuts, factors, sources, targets, buffers, in_sems, out_sems):
    layer, rows, moment, ortho, mods, noise = buffers[:6]
    weights, adam = buffers[6:10], buffers[10:]
    order = [4, 5, 10, 11, 12, 13, 14, 15, 3, 6, 7, 8, 9, 2, 0, 1]
    arriving, leaving = {}, []
    for k in order:
        arriving[k] = pltpu.make_async_copy(sources[k], buffers[k], in_sems.at[k])
        arriving[k].start()

    def leave(source, target):
        copy = pltpu.make_async_copy(source, target, out_sems.at[len(leaving)])
        copy.start()
        leaving.append(copy)

    def arrive(*places):
        for k in places:
            arriving[k].wait()

    moment_outs, weight_outs, adam_outs = targets[2:6], targets[6:10], targets[10:]
    weight, first, second, bias, first_bias, second_bias = adam
    micro_count = noise.shape[0]
    arrive(*order[:8])
    for number in range(weight.shape[0]):
        terms = [mods[b * 4 + number : b * 4 + number + 1, :] for b in range(micro_count)]
        grad = lax.dot_general(
            noise[...], jnp.concatenate(terms, axis=0), TN, precision=HIGH, preferred_element_type=F32
        )
        place = slice(number, number + 1)
        stepped = adam_step(weight[number], first[number], second[number], grad)
        for ref, value in zip((first, second, weight), stepped):
            ref[number] = value
        stepped = adam_step(bias[place, :], first_bias[place, :], second_bias[place, :], sum(terms))
        for ref, value in zip((first_bias, second_bias, bias), stepped):
            ref[place, :] = value
        for ref, target in zip((first, second, weight), adam_outs[:3]):
            leave(ref.at[number], target.at[number])
    for ref, target in zip((first_bias, second_bias, bias), adam_outs[3:]):
        leave(ref, target)
    arrive(3)
    for number in range(4):
        arrive(6 + number)
        step = ortho[number, :, : cuts[number + 1] - cuts[number]].astype(F32)
        weights[number][...] = (
            weights[number][...] * (1.0 - LR_MUON * DECAY_WEIGHT) - (LR_MUON * factors[number]) * step
        )
        leave(weights[number], weight_outs[number])
    arrive(2)
    for number in range(4):
        leave(moment.at[:, cuts[number] : cuts[number + 1]], moment_outs[number])
    for k, ref in ((0, layer), (1, rows)):
        arrive(k)
        leave(ref, targets[k])
    for copy in leaving:
        copy.wait()


def adam_step(weight, first_old, second_old, gradient):
    first_new = BETA_FIRST * first_old + (1.0 - BETA_FIRST) * gradient
    second_new = BETA_SECOND * second_old + (1.0 - BETA_SECOND) * gradient * gradient
    first_hat = first_new / (1.0 - BETA_FIRST**STEP)
    second_hat = second_new / (1.0 - BETA_SECOND**STEP)
    updated = weight * (1.0 - LR_ADAM * DECAY_WEIGHT) - LR_ADAM * first_hat / (
        jnp.sqrt(second_hat) + EPS_ADAM
    )
    return (first_new, second_new, updated)


def orthogonal(matrix):
    scale = 1.0 / (jnp.sqrt(jnp.sum(matrix * matrix)) + 1e-07)
    gram = jnp.dot(matrix, matrix.T, precision=HIGH) * (scale * scale)
    eye = jnp.eye(gram.shape[0], dtype=F32)
    chain = None
    for repeat in range(NS_STEPS):
        factor = NEWTON_A * eye + NEWTON_B * gram + NEWTON_C * jnp.dot(gram, gram, precision=HIGH)
        chain = factor if chain is None else jnp.dot(factor, chain, precision=HIGH)
        if repeat < NS_STEPS - 1:
            gram = jnp.dot(factor, jnp.dot(factor, gram, precision=HIGH), precision=HIGH)
    return jnp.dot(chain, matrix, precision=HIGH) * scale


def per_device(
    node_state,
    noise_embed,
    out_grad,
    neighbours,
    patch_sizes,
    w_project,
    w_output,
    w_expand,
    w_contract,
    momentum_project,
    momentum_output,
    momentum_expand,
    momentum_contract,
    w_modulate,
    b_modulate,
    first_modulate,
    second_modulate,
    first_bias,
    second_bias,
):
    micro_count, capacity, share = node_state.shape
    head_count = lax.axis_size("heads")
    patch_count = lax.axis_size("nodes")
    full_width = share * head_count
    head_dim = w_output.shape[0]
    patch_index = lax.axis_index("nodes")
    head_index = lax.axis_index("heads")
    inv_head = head_dim ** (-0.5)
    hidden = w_expand.shape[1]
    shard_rows = w_project.shape[0]
    own_gather = patch_count == 8

    index_rows = neighbours.reshape(micro_count, capacity // 16, 256)
    weights = [w_project, w_output.T, w_expand, w_contract.T]
    moments = [momentum_project, momentum_output.T, momentum_expand, momentum_contract.T]
    cuts = (0, 3 * head_dim, 4 * head_dim, 4 * head_dim + hidden, 4 * head_dim + 2 * hidden)
    factors = (1.0, 1.0, 1.0, (head_count * hidden / full_width) ** 0.5)
    weight_width = cuts[4]
    vmem = pl.BlockSpec(memory_space=pltpu.VMEM)
    anywhere = pl.BlockSpec(memory_space=pl.ANY)
    def scratch(dtype, *shape):
        return pltpu.VMEM(shape, dtype)

    rows_all = (head_count, micro_count, capacity, share)
    blocks = (micro_count, 2, 2, capacity, head_dim)
    half_blocks = (micro_count, 2, capacity, head_dim)
    rows_wide = (micro_count, capacity, full_width)
    rows_hidden = (micro_count, capacity, hidden)
    rows_own = (micro_count, capacity, head_dim)
    key_value_rows = (capacity, 2 * head_dim)
    eighth = full_width // 8
    out_rows = [
        scratch(BF16, micro_count, capacity, share),
        scratch(F32, micro_count, capacity, share),
    ]
    scratches = [
        scratch(F32, eighth, weight_width),
        scratch(F32, eighth, weight_width),
        scratch(BF16, eighth, weight_width),
        scratch(BF16, 8, eighth, weight_width),
        scratch(BF16, head_count, 8, eighth, head_dim),
    ]
    scratches = out_rows + (scratches if own_gather else [])
    scratches += [
        scratch(BF16, *rows_all),
        scratch(BF16, *rows_all),
        scratch(F32, head_count, 4 * micro_count, share),
        scratch(BF16, 2, *rows_all),
        scratch(BF16, 3 * micro_count, capacity, full_width),
        scratch(BF16, *rows_own),
        scratch(BF16, micro_count, 3, *key_value_rows),
        scratch(BF16, micro_count, capacity, 3 * capacity),
        scratch(BF16, *rows_all),
        scratch(F32, *rows_wide),
        scratch(BF16, *rows_wide),
        scratch(BF16, *rows_hidden),
        scratch(BF16, *rows_hidden),
        scratch(F32, *blocks),
        scratch(F32, *half_blocks),
        scratch(BF16, *half_blocks),
        scratch(BF16, *half_blocks),
        scratch(F32, *blocks),
        scratch(BF16, *blocks),
        scratch(BF16, *half_blocks),
        scratch(F32, *half_blocks),
        scratch(BF16, *rows_own),
        scratch(F32, *rows_own),
        scratch(BF16, *rows_wide),
        scratch(BF16, *rows_own),
        scratch(BF16, capacity, 3 * capacity),
        scratch(F32, micro_count, *key_value_rows),
        scratch(BF16, micro_count, 2, *key_value_rows),
        scratch(BF16, micro_count, 2, *key_value_rows),
        scratch(BF16, micro_count, capacity, 3 * head_dim),
        scratch(F32, head_count, 4 * micro_count, share),
        scratch(F32, 8, 4 * micro_count, share),
        scratch(F32, 2, 4, eighth, weight_width),
        scratch(BF16, 2, 4, eighth, weight_width),
        scratch(BF16, 4, eighth, weight_width),
        scratch(BF16, 3, eighth, weight_width),
        scratch(BF16, 3, 2, eighth, weight_width),
    ]
    last = [
        scratch(BF16, eighth, weight_width),
        scratch(BF16, head_count, 2, 4, eighth, hidden),
        scratch(F32, full_width, full_width),
        scratch(BF16, 2, 2, full_width, full_width),
        scratch(BF16, 4, eighth, hidden),
    ]
    semaphores = [pltpu.SemaphoreType.DMA((count,)) for count in (112, 112, 16, 16, 16)]
    operands = [patch_sizes.T, node_state, out_grad, index_rows, noise_embed, w_modulate, b_modulate]
    out_shape = [
        jax.ShapeDtypeStruct((micro_count, capacity, share), BF16),
        jax.ShapeDtypeStruct((micro_count, capacity, share), F32),
    ]
    summed_shape = jax.ShapeDtypeStruct((4 * micro_count, share), F32)
    if own_gather:
        operands += weights + moments
        out_shape += [
            jax.ShapeDtypeStruct((eighth, weight_width), F32),
            jax.ShapeDtypeStruct((4, eighth, hidden), BF16),
            summed_shape,
        ]
        scratches += last
    else:
        low_cat = jnp.concatenate(weights, axis=1).astype(BF16)
        low_cat = lax.all_gather(low_cat, "nodes", axis=0, tiled=True)
        low_cat = low_cat.reshape(8, eighth, weight_width)
        output_all = lax.all_gather(
            low_cat[:, :, 3 * head_dim : 4 * head_dim], "heads", axis=0, tiled=False
        )
        operands += [low_cat, output_all]
        out_shape += [jax.ShapeDtypeStruct((8, eighth, weight_width), F32), summed_shape]

    def layer_body(*refs):
        refs = list(refs)
        if own_gather:
            refs[7:15] = [refs[7:11], refs[11:15]]
        else:
            gathered = refs[7:9]
            refs[7:9] = [None, None]
            refs[12:12] = [None]
            refs[16:16] = [None] * 3 + gathered
            refs[-5:-5] = [None] * len(last)
        layer_kernel(patch_count, own_gather, *refs)

    updated = pl.pallas_call(
        layer_body,
        out_shape=out_shape,
        in_specs=[vmem] * min(len(operands), 11) + [anywhere] * max(len(operands) - 11, 0),
        out_specs=[anywhere] * 2 + [anywhere if own_gather else vmem] + [vmem] * (len(out_shape) - 3),
        scratch_shapes=scratches + semaphores,
        compiler_params=pltpu.CompilerParams(
            collective_id=0, has_side_effects=True, vmem_limit_bytes=60 << 20
        ),
        name="layer",
    )(*operands)
    if own_gather:
        layer_output, input_grad, moment_cat, ortho_all, mod_summed = updated
    else:
        layer_output, input_grad, grad_cat, mod_summed = updated
        mod_summed = lax.psum(mod_summed, "nodes")
        moment_cat = MOMENTUM_DECAY * jnp.concatenate(moments, axis=1) + lax.psum_scatter(
            grad_cat.reshape(full_width, weight_width), "nodes", scatter_dimension=0, tiled=True
        )
        whole = lax.all_gather(moment_cat.astype(BF16), ("nodes", "heads"), axis=0, tiled=False)
        whole = whole.reshape(patch_count, head_count, shard_rows, weight_width)
        whole = whole.transpose(0, 2, 1, 3).reshape(full_width, head_count, weight_width).astype(F32)
        pieces = []
        for number in range(4):
            columns = cuts[number + 1] - cuts[number]
            matrix = whole[:, :, cuts[number] : cuts[number + 1]].reshape(full_width, head_count * columns)
            ortho = lax.dynamic_slice(
                orthogonal(matrix),
                (patch_index * shard_rows, head_index * columns),
                (shard_rows, columns),
            )
            pieces.append(jnp.pad(ortho, ((0, 0), (0, hidden - columns))))
        ortho_all = jnp.stack(pieces)
    adam = [w_modulate, first_modulate, second_modulate, b_modulate, first_bias, second_bias]

    def finish_body(*refs):
        finish_kernel(cuts, factors, refs[:16], refs[16:32], refs[32:48], *refs[48:])

    shards = [jax.ShapeDtypeStruct(weight.shape, F32) for weight in weights]
    given = [layer_output, input_grad, moment_cat, ortho_all, mod_summed, noise_embed, *weights, *adam]
    finished = pl.pallas_call(
        finish_body,
        out_shape=[
            jax.ShapeDtypeStruct(layer_output.shape, BF16),
            jax.ShapeDtypeStruct(input_grad.shape, F32),
            *shards,
            *shards,
            *[jax.ShapeDtypeStruct(array.shape, F32) for array in adam],
        ],
        in_specs=[anywhere] * 16,
        out_specs=[anywhere] * 16,
        scratch_shapes=[scratch(array.dtype, *array.shape) for array in given]
        + [pltpu.SemaphoreType.DMA((16,)), pltpu.SemaphoreType.DMA((32,))],
        compiler_params=pltpu.CompilerParams(vmem_limit_bytes=60 << 20),
        name="finish",
    )(*given)

    def unpack(project, output, expand, contract):
        return (project, output.T, expand, contract.T)

    return (*finished[:2], *unpack(*finished[2:6]), *unpack(*finished[6:10]), *finished[10:])


def solution(mesh):
    in_specs = (
        P(None, "nodes", "heads"),
        P(),
        P(None, "nodes", "heads"),
        P(None, "nodes", None),
        P(None, "nodes"),
        P("nodes", "heads"),
        P("heads", "nodes"),
        P("nodes", "heads"),
        P("heads", "nodes"),
        P("nodes", "heads"),
        P("heads", "nodes"),
        P("nodes", "heads"),
        P("heads", "nodes"),
        P(None, None, "heads"),
        P(None, "heads"),
        P(None, None, "heads"),
        P(None, None, "heads"),
        P(None, "heads"),
        P(None, "heads"),
    )
    out_specs = (
        P(None, "nodes", "heads"),
        P(None, "nodes", "heads"),
        P("nodes", "heads"),
        P("heads", "nodes"),
        P("nodes", "heads"),
        P("heads", "nodes"),
        P("nodes", "heads"),
        P("heads", "nodes"),
        P("nodes", "heads"),
        P("heads", "nodes"),
        P(None, None, "heads"),
        P(None, None, "heads"),
        P(None, None, "heads"),
        P(None, "heads"),
        P(None, "heads"),
        P(None, "heads"),
    )
    return jax.shard_map(
        per_device, mesh=mesh, in_specs=in_specs, out_specs=out_specs, check_vma=False
    )
```
